32 devices in a mesh: seq: 16 (over z, y, x), head: 2 (over core).
Axes of the slice: x: 2, y: 2, z: 4, core: 2. Of those that a mesh axis runs over, the one named last changes fastest.
Arguments:
- queries: bfloat16 [2048, 4096], P('seq', 'head'), may hold values from -0.71875 to 0.71875
- key_rows: bfloat16 [2048, 4096], P('seq', 'head'), may hold values from -0.71875 to 0.71875
- value_rows: bfloat16 [2048, 4096], P('seq', 'head'), may hold values from -0.71875 to 0.71875
- segment_ids: int32 [2048], P('seq'), may hold values from 0 to 7, never falling along the last dimension, each value on 1 to 512 neighbouring positions
- decay_span: float32 [32], P('head'), may hold values from 30 to 20480, as said below
- norm_gain: float32 [4096], P('head'), may hold values from 0.5 to 1.5
- out_grad: bfloat16 [2048, 4096], P('seq', 'head'), may hold values from -0.71875 to 0.71875
Outputs:
- query_grad: bfloat16 [2048, 4096], P('seq', 'head')
- key_grad: bfloat16 [2048, 4096], P('seq', 'head')
- value_grad: bfloat16 [2048, 4096], P('seq', 'head')
- gain_grad: float32 [4096], P('head')
The draws below stay inside these ranges and needn't reach their ends.
Inputs may be any that keep to these rules, and one draw needn't show every extreme that they name: segment_ids never falls along the segment; every document of the 8 has a token and the longest has 512. The decay per token of head h is exp(-1 / decay_span[h]).
All inputs are finite; a program needn't handle non-finite values.
Results may differ from the reference program's by a relative error of at most 0.0012.
Values sent between devices are 32-bit elements; how exact they have to be, the bound alone decides.
No kernel may reach another device: no remote copies, remote signals or barrier semaphores. Data moves between devices by JAX's collectives and lax.ppermute only.
A program may use at most 64 MiB of HBM per device.

```python
import math
import jax
import jax.numpy as jnp
import numpy as np
from jax import lax

HEADS = 32
HEAD_DIM = 128
DOCS = 8
TOKENS = 2048
FEATURES = 4096
DOC_MOST = 512


def draw_decay_span(key, part):
    key_pick, key_fast, key_slow, key_place = jax.random.split(jax.random.fold_in(key, 17), 4)
    fast_share = 0.5
    chooser = jax.random.uniform(key_pick, (HEADS,), jnp.float32)
    fast_span = jax.random.uniform(key_fast, (HEADS,), jnp.float32, 30.0, 50.0)
    low_log = jnp.log(jnp.float32(0.5 * TOKENS))
    high_log = jnp.log(jnp.float32(10.0 * TOKENS))
    slow_span = jnp.exp(jax.random.uniform(key_slow, (HEADS,), jnp.float32, low_log, high_log))
    spans = jnp.where(chooser < fast_share, fast_span, slow_span)
    place = jax.random.randint(key_place, (), 0, HEADS)
    spans = spans.at[place].set(30.0)
    spans = spans.at[(place + 1) % HEADS].set(jnp.float32(10.0 * TOKENS))
    return spans.astype(jnp.float32)


def levels(stream_key, dims, cuts, low, high):
    factor_of, own = 1.0, jax.random.fold_in(stream_key, 6)
    for dim, parts in cuts:
        heights = jnp.exp(jax.random.uniform(jax.random.fold_in(own, dim), (parts,), jnp.float32, low / len(cuts), high / len(cuts)))
        factor_of = factor_of * jnp.repeat(heights, dims[dim] // parts).reshape([-1 if axis == dim else 1 for axis in range(len(dims))])
    return factor_of


def length_profile(number_of, total, bound, skew):
    loads = [(1 << 20) // math.isqrt(rank ** skew) + 1 for rank in range(2, number_of + 1)]
    surplus, holding = total - bound - (number_of - 1), [1] * (number_of - 1)
    while surplus > 0:
        candidates = [i for i in range(number_of - 1) if holding[i] < bound]
        mass, budget = sum([loads[i] for i in candidates]), surplus
        for i in candidates:
            addition = min(bound - holding[i], max(1, budget * loads[i] // mass), surplus)
            holding[i] = holding[i] + addition
            surplus = surplus - addition
    return np.array([bound] + holding)


def ragged_sizes(rng, count, total, limit, skew):
    if count == 2:
        one = jax.random.randint(rng, (), max(1, total - limit), min(limit, total - 1) + 1)
        return jnp.stack([one, total - one])
    tallies = jnp.asarray(length_profile(count, total, limit, skew), jnp.int32)
    couples = (count - 1) // 2
    source_of, taker = tallies[1:1 + 2 * couples:2], tallies[2:2 + 2 * couples:2]
    margin = jnp.minimum(source_of - 1, limit - taker)
    passed = jax.random.randint(jax.random.fold_in(rng, 1), (couples,), 0, 1 << 20) % (margin + 1)
    tallies = tallies.at[1:1 + 2 * couples:2].set(source_of - passed).at[2:2 + 2 * couples:2].set(taker + passed)
    return tallies[jax.random.permutation(jax.random.fold_in(rng, 2), count)]


def normal_values(stream_key, extent, width, most, pieces=(), held_as=jnp.bfloat16):
    values = jax.random.normal(stream_key, extent, jnp.float32) * width
    if len(pieces) > 0:
        values = levels(stream_key, extent, pieces, -0.22, 0.18) * values
    return jnp.clip(values, min=-most, max=most).astype(held_as)


def setup_inputs(seed: int = 0) -> dict:
    splits = jax.random.split(jax.random.key(seed), 8)
    return {
        "queries": normal_values(splits[0], (TOKENS, FEATURES), 0.12, 0.71875, ((0, 16), (1, 2))),
        "key_rows": normal_values(splits[1], (TOKENS, FEATURES), 0.12, 0.71875, ((0, 16), (1, 2))),
        "value_rows": normal_values(splits[2], (TOKENS, FEATURES), 0.12, 0.71875, ((0, 16), (1, 2))),
        "segment_ids": jnp.searchsorted(jnp.cumsum(ragged_sizes(splits[3], DOCS, TOKENS, DOC_MOST, 0)), jnp.arange(TOKENS), side="right").astype(jnp.int32),
        "decay_span": draw_decay_span(jax.random.fold_in(splits[7], 71), 0),
        "norm_gain": jnp.clip(1.0 + 0.1 * jax.random.normal(splits[5], (FEATURES,), jnp.float32), 0.5, 1.5),
        "out_grad": normal_values(splits[6], (TOKENS, FEATURES), 0.12, 0.71875, ((0, 16), (1, 2))),
    }


exact = lax.Precision.HIGHEST

def reference(queries, key_rows, value_rows, segment_ids, decay_span, norm_gain, out_grad):
    group_rows = 128
    group_count = TOKENS // group_rows
    all_features = HEADS * HEAD_DIM
    spans = decay_span.astype(jnp.float32)
    gain_vec = norm_gain.astype(jnp.float32)
    offsets = jnp.arange(group_rows).astype(jnp.float32)
    offset_gap = offsets[:, None] - offsets[None, :]
    causal = offset_gap >= 0
    decay_tile = jnp.where(causal[None], jnp.exp(-jnp.maximum(offset_gap, 0.0)[None] / spans[:, None, None]), 0.0)
    into_weight = jnp.exp(-(offsets + 1.0)[:, None] / spans[None, :])
    tail_weight = jnp.exp(-(group_rows - 1.0 - offsets)[:, None] / spans[None, :])
    start_weight = jnp.exp(-offsets[:, None] / spans[None, :])
    next_weight = jnp.exp(-(group_rows - offsets)[:, None] / spans[None, :])
    whole_weight = jnp.exp(-group_rows / spans)

    def split_heads(array):
        return array.reshape(group_count, group_rows, HEADS, HEAD_DIM)
    query_blocks = split_heads(queries)
    key_blocks = split_heads(key_rows)
    value_blocks = split_heads(value_rows)
    grad_blocks = out_grad.reshape(group_count, group_rows, all_features)
    seg_blocks = segment_ids.astype(jnp.float32).reshape(group_count, group_rows)

    def forward_step(carry, inputs):
        state_now, carry_seg = carry
        query_blk, key_blk, value_blk, dy_blk, seg_blk = inputs
        query_blk = query_blk.astype(jnp.float32)
        key_blk = key_blk.astype(jnp.float32)
        value_blk = value_blk.astype(jnp.float32)
        dy_full = dy_blk.astype(jnp.float32)
        same_doc = (seg_blk[:, None] == seg_blk[None, :]).astype(jnp.float32)
        weights = decay_tile * same_doc[None]
        scores = jnp.einsum('thd,shd->hts', query_blk, key_blk, precision=exact) * weights
        inter_on = jnp.where((seg_blk == carry_seg)[:, None], into_weight, 0.0)
        attended = jnp.einsum('hts,shd->thd', scores, value_blk, precision=exact)
        attended = attended + inter_on[:, :, None] * jnp.einsum('thi,hij->thj', query_blk, state_now, precision=exact)
        flat_out = attended.reshape(group_rows, all_features)
        inv_scale = lax.rsqrt(lax.optimization_barrier(jnp.sum(flat_out * flat_out, axis=1)) / all_features + 1e-06)
        cross = lax.optimization_barrier(jnp.sum(dy_full * gain_vec[None, :] * flat_out, axis=1))
        out_back = gain_vec[None, :] * dy_full * inv_scale[:, None] - flat_out * (inv_scale * inv_scale * inv_scale * cross / all_features)[:, None]
        gain_part = lax.optimization_barrier(jnp.sum(dy_full * flat_out * inv_scale[:, None], axis=0))
        back_heads = out_back.reshape(group_rows, HEADS, HEAD_DIM)
        grad_scores = jnp.einsum('thd,shd->hts', back_heads, value_blk, precision=exact) * weights
        query_part = jnp.einsum('hts,shd->thd', grad_scores, key_blk, precision=exact)
        query_part = query_part + inter_on[:, :, None] * jnp.einsum('thj,hij->thi', back_heads, state_now, precision=exact)
        tail_on = jnp.where((seg_blk == seg_blk[-1])[:, None], tail_weight, 0.0)
        passes = jnp.logical_and(seg_blk[0] == seg_blk[-1], seg_blk[0] == carry_seg)
        factor = jnp.where(passes, whole_weight, 0.0)
        new_state = jnp.einsum('thi,thj->hij', key_blk * tail_on[:, :, None], value_blk, precision=exact) + factor[:, None, None] * state_now
        return ((new_state, seg_blk[-1]), (back_heads, query_part.reshape(group_rows, all_features).astype(jnp.bfloat16), gain_part))
    start_carry = (jnp.zeros((HEADS, HEAD_DIM, HEAD_DIM), jnp.float32), jnp.float32(-1.0))
    _, (back_blocks, query_grad, gain_parts) = lax.scan(forward_step, start_carry, (query_blocks, key_blocks, value_blocks, grad_blocks, seg_blocks))

    def backward_step(carry, inputs):
        grad_state, carry_seg = carry
        query_blk, key_blk, value_blk, back_heads, seg_blk = inputs
        query_blk = query_blk.astype(jnp.float32)
        key_blk = key_blk.astype(jnp.float32)
        value_blk = value_blk.astype(jnp.float32)
        same_doc = (seg_blk[:, None] == seg_blk[None, :]).astype(jnp.float32)
        weights = decay_tile * same_doc[None]
        scores = jnp.einsum('thd,shd->hts', query_blk, key_blk, precision=exact) * weights
        grad_scores = jnp.einsum('thd,shd->hts', back_heads, value_blk, precision=exact) * weights
        back_on = jnp.where((seg_blk == carry_seg)[:, None], next_weight, 0.0)
        key_part = jnp.einsum('hts,thd->shd', grad_scores, query_blk, precision=exact)
        key_part = key_part + back_on[:, :, None] * jnp.einsum('hij,shj->shi', grad_state, value_blk, precision=exact)
        value_part = jnp.einsum('hts,thd->shd', scores, back_heads, precision=exact)
        value_part = value_part + back_on[:, :, None] * jnp.einsum('hij,shi->shj', grad_state, key_blk, precision=exact)
        start_on = jnp.where((seg_blk == seg_blk[0])[:, None], start_weight, 0.0)
        passes = jnp.logical_and(seg_blk[0] == seg_blk[-1], seg_blk[-1] == carry_seg)
        factor = jnp.where(passes, whole_weight, 0.0)
        new_state = jnp.einsum('thi,thj->hij', query_blk * start_on[:, :, None], back_heads, precision=exact) + factor[:, None, None] * grad_state
        return ((new_state, seg_blk[0]), (key_part.reshape(group_rows, all_features).astype(jnp.bfloat16), value_part.reshape(group_rows, all_features).astype(jnp.bfloat16)))
    _, (key_grad, value_grad) = lax.scan(backward_step, start_carry, (query_blocks, key_blocks, value_blocks, back_blocks, seg_blocks), reverse=True)
    gain_grad = lax.optimization_barrier(jnp.sum(gain_parts, axis=0))
    return (query_grad.reshape(TOKENS, all_features), key_grad.reshape(TOKENS, all_features), value_grad.reshape(TOKENS, all_features), gain_grad)
```

```python
import jax
import jax.numpy as jnp
from jax import lax
from jax.experimental import pallas as pl
from jax.experimental.pallas import tpu as pltpu
from jax.sharding import PartitionSpec as P

GROUP = 4
INFO = 8
FAR = 1e9
f32 = jnp.float32
bf16 = jnp.bfloat16


def dot(a, b, over_a=1, over_b=0):
    return lax.dot_general(a, b, (((over_a,), (over_b,)), ((), ())), preferred_element_type=f32)


def halves(x):
    high = x.astype(bf16)
    return high, (x - high.astype(f32)).astype(bf16)


def decay(steps, span):
    return jnp.exp(-steps / span)


class Sizes:
    def __init__(self, queries, decay_span):
        self.rows = queries.shape[0]
        self.heads = decay_span.shape[0]
        self.dim = queries.shape[1] // self.heads
        self.per = self.heads // GROUP
        self.wide = self.per * self.dim
        self.state = self.per * self.dim
        self.pad = -(-self.per // 8) * 8


def markers(seg_ref, size):
    row = seg_ref[...].astype(f32) + 1.0
    return row, jnp.broadcast_to(row, (size.dim, size.rows)).T


def position(size):
    return lax.broadcasted_iota(jnp.int32, (size.rows, size.dim), 0).astype(f32)


def pair_weight(row, size):
    shape = (size.rows, size.rows)
    here = jnp.broadcast_to(row, shape)
    at = lax.broadcasted_iota(jnp.int32, shape, 0)
    by = lax.broadcasted_iota(jnp.int32, shape, 1)
    live = jnp.logical_and(at >= by, here == here.T)
    return jnp.maximum(at - by, 0).astype(f32), live


def info_rows(first_row, second_row, dim):
    index = lax.broadcasted_iota(jnp.int32, (INFO, dim), 0)
    return jnp.where(index == 0, first_row, jnp.where(index == 1, second_row, 0.0))


def span_at(spans, group, size, h):
    return jnp.full((1, size.dim), spans[group * size.per + h], f32)


def call(body, size, name, groups, spans, seg, inputs, outputs, flops, moved):
    def spec(array, chunk):
        if chunk is None:
            return pl.BlockSpec(array.shape, lambda i, g: (0,) * len(array.shape))
        return pl.BlockSpec((array.shape[0], size.wide), lambda i, g: (0, g[chunk]))

    def whole(shape):
        return pl.BlockSpec(shape, lambda i, g: (0,) * len(shape))

    in_specs = [pl.BlockSpec(memory_space=pltpu.SMEM), whole(seg.shape)]
    in_specs += [spec(array, chunk) for array, chunk in inputs]
    return pl.pallas_call(
        body,
        grid_spec=pltpu.PrefetchScalarGridSpec(
            num_scalar_prefetch=1,
            grid=(1,),
            in_specs=in_specs,
            out_specs=[whole(o.shape) for o in outputs],
        ),
        out_shape=outputs,
        compiler_params=pltpu.CompilerParams(vmem_limit_bytes=40 * 1024 * 1024),
        cost_estimate=pl.CostEstimate(flops=flops, bytes_accessed=moved, transcendentals=0),
        name=name,
    )(groups, spans, seg, *[array for array, _ in inputs])


def key_value_states(size, chunks, groups, spans, seg, key_rows, value_rows):
    n = len(chunks)

    def body(g_ref, spans, seg_ref, *refs):
        ins, outs = refs[: 2 * n], refs[2 * n :]
        row, mark = markers(seg_ref, size)
        last, first = mark[size.rows - 1 :, :], mark[:1, :]
        ahead = (size.rows - 1.0) - position(size)
        for c, chunk in enumerate(chunks):
            for h in range(size.per):
                cols = slice(h * size.dim, (h + 1) * size.dim)
                span = span_at(spans, g_ref[chunk], size, h)
                weight = jnp.where(mark == last, decay(ahead, span), 0.0)
                key = ins[2 * c][:, cols]
                high, low = halves(ins[2 * c + 1][:, cols].astype(f32) * weight)
                outs[c][cols, :] = dot(
                    jnp.concatenate([key, key], 0), jnp.concatenate([high, low], 0), 0, 0
                )
            outs[c][size.state :, :] = info_rows(last, first, size.dim)

    inputs = []
    for chunk in chunks:
        inputs += [(key_rows, chunk), (value_rows, chunk)]
    shape = jax.ShapeDtypeStruct((size.state + INFO, size.dim), f32)
    cost = n * size.per * 4 * size.rows * size.dim * size.dim
    return call(
        body, size, "states", groups, spans, seg, inputs, [shape] * n, cost, n * size.wide * 1024
    )


def local_attended(size, chunks, groups, spans, seg, queries, key_rows, value_rows):
    n = len(chunks)

    def body(g_ref, spans, seg_ref, *refs):
        ins, outs = refs[: 3 * n], refs[3 * n :]
        row, _ = markers(seg_ref, size)
        gap, live = pair_weight(row, size)
        for c, chunk in enumerate(chunks):
            for h in range(size.per):
                cols = slice(h * size.dim, (h + 1) * size.dim)
                span = spans[g_ref[chunk] * size.per + h]
                weight = jnp.where(live, decay(gap, jnp.full((1, size.rows), span, f32)), 0.0)
                query, key, value = (ins[3 * c + i][:, cols] for i in range(3))
                high, low = halves(dot(query, key, 1, 1) * weight)
                outs[c][:, cols] = dot(
                    jnp.concatenate([high, low], 1), jnp.concatenate([value, value], 0)
                )

    inputs = []
    for chunk in chunks:
        inputs += [(queries, chunk), (key_rows, chunk), (value_rows, chunk)]
    shape = jax.ShapeDtypeStruct((size.rows, size.wide), f32)
    cost = n * size.per * 6 * size.rows * size.dim * size.dim
    return call(
        body, size, "local", groups, spans, seg, inputs, [shape] * n, cost, n * size.wide * 1024
    )


def places(g_ref, backward):
    if backward:
        return [GROUP - 1 - g_ref[k] for k in range(GROUP)]
    return [g_ref[k] for k in range(GROUP)]


def group_total(size, backward, groups, spans, seg, parts):
    mark_row = size.state + (1 if backward else 0)

    def body(g_ref, spans, seg_ref, *refs):
        ins, out = refs[:GROUP], refs[GROUP]
        place = places(g_ref, backward)
        marks = [ref[mark_row : mark_row + 1, :] for ref in ins]
        end = marks[0]
        for mark in marks[1:]:
            end = jnp.minimum(end, mark) if backward else jnp.maximum(end, mark)
        for h in range(size.per):
            cols = slice(h * size.dim, (h + 1) * size.dim)
            span = span_at(spans, g_ref[0], size, h)
            total = None
            for k in range(GROUP):
                steps = ((GROUP - 1 - place[k]) * size.rows).astype(f32)
                factor = jnp.where(marks[k] == end, decay(steps, span), 0.0)
                term = factor * ins[k][cols, :]
                total = term if total is None else total + term
            out[cols, :] = total
        out[size.state :, :] = info_rows(end, end, size.dim)

    shape = jax.ShapeDtypeStruct((size.state + INFO, size.dim), f32)
    return call(
        body, size, "total", groups, spans, seg, [(p, None) for p in parts], [shape],
        size.state * size.dim * 8, size.state * size.dim * 20,
    )[0]


def group_prefixes(size, backward, groups, spans, seg, parts, entering, riders=()):
    mark_row = size.state + (1 if backward else 0)
    extra = sum(r.shape[0] for r in riders)

    def body(g_ref, spans, seg_ref, *refs):
        ins, enter = refs[:GROUP], refs[GROUP]
        rides, outs = refs[GROUP + 1 : GROUP + 1 + len(riders)], refs[GROUP + 1 + len(riders) :]
        place = places(g_ref, backward)
        marks = [ref[mark_row : mark_row + 1, :] for ref in ins]
        outer = enter[size.state : size.state + 1, :]
        if backward:
            outer = jnp.where(outer == 0.0, FAR, outer)
        carry = []
        for to in range(GROUP):
            now = outer
            for k in range(GROUP):
                if backward:
                    now = jnp.where(place[k] < place[to], jnp.minimum(now, marks[k]), now)
                else:
                    now = jnp.where(place[k] < place[to], jnp.maximum(now, marks[k]), now)
            carry.append(now)
            outs[to][size.state : size.state + INFO, :] = info_rows(now, now, size.dim)
            at = size.state + INFO
            for ride in rides:
                outs[to][at : at + ride.shape[0], :] = ride[...]
                at += ride.shape[0]
        for h in range(size.per):
            cols = slice(h * size.dim, (h + 1) * size.dim)
            span = span_at(spans, g_ref[0], size, h)
            for to in range(GROUP):
                steps = (place[to] * size.rows).astype(f32)
                total = jnp.where(outer == carry[to], decay(steps, span), 0.0) * enter[cols, :]
                for k in range(GROUP):
                    gap = place[to] - 1 - place[k]
                    steps = (jnp.maximum(gap, 0) * size.rows).astype(f32)
                    live = jnp.logical_and(marks[k] == carry[to], gap >= 0)
                    total += jnp.where(live, decay(steps, span), 0.0) * ins[k][cols, :]
                outs[to][cols, :] = total

    shape = jax.ShapeDtypeStruct((size.state + INFO + extra, size.dim), f32)
    inputs = [(p, None) for p in parts] + [(entering, None)] + [(r, None) for r in riders]
    return call(
        body, size, "prefixes", groups, spans, seg, inputs, [shape] * GROUP,
        size.state * size.dim * 40, size.state * size.dim * 36,
    )


def whole_attended(size, groups, spans, seg, queries, out_grad, gain, local, entering):
    chunks = range(GROUP)

    def body(g_ref, spans, seg_ref, *refs):
        ins, outs = refs[: 5 * GROUP], refs[5 * GROUP :]
        _, mark = markers(seg_ref, size)
        behind = position(size) + 1.0
        square = jnp.zeros((size.rows, size.dim), f32)
        cross = jnp.zeros((size.rows, size.dim), f32)
        for c, chunk in enumerate(chunks):
            query_ref, grad_ref, gain_ref, local_ref, state_ref = ins[5 * c : 5 * c + 5]
            live = mark == state_ref[size.state : size.state + 1, :]
            for h in range(size.per):
                cols = slice(h * size.dim, (h + 1) * size.dim)
                span = span_at(spans, g_ref[chunk], size, h)
                weight = jnp.where(live, decay(behind, span), 0.0)
                query = query_ref[:, cols]
                high, low = halves(state_ref[cols, :])
                inter = dot(jnp.concatenate([query, query], 1), jnp.concatenate([high, low], 0))
                out = local_ref[:, cols] + weight * inter
                outs[c][:, cols] = out
                square += out * out
                cross += grad_ref[:, cols].astype(f32) * gain_ref[:, cols] * out
        square = jnp.sum(square.T, axis=0, keepdims=True)
        cross = jnp.sum(cross.T, axis=0, keepdims=True)
        index = lax.broadcasted_iota(jnp.int32, (8, size.rows), 0)
        outs[GROUP][...] = jnp.where(index == 0, square, jnp.where(index == 1, cross, 0.0))

    inputs = []
    for c in chunks:
        inputs += [(queries, c), (out_grad, c), (gain, c), (local[c], None), (entering[c], None)]
    shapes = [jax.ShapeDtypeStruct((size.rows, size.wide), f32)] * GROUP
    shapes.append(jax.ShapeDtypeStruct((8, size.rows), f32))
    return call(
        body, size, "attended", groups, spans, seg, inputs, shapes,
        size.heads * 4 * size.rows * size.dim * size.dim, size.heads * size.dim * size.rows * 16,
    )


def output_grad_states(size, chunks, features, groups, spans, seg, queries, out_grad, gain, attended, sums, before=()):
    n = len(chunks)

    def body(g_ref, spans, seg_ref, *refs):
        sums_ref, ins = refs[0], refs[1 : 1 + 4 * n]
        earlier = refs[1 + 4 * n : 1 + 4 * n + len(before)]
        outs = refs[1 + 4 * n + len(before) :]
        row, mark = markers(seg_ref, size)
        last, first = mark[size.rows - 1 :, :], mark[:1, :]
        wide = (size.dim, size.rows)
        square = jnp.broadcast_to(sums_ref[0:1, :], wide).T
        cross = jnp.broadcast_to(sums_ref[1:2, :], wide).T
        inv = lax.rsqrt(square / features + 1e-06)
        pull = inv * inv * inv * cross / features
        gone = position(size)
        for c, chunk in enumerate(chunks):
            query_ref, grad_ref, gain_ref, att_ref = ins[4 * c : 4 * c + 4]
            back_ref, state_ref = outs[2 * c : 2 * c + 2]
            rows = []
            for h in range(size.per):
                cols = slice(h * size.dim, (h + 1) * size.dim)
                span = span_at(spans, g_ref[chunk], size, h)
                weight = jnp.where(mark == first, decay(gone, span), 0.0)
                grad = grad_ref[:, cols].astype(f32) * inv
                att = att_ref[:, cols]
                back = gain_ref[:, cols] * grad - att * pull
                back_ref[:, cols] = back
                rows.append(jnp.sum(grad * att, axis=0, keepdims=True))
                query = query_ref[:, cols]
                high, low = halves(back * weight)
                state_ref[cols, :] = dot(
                    jnp.concatenate([query, query], 0), jnp.concatenate([high, low], 0), 0, 0
                )
            state_ref[size.state :, :] = info_rows(last, first, size.dim)
            index = lax.broadcasted_iota(jnp.int32, (size.pad, size.dim), 0)
            gains = jnp.zeros((size.pad, size.dim), f32)
            for h, row in enumerate(rows):
                gains = jnp.where(index == h, row, gains)
            at = chunk * size.pad if before else c * size.pad
            outs[2 * n][at : at + size.pad, :] = gains
        for ref, (k, _) in zip(earlier, before):
            outs[2 * n][k * size.pad : (k + 1) * size.pad, :] = ref[...]

    inputs = [(sums, None)]
    for chunk in chunks:
        inputs += [(queries, chunk), (out_grad, chunk), (gain, chunk), (attended[chunk], None)]
    inputs += [(rows, None) for _, rows in before]
    shapes = []
    for _ in chunks:
        shapes.append(jax.ShapeDtypeStruct((size.rows, size.wide), f32))
        shapes.append(jax.ShapeDtypeStruct((size.state + INFO, size.dim), f32))
    held = GROUP if before else n
    shapes.append(jax.ShapeDtypeStruct((held * size.pad, size.dim), f32))
    outs = call(
        body, size, "back", groups, spans, seg, inputs, shapes,
        n * size.per * 4 * size.rows * size.dim * size.dim, n * size.wide * size.rows * 16,
    )
    return outs[0 : 2 * n : 2], outs[1 : 2 * n : 2], outs[2 * n]


def local_gradients(size, groups, spans, seg, queries, key_rows, value_rows, back, entering):
    def body(g_ref, spans, seg_ref, *refs):
        ins, outs = refs[: 5 * GROUP], refs[5 * GROUP :]
        row, mark = markers(seg_ref, size)
        gap, pairs = pair_weight(row, size)
        behind = position(size) + 1.0
        for c in range(GROUP):
            query_ref, key_ref, value_ref, back_ref, state_ref = ins[5 * c : 5 * c + 5]
            live = mark == state_ref[size.state : size.state + 1, :]
            for h in range(size.per):
                cols = slice(h * size.dim, (h + 1) * size.dim)
                span = spans[g_ref[c] * size.per + h]
                weight = jnp.where(pairs, decay(gap, jnp.full((1, size.rows), span, f32)), 0.0)
                query, key, value = query_ref[:, cols], key_ref[:, cols], value_ref[:, cols]
                high, low = halves(back_ref[:, cols])
                grads = dot(
                    jnp.concatenate([high, low], 1), jnp.concatenate([value, value], 1), 1, 1
                )
                grads_high, grads_low = halves(grads * weight)
                part = dot(
                    jnp.concatenate([grads_high, grads_low], 1), jnp.concatenate([key, key], 0)
                )
                state_high, state_low = halves(state_ref[cols, :])
                inter = dot(
                    jnp.concatenate([high, high, low], 1),
                    jnp.concatenate([state_high, state_low, state_high], 1),
                    1, 1,
                )
                into = jnp.where(live, decay(behind, jnp.full((1, size.dim), span, f32)), 0.0)
                start = pl.multiple_of(g_ref[c] * size.wide + h * size.dim, size.dim)
                outs[0][:, pl.ds(start, size.dim)] = (part + into * inter).astype(bf16)
                outs[1 + 2 * c][:, cols] = dot(
                    jnp.concatenate([grads_high, grads_low], 0),
                    jnp.concatenate([query, query], 0),
                    0, 0,
                )
                score_high, score_low = halves(dot(query, key, 1, 1) * weight)
                outs[2 + 2 * c][:, cols] = dot(
                    jnp.concatenate([score_high, score_high, score_low], 0),
                    jnp.concatenate([high, low, high], 0),
                    0, 0,
                )

    inputs = []
    for c in range(GROUP):
        inputs += [(queries, c), (key_rows, c), (value_rows, c), (back[c], None), (entering[c], None)]
    shapes = [jax.ShapeDtypeStruct((size.rows, size.heads * size.dim), bf16)]
    shapes += [jax.ShapeDtypeStruct((size.rows, size.wide), f32)] * (2 * GROUP)
    outs = call(
        body, size, "gradients", groups, spans, seg, inputs, shapes,
        size.heads * 26 * size.rows * size.dim * size.dim, size.heads * size.dim * size.rows * 24,
    )
    return outs[0], outs[1::2], outs[2::2]


def final_gradients(size, groups, spans, seg, key_rows, value_rows, local_key, local_value, entering):
    def body(g_ref, spans, seg_ref, *refs):
        ins, outs = refs[: 5 * GROUP], refs[5 * GROUP :]
        _, mark = markers(seg_ref, size)
        left = size.rows - position(size)
        for c in range(GROUP):
            key_ref, value_ref, local_key_ref, local_value_ref, state_ref = ins[5 * c : 5 * c + 5]
            live = mark == state_ref[size.state : size.state + 1, :]
            for h in range(size.per):
                cols = slice(h * size.dim, (h + 1) * size.dim)
                span = span_at(spans, g_ref[c], size, h)
                weight = jnp.where(live, decay(left, span), 0.0)
                key, value = key_ref[:, cols], value_ref[:, cols]
                high, low = halves(state_ref[cols, :])
                keys = dot(
                    jnp.concatenate([value, value], 1), jnp.concatenate([high, low], 1), 1, 1
                )
                values = dot(jnp.concatenate([key, key], 1), jnp.concatenate([high, low], 0))
                start = pl.multiple_of(g_ref[c] * size.wide + h * size.dim, size.dim)
                here = pl.ds(start, size.dim)
                outs[0][:, here] = (local_key_ref[:, cols] + weight * keys).astype(bf16)
                outs[1][:, here] = (local_value_ref[:, cols] + weight * values).astype(bf16)
                total = None
                for k in range(GROUP):
                    at = size.state + INFO + (k ^ c) * size.pad + h
                    row = ins[5 * k + 4][at : at + 1, :]
                    total = row if total is None else total + row
                outs[2][:, here] = total

    inputs = []
    for c in range(GROUP):
        inputs += [
            (key_rows, c), (value_rows, c), (local_key[c], None), (local_value[c], None),
            (entering[c], None),
        ]
    features = size.heads * size.dim
    shapes = [jax.ShapeDtypeStruct((size.rows, features), bf16)] * 2
    shapes.append(jax.ShapeDtypeStruct((1, features), f32))
    return call(
        body, size, "final", groups, spans, seg, inputs, shapes,
        size.heads * 8 * size.rows * size.dim * size.dim, features * size.rows * 24,
    )


def swap(array, distance):
    members = lax.axis_size("seq")
    return lax.ppermute(array, "seq", [(i, i ^ distance) for i in range(members)])


def shifted(array, by):
    members = lax.axis_size("seq")
    pairs = [(i, i + by) for i in range(members) if 0 <= i + by < members]
    return lax.ppermute(array, "seq", pairs)


def from_other_groups(size, backward, spans, me, total):
    members = lax.axis_size("seq")
    span_tokens = GROUP * size.rows
    longest = members * size.rows // 4
    needed = max(longest - 2, 0) // span_tokens + 1
    way = -GROUP if backward else GROUP
    result = shifted(total, way)
    reach = 1
    mine = lax.dynamic_slice(spans, (me * size.per,), (size.per,))
    while reach < needed:
        incoming = shifted(result, way * reach)
        passes = incoming[size.state, 0] == result[size.state, 0]
        factor = jnp.where(passes, jnp.exp(-(reach * span_tokens) / mine), 0.0)
        factor = jnp.repeat(factor, size.dim)[:, None]
        result = result.at[: size.state].add(factor * incoming[: size.state])
        reach *= 2
    return result


def travel(size, backward, groups, spans, seg, me, states, riders=lambda: ()):
    parts = [states[0]] + [swap(states[k], k) for k in range(1, GROUP)]
    total = group_total(size, backward, groups, spans, seg, parts)
    entering = from_other_groups(size, backward, spans, me, total)
    outs = group_prefixes(size, backward, groups, spans, seg, parts, entering, riders())
    return [outs[0]] + [swap(outs[k], k) for k in range(1, GROUP)]


def local(queries, key_rows, value_rows, segment_ids, decay_span, norm_gain, out_grad):
    size = Sizes(queries, decay_span)
    features = size.heads * size.dim * lax.axis_size("head")
    members = lax.axis_size("seq")
    me = lax.rem(lax.axis_index("seq"), GROUP)
    groups = jnp.bitwise_xor(jnp.arange(GROUP, dtype=jnp.int32), me.astype(jnp.int32))
    seg = segment_ids.reshape(1, size.rows)
    gain = norm_gain.reshape(1, size.heads * size.dim)
    common = (groups, decay_span, seg)

    states = {}
    for chunk in (3, 1, 2, 0):
        states[chunk] = key_value_states(size, (chunk,), *common, key_rows, value_rows)[0]
    nearby = local_attended(size, range(GROUP), *common, queries, key_rows, value_rows)
    entering = travel(size, False, *common, me, states)

    outs = whole_attended(size, *common, queries, out_grad, gain, nearby, entering)
    attended, sums = outs[:GROUP], lax.psum(outs[GROUP], "head")

    back, grad_states, rows = {}, {}, {}
    for chunk in (3, 1, 2):
        b, s, r = output_grad_states(
            size, (chunk,), features, *common, queries, out_grad, gain, attended, sums
        )
        back[chunk], grad_states[chunk], rows[chunk] = b[0], s[0], r
    before = [(k, rows[k]) for k in (3, 1, 2)]
    b, s, gains = output_grad_states(
        size, (0,), features, *common, queries, out_grad, gain, attended, sums, before
    )
    back[0], grad_states[0] = b[0], s[0]

    distance = GROUP
    while distance < members:
        gains = gains + swap(gains, distance)
        distance *= 2

    leaving = travel(size, True, *common, me, grad_states, lambda: (gains,))
    query_grad, local_key, local_value = local_gradients(
        size, *common, queries, key_rows, value_rows, back, entering
    )
    key_grad, value_grad, gain_grad = final_gradients(
        size, *common, key_rows, value_rows, local_key, local_value, leaving
    )
    return query_grad, key_grad, value_grad, gain_grad.reshape(size.heads * size.dim)


def solution(mesh):
    rows = P("seq", "head")
    in_specs = (rows, rows, rows, P("seq"), P("head"), P("head"), rows)
    return jax.shard_map(
        local, mesh=mesh, in_specs=in_specs, out_specs=(rows, rows, rows, P("head")), check_vma=False
    )
```

```python
import jax
import jax.numpy as jnp
from jax import lax
from jax.experimental import pallas as pl
from jax.experimental.pallas import tpu as pltpu
from jax.sharding import PartitionSpec as P

GROUP = 4
INFO = 8
FAR = 1e9
f32 = jnp.float32
bf16 = jnp.bfloat16
HBM = pl.BlockSpec(memory_space=pltpu.HBM)
VMEM = pl.BlockSpec(memory_space=pltpu.VMEM)


def dot(a, b, over_a=1, over_b=0):
    return lax.dot_general(a, b, (((over_a,), (over_b,)), ((), ())), preferred_element_type=f32)


def halves(x):
    high = x.astype(bf16)
    return high, (x - high.astype(f32)).astype(bf16)


def decay(steps, span):
    return jnp.exp(-steps / span)


class Sizes:
    def __init__(self, queries, decay_span):
        self.rows = queries.shape[0]
        self.heads = decay_span.shape[0]
        self.features = queries.shape[1]
        self.dim = self.features // self.heads
        self.per = self.heads // GROUP
        self.wide = self.per * self.dim
        self.state = self.per * self.dim
        self.pad = -(-self.per // 8) * 8
        self.payload = jax.ShapeDtypeStruct((self.state + INFO, self.dim), f32)
        self.block = jax.ShapeDtypeStruct((self.rows, self.features), f32)
        self.gains = jax.ShapeDtypeStruct((GROUP * self.pad, self.dim), f32)


def markers(seg_ref, size):
    row = seg_ref[...].astype(f32) + 1.0
    return row, jnp.broadcast_to(row, (size.dim, size.rows)).T


def position(size):
    return lax.broadcasted_iota(jnp.int32, (size.rows, size.dim), 0).astype(f32)


def pair_weight(row, size):
    shape = (size.rows, size.rows)
    here = jnp.broadcast_to(row, shape)
    at = lax.broadcasted_iota(jnp.int32, shape, 0)
    by = lax.broadcasted_iota(jnp.int32, shape, 1)
    live = jnp.logical_and(at >= by, here == here.T)
    return jnp.maximum(at - by, 0).astype(f32), live


def info_rows(first_row, second_row, dim):
    index = lax.broadcasted_iota(jnp.int32, (INFO, dim), 0)
    return jnp.where(index == 0, first_row, jnp.where(index == 1, second_row, 0.0))


def partners():
    me = jnp.bitwise_and(lax.axis_index("seq"), GROUP - 1)
    return [jnp.bitwise_xor(me, k) for k in range(GROUP)]


def places(backward):
    return [GROUP - 1 - p for p in partners()] if backward else partners()


def columns(size, group, h=None):
    if h is None:
        return pl.ds(pl.multiple_of(group * size.wide, size.wide), size.wide)
    return pl.ds(pl.multiple_of(group * size.wide + h * size.dim, size.dim), size.dim)


def span_of(spans_ref, size, group, h):
    return spans_ref[pl.ds(group * size.per + h, 1), :]


def square_span(span, size):
    return span[:, :1] if size.rows != size.dim else span


def call(body, name, inputs, outputs, flops, moved, scratch=(), in_specs=None, out_specs=None):
    return pl.pallas_call(
        body,
        out_shape=outputs,
        in_specs=in_specs if in_specs is not None else [VMEM] * len(inputs),
        out_specs=out_specs if out_specs is not None else [VMEM] * len(outputs),
        scratch_shapes=list(scratch),
        compiler_params=pltpu.CompilerParams(vmem_limit_bytes=16 * 1024 * 1024),
        cost_estimate=pl.CostEstimate(flops=flops, bytes_accessed=moved, transcendentals=0),
        name=name,
    )(*inputs)


def key_value_states(size, chunks, seg, spans, key_rows, value_rows):
    n = len(chunks)

    def body(seg_ref, spans_ref, key_hbm, value_hbm, *refs):
        outs, (keys, values, sems) = refs[:n], refs[n:]
        group = partners()
        copies = []
        for c, chunk in enumerate(chunks):
            here = columns(size, group[chunk])
            pair = (
                pltpu.make_async_copy(key_hbm.at[:, here], keys.at[c], sems.at[0, c]),
                pltpu.make_async_copy(value_hbm.at[:, here], values.at[c], sems.at[1, c]),
            )
            for copy in pair:
                copy.start()
            copies.append(pair)
        row, mark = markers(seg_ref, size)
        last, first = mark[size.rows - 1 :, :], mark[:1, :]
        ahead = (size.rows - 1.0) - position(size)
        for c, chunk in enumerate(chunks):
            for copy in copies[c]:
                copy.wait()
            for h in range(size.per):
                cols = slice(h * size.dim, (h + 1) * size.dim)
                span = span_of(spans_ref, size, group[chunk], h)
                weight = jnp.where(mark == last, decay(ahead, span), 0.0)
                key = keys[c, :, cols]
                high, low = halves(values[c, :, cols].astype(f32) * weight)
                outs[c][cols, :] = dot(
                    jnp.concatenate([key, key], 0), jnp.concatenate([high, low], 0), 0, 0
                )
            outs[c][size.state :, :] = info_rows(last, first, size.dim)

    held = (n, size.rows, size.wide)
    return call(
        body, "states", (seg, spans, key_rows, value_rows), [size.payload] * n,
        n * size.per * 4 * size.rows * size.dim * size.dim, n * size.wide * size.rows * 8,
        [pltpu.VMEM(held, bf16), pltpu.VMEM(held, bf16), pltpu.SemaphoreType.DMA((2, n))],
        [VMEM, VMEM, HBM, HBM],
    )


def nearby_attended(size, seg, spans, queries, key_rows, value_rows):
    def body(seg_ref, spans_ref, query_ref, key_ref, value_ref, out_ref):
        row, _ = markers(seg_ref, size)
        gap, live = pair_weight(row, size)
        for h in range(size.heads):
            cols = slice(h * size.dim, (h + 1) * size.dim)
            span = square_span(spans_ref[h : h + 1, :], size)
            weight = jnp.where(live, decay(gap, span), 0.0)
            query, key, value = query_ref[:, cols], key_ref[:, cols], value_ref[:, cols]
            high, low = halves(dot(query, key, 1, 1) * weight)
            out_ref[:, cols] = dot(
                jnp.concatenate([high, low], 1), jnp.concatenate([value, value], 0)
            )

    return call(
        body, "nearby", (seg, spans, queries, key_rows, value_rows), [size.block],
        size.heads * 6 * size.rows * size.dim * size.dim, size.features * size.rows * 10,
    )[0]


def group_total(size, backward, spans, parts, riders=()):
    mark_row = size.state + (1 if backward else 0)

    def body(spans_ref, *refs):
        ins, out = refs[:GROUP], refs[GROUP + len(riders)]
        place = places(backward)
        marks = [ref[mark_row : mark_row + 1, :] for ref in ins]
        end = marks[0]
        for mark in marks[1:]:
            end = jnp.minimum(end, mark) if backward else jnp.maximum(end, mark)
        me = partners()[0]
        for h in range(size.per):
            cols = slice(h * size.dim, (h + 1) * size.dim)
            span = span_of(spans_ref, size, me, h)
            total = None
            for k in range(GROUP):
                steps = ((GROUP - 1 - place[k]) * size.rows).astype(f32)
                factor = jnp.where(marks[k] == end, decay(steps, span), 0.0)
                term = factor * ins[k][cols, :]
                total = term if total is None else total + term
            out[cols, :] = total
        out[size.state :, :] = info_rows(end, end, size.dim)
        if riders:
            refs[-1][...] = refs[GROUP][...] + refs[GROUP + 1][...]

    outputs = [size.payload] + ([size.gains] if riders else [])
    return call(
        body, "total", (spans, *parts, *riders), outputs,
        size.state * size.dim * 8, size.state * size.dim * 20,
    )


def group_prefixes(size, backward, spans, parts, entering, riders=()):
    mark_row = size.state + (1 if backward else 0)
    extra = sum(r.shape[0] for r in riders)

    def body(spans_ref, *refs):
        ins, enter = refs[:GROUP], refs[GROUP]
        rides, outs = refs[GROUP + 1 : GROUP + 1 + len(riders)], refs[GROUP + 1 + len(riders) :]
        place = places(backward)
        me = partners()[0]
        marks = [ref[mark_row : mark_row + 1, :] for ref in ins]
        outer = enter[size.state : size.state + 1, :]
        if backward:
            outer = jnp.where(outer == 0.0, FAR, outer)
        carry = []
        for to in range(GROUP):
            now = outer
            for k in range(GROUP):
                if backward:
                    now = jnp.where(place[k] < place[to], jnp.minimum(now, marks[k]), now)
                else:
                    now = jnp.where(place[k] < place[to], jnp.maximum(now, marks[k]), now)
            carry.append(now)
            outs[to][size.state : size.state + INFO, :] = info_rows(now, now, size.dim)
            at = size.state + INFO
            for ride in rides:
                outs[to][at : at + ride.shape[0], :] = ride[...]
                at += ride.shape[0]
        for h in range(size.per):
            cols = slice(h * size.dim, (h + 1) * size.dim)
            span = span_of(spans_ref, size, me, h)
            for to in range(GROUP):
                steps = (place[to] * size.rows).astype(f32)
                total = jnp.where(outer == carry[to], decay(steps, span), 0.0) * enter[cols, :]
                for k in range(GROUP):
                    if k == to:
                        continue
                    gap = place[to] - 1 - place[k]
                    steps = (jnp.maximum(gap, 0) * size.rows).astype(f32)
                    live = jnp.logical_and(marks[k] == carry[to], gap >= 0)
                    total += jnp.where(live, decay(steps, span), 0.0) * ins[k][cols, :]
                outs[to][cols, :] = total

    shape = jax.ShapeDtypeStruct((size.state + INFO + extra, size.dim), f32)
    return call(
        body, "prefixes", (spans, *parts, entering, *riders), [shape] * GROUP,
        size.state * size.dim * 40, size.state * size.dim * 36,
    )


def whole_attended(size, seg, spans, queries, out_grad, gain, near, entering):
    def body(seg_ref, spans_ref, query_ref, grad_ref, gain_ref, near_ref, *refs):
        states, (out_ref, sums_ref) = refs[:GROUP], refs[GROUP:]
        group = partners()
        _, mark = markers(seg_ref, size)
        behind = position(size) + 1.0
        square = jnp.zeros((size.rows, size.dim), f32)
        cross = jnp.zeros((size.rows, size.dim), f32)
        for c in range(GROUP):
            live = mark == states[c][size.state : size.state + 1, :]
            for h in range(size.per):
                here = columns(size, group[c], h)
                span = span_of(spans_ref, size, group[c], h)
                weight = jnp.where(live, decay(behind, span), 0.0)
                query = query_ref[:, here]
                high, low = halves(states[c][h * size.dim : (h + 1) * size.dim, :])
                inter = dot(jnp.concatenate([query, query], 1), jnp.concatenate([high, low], 0))
                out = near_ref[:, here] + weight * inter
                out_ref[:, here] = out
                square += out * out
                cross += grad_ref[:, here].astype(f32) * gain_ref[:, here] * out
        square = jnp.sum(square.T, axis=0, keepdims=True)
        cross = jnp.sum(cross.T, axis=0, keepdims=True)
        index = lax.broadcasted_iota(jnp.int32, (8, size.rows), 0)
        sums_ref[...] = jnp.where(index == 0, square, jnp.where(index == 1, cross, 0.0))

    return call(
        body, "attended", (seg, spans, queries, out_grad, gain, near, *entering),
        [size.block, jax.ShapeDtypeStruct((8, size.rows), f32)],
        size.heads * 4 * size.rows * size.dim * size.dim, size.features * size.rows * 16,
    )


def output_grad_states(size, chunks, norm, seg, spans, queries, out_grad, gain, attended, sums, before=()):
    n = len(chunks)

    def body(seg_ref, spans_ref, query_ref, grad_ref, gain_ref, att_ref, sums_ref, *refs):
        outs = refs[len(before) :]
        group = partners()
        row, mark = markers(seg_ref, size)
        last, first = mark[size.rows - 1 :, :], mark[:1, :]
        wide = (size.dim, size.rows)
        square = jnp.broadcast_to(sums_ref[0:1, :], wide).T
        cross = jnp.broadcast_to(sums_ref[1:2, :], wide).T
        inv = lax.rsqrt(square / norm + 1e-06)
        pull = inv * inv * inv * cross / norm
        gone = position(size)
        for c, chunk in enumerate(chunks):
            back_ref, state_ref = outs[2 * c : 2 * c + 2]
            index = lax.broadcasted_iota(jnp.int32, (size.pad, size.dim), 0)
            gains = jnp.zeros((size.pad, size.dim), f32)
            for h in range(size.per):
                here = columns(size, group[chunk], h)
                cols = slice(h * size.dim, (h + 1) * size.dim)
                span = span_of(spans_ref, size, group[chunk], h)
                weight = jnp.where(mark == first, decay(gone, span), 0.0)
                grad = grad_ref[:, here].astype(f32) * inv
                att = att_ref[:, here]
                back = gain_ref[:, here] * grad - att * pull
                back_ref[:, cols] = back
                gains = jnp.where(index == h, jnp.sum(grad * att, axis=0, keepdims=True), gains)
                query = query_ref[:, here]
                high, low = halves(back * weight)
                state_ref[cols, :] = dot(
                    jnp.concatenate([query, query], 0), jnp.concatenate([high, low], 0), 0, 0
                )
            state_ref[size.state :, :] = info_rows(last, first, size.dim)
            outs[2 * n][chunk * size.pad : (chunk + 1) * size.pad, :] = gains
        for chunk in range(GROUP):
            if chunk not in chunks:
                at = slice(chunk * size.pad, (chunk + 1) * size.pad)
                held = refs[0][at, :] if before else jnp.zeros((size.pad, size.dim), f32)
                outs[2 * n][at, :] = held

    part = jax.ShapeDtypeStruct((size.rows, size.wide), f32)
    outs = call(
        body, "back", (seg, spans, queries, out_grad, gain, attended, sums, *before),
        [part, size.payload] * n + [size.gains],
        n * size.per * 4 * size.rows * size.dim * size.dim, n * size.wide * size.rows * 16,
    )
    return outs[0 : 2 * n : 2], outs[1 : 2 * n : 2], outs[2 * n]


def local_gradients(size, seg, spans, queries, key_rows, value_rows, back, entering):
    def body(seg_ref, spans_ref, query_ref, key_ref, value_ref, *refs):
        backs, states = refs[:GROUP], refs[GROUP : 2 * GROUP]
        out_hbm, local_key, local_value, done, sems = refs[2 * GROUP :]
        group = partners()
        row, mark = markers(seg_ref, size)
        gap, pairs = pair_weight(row, size)
        behind = position(size) + 1.0
        copies = []
        for c in range(GROUP):
            live = mark == states[c][size.state : size.state + 1, :]
            for h in range(size.per):
                here = columns(size, group[c], h)
                cols = slice(h * size.dim, (h + 1) * size.dim)
                span = span_of(spans_ref, size, group[c], h)
                weight = jnp.where(pairs, decay(gap, square_span(span, size)), 0.0)
                query, key, value = query_ref[:, here], key_ref[:, here], value_ref[:, here]
                high, low = halves(backs[c][:, cols])
                grads = dot(
                    jnp.concatenate([high, low], 1), jnp.concatenate([value, value], 1), 1, 1
                )
                grads_high, grads_low = halves(grads * weight)
                part = dot(
                    jnp.concatenate([grads_high, grads_low], 1), jnp.concatenate([key, key], 0)
                )
                state_high, state_low = halves(states[c][cols, :])
                inter = dot(
                    jnp.concatenate([high, high, low], 1),
                    jnp.concatenate([state_high, state_low, state_high], 1),
                    1, 1,
                )
                into = jnp.where(live, decay(behind, span), 0.0)
                done[c, :, cols] = (part + into * inter).astype(bf16)
                local_key[:, here] = dot(
                    jnp.concatenate([grads_high, grads_low], 0),
                    jnp.concatenate([query, query], 0),
                    0, 0,
                )
                score_high, score_low = halves(dot(query, key, 1, 1) * weight)
                local_value[:, here] = dot(
                    jnp.concatenate([score_high, score_high, score_low], 0),
                    jnp.concatenate([high, low, high], 0),
                    0, 0,
                )
            copies.append(
                pltpu.make_async_copy(
                    done.at[c], out_hbm.at[:, columns(size, group[c])], sems.at[c]
                )
            )
            copies[c].start()
        for copy in copies:
            copy.wait()

    return call(
        body, "gradients", (seg, spans, queries, key_rows, value_rows, *back, *entering),
        [jax.ShapeDtypeStruct((size.rows, size.features), bf16), size.block, size.block],
        size.heads * 26 * size.rows * size.dim * size.dim, size.features * size.rows * 24,
        [pltpu.VMEM((GROUP, size.rows, size.wide), bf16), pltpu.SemaphoreType.DMA((GROUP,))],
        None, [HBM, VMEM, VMEM],
    )


def final_gradients(size, seg, spans, key_rows, value_rows, local_key, local_value, entering):
    def body(seg_ref, spans_ref, key_ref, value_ref, local_key_ref, local_value_ref, *refs):
        states, (keys_hbm, values_hbm, gain_hbm) = refs[:GROUP], refs[GROUP : GROUP + 3]
        keys, values, gains, sems = refs[GROUP + 3 :]
        group = partners()
        _, mark = markers(seg_ref, size)
        left = size.rows - position(size)
        for c in range(GROUP):
            for h in range(size.per):
                total = None
                for k in range(GROUP):
                    at = size.state + INFO + (k ^ c) * size.pad + h
                    row = states[k][at : at + 1, :]
                    total = row if total is None else total + row
                gains[:, columns(size, group[c], h)] = total
        copies = [pltpu.make_async_copy(gains, gain_hbm, sems.at[2, 0])]
        copies[0].start()
        for c in range(GROUP):
            live = mark == states[c][size.state : size.state + 1, :]
            for h in range(size.per):
                here = columns(size, group[c], h)
                cols = slice(h * size.dim, (h + 1) * size.dim)
                span = span_of(spans_ref, size, group[c], h)
                weight = jnp.where(live, decay(left, span), 0.0)
                key, value = key_ref[:, here], value_ref[:, here]
                high, low = halves(states[c][cols, :])
                from_values = dot(
                    jnp.concatenate([value, value], 1), jnp.concatenate([high, low], 1), 1, 1
                )
                from_keys = dot(jnp.concatenate([key, key], 1), jnp.concatenate([high, low], 0))
                keys[c, :, cols] = (local_key_ref[:, here] + weight * from_values).astype(bf16)
                values[c, :, cols] = (local_value_ref[:, here] + weight * from_keys).astype(bf16)
            here = columns(size, group[c])
            for copy in (
                pltpu.make_async_copy(keys.at[c], keys_hbm.at[:, here], sems.at[0, c]),
                pltpu.make_async_copy(values.at[c], values_hbm.at[:, here], sems.at[1, c]),
            ):
                copy.start()
                copies.append(copy)
        for copy in copies:
            copy.wait()

    shape = jax.ShapeDtypeStruct((size.rows, size.features), bf16)
    held = pltpu.VMEM((GROUP, size.rows, size.wide), bf16)
    return call(
        body, "final", (seg, spans, key_rows, value_rows, local_key, local_value, *entering),
        [shape, shape, jax.ShapeDtypeStruct((1, size.features), f32)],
        size.heads * 8 * size.rows * size.dim * size.dim, size.features * size.rows * 24,
        [held, held, pltpu.VMEM((1, size.features), f32), pltpu.SemaphoreType.DMA((3, GROUP))],
        None, [HBM] * 3,
    )


def swap(array, distance):
    members = lax.axis_size("seq")
    return lax.ppermute(array, "seq", [(i, i ^ distance) for i in range(members)])


def shifted(array, by):
    members = lax.axis_size("seq")
    pairs = [(i, i + by) for i in range(members) if 0 <= i + by < members]
    return lax.ppermute(array, "seq", pairs)


def from_other_groups(size, backward, decay_span, total):
    members = lax.axis_size("seq")
    tokens = GROUP * size.rows
    longest = members * size.rows // 4
    needed = max(longest - 2, 0) // tokens + 1
    way = -GROUP if backward else GROUP
    result = shifted(total, way)
    reach = 1
    mine = lax.dynamic_slice(decay_span, (partners()[0] * size.per,), (size.per,))
    while reach < needed:
        incoming = shifted(result, way * reach)
        passes = incoming[size.state, 0] == result[size.state, 0]
        factor = jnp.where(passes, jnp.exp(-(reach * tokens) / mine), 0.0)
        factor = jnp.repeat(factor, size.dim)[:, None]
        result = result.at[: size.state].add(factor * incoming[: size.state])
        reach *= 2
    return result


def local(queries, key_rows, value_rows, segment_ids, decay_span, norm_gain, out_grad):
    size = Sizes(queries, decay_span)
    norm = size.features * lax.axis_size("head")
    members = lax.axis_size("seq")
    seg = segment_ids.reshape(1, size.rows)
    gain = norm_gain.reshape(1, size.features)
    spans = jnp.broadcast_to(decay_span[:, None], (size.heads, size.dim))
    common = (seg, spans)

    sent = key_value_states(size, (3, 1, 2), *common, key_rows, value_rows)
    kept = key_value_states(size, (0,), *common, key_rows, value_rows)
    states = [kept[0], sent[1], sent[2], sent[0]]
    near = nearby_attended(size, *common, queries, key_rows, value_rows)
    parts = [states[0]] + [swap(states[k], k) for k in range(1, GROUP)]
    total = group_total(size, False, spans, parts)[0]
    outer = from_other_groups(size, False, decay_span, total)
    outs = group_prefixes(size, False, spans, parts, outer)
    entering = [outs[0]] + [swap(outs[k], k) for k in range(1, GROUP)]

    attended, sums = whole_attended(size, *common, queries, out_grad, gain, near, entering)
    sums = lax.psum(sums, "head")
    normed = (norm, *common, queries, out_grad, gain, attended, sums)
    back_sent, sent, gains = output_grad_states(size, (3, 1, 2), *normed)
    back_kept, kept, gains = output_grad_states(size, (0,), *normed, (gains,))
    back = [back_kept[0], back_sent[1], back_sent[2], back_sent[0]]
    states = [kept[0], sent[1], sent[2], sent[0]]

    parts = [states[0]] + [swap(states[k], k) for k in range(1, GROUP)]
    distance, arrived = GROUP, jnp.zeros_like(gains)
    while distance < members:
        gains = gains + arrived if distance > GROUP else gains
        arrived = swap(gains, distance)
        distance *= 2
    total, gains = group_total(size, True, spans, parts, (gains, arrived))
    outer = from_other_groups(size, True, decay_span, total)
    outs = group_prefixes(size, True, spans, parts, outer, (gains,))
    leaving = [outs[0]] + [swap(outs[k], k) for k in range(1, GROUP)]

    query_grad, local_key, local_value = local_gradients(
        size, *common, queries, key_rows, value_rows, back, entering
    )
    key_grad, value_grad, gain_grad = final_gradients(
        size, *common, key_rows, value_rows, local_key, local_value, leaving
    )
    return query_grad, key_grad, value_grad, gain_grad.reshape(size.features)


def solution(mesh):
    rows = P("seq", "head")
    in_specs = (rows, rows, rows, P("seq"), P("head"), P("head"), rows)
    return jax.shard_map(
        local, mesh=mesh, in_specs=in_specs, out_specs=(rows, rows, rows, P("head")), check_vma=False
    )
```

```python
import jax
import jax.numpy as jnp
from jax import lax
from jax.experimental import pallas as pl
from jax.experimental.pallas import tpu as pltpu
from jax.sharding import PartitionSpec as P

GROUP = 4
INFO = 8
FAR = 1e9
f32 = jnp.float32
bf16 = jnp.bfloat16
HBM = pl.BlockSpec(memory_space=pltpu.HBM)
VMEM = pl.BlockSpec(memory_space=pltpu.VMEM)


def dot(a, b, over_a=1, over_b=0):
    return lax.dot_general(a, b, (((over_a,), (over_b,)), ((), ())), preferred_element_type=f32)


def halves(x):
    high = x.astype(bf16)
    return high, (x - high.astype(f32)).astype(bf16)


def decay(steps, span):
    return jnp.exp(-steps / span)


class Sizes:
    def __init__(self, queries, decay_span):
        self.rows = queries.shape[0]
        self.heads = decay_span.shape[0]
        self.features = queries.shape[1]
        self.dim = self.features // self.heads
        self.per = self.heads // GROUP
        self.wide = self.per * self.dim
        self.pad = -(-self.per // 8) * 8
        self.waves = 2 if self.per % 2 == 0 else 1
        self.each = self.per // self.waves
        self.state = self.each * self.dim
        self.payload = jax.ShapeDtypeStruct((self.state + INFO, self.dim), f32)
        self.block = jax.ShapeDtypeStruct((self.rows, self.features), f32)
        self.gains = jax.ShapeDtypeStruct((GROUP * self.pad, self.dim), f32)


def position(size):
    return lax.broadcasted_iota(jnp.int32, (size.rows, size.dim), 0).astype(f32)


def pair_weight(mark, size):
    shape = (size.rows, size.rows)
    here = mark if size.rows == size.dim else jnp.broadcast_to(mark[:, :1], shape)
    at = lax.broadcasted_iota(jnp.int32, shape, 0)
    by = lax.broadcasted_iota(jnp.int32, shape, 1)
    live = jnp.logical_and(at >= by, here == here.T)
    return jnp.maximum(at - by, 0).astype(f32), live


def info_rows(first_row, second_row, dim):
    index = lax.broadcasted_iota(jnp.int32, (INFO, dim), 0)
    return jnp.where(index == 0, first_row, jnp.where(index == 1, second_row, 0.0))


def partners():
    me = jnp.bitwise_and(lax.axis_index("seq"), GROUP - 1)
    return [jnp.bitwise_xor(me, k) for k in range(GROUP)]


def places(backward):
    return [GROUP - 1 - p for p in partners()] if backward else partners()


def columns(size, group, h=None):
    if h is None:
        return pl.ds(pl.multiple_of(group * size.wide, size.wide), size.wide)
    return pl.ds(pl.multiple_of(group * size.wide + h * size.dim, size.dim), size.dim)


def wave_heads(size, wave):
    return [(wave * size.each + i, slice(i * size.dim, (i + 1) * size.dim)) for i in range(size.each)]


def all_pieces(size):
    return [(chunk, wave) for wave in range(size.waves) for chunk in range(GROUP)]


def span_of(spans_ref, size, group, h):
    return spans_ref[pl.ds(group * size.per + h, 1), :]


def square_span(span, size):
    return span[:, :1] if size.rows != size.dim else span


def call(body, name, inputs, outputs, flops, moved, scratch=(), in_specs=None, out_specs=None, vmem=16):
    return pl.pallas_call(
        body,
        out_shape=outputs,
        in_specs=in_specs if in_specs is not None else [VMEM] * len(inputs),
        out_specs=out_specs if out_specs is not None else [VMEM] * len(outputs),
        scratch_shapes=list(scratch),
        compiler_params=pltpu.CompilerParams(vmem_limit_bytes=vmem * 1024 * 1024),
        cost_estimate=pl.CostEstimate(flops=flops, bytes_accessed=moved, transcendentals=0),
        name=name,
    )(*inputs)


def key_value_states(size, pieces, seg, decay_span, key_rows, value_rows):
    n = len(pieces)
    wide = size.each * size.dim

    def body(seg_hbm, span_hbm, key_hbm, value_hbm, *refs):
        outs, mark_ref, spans_ref = refs[:n], refs[n], refs[n + 1]
        seg_row, span_row, keys, values, sems = refs[n + 2 :]
        group = partners()
        small = (
            pltpu.make_async_copy(seg_hbm, seg_row, sems.at[2, 0]),
            pltpu.make_async_copy(span_hbm, span_row, sems.at[2, 1]),
        )
        copies = []
        for copy in small:
            copy.start()
        for c, (chunk, wave) in enumerate(pieces):
            here = pl.ds(pl.multiple_of(group[chunk] * size.wide + wave * wide, wide), wide)
            pair = (
                pltpu.make_async_copy(key_hbm.at[:, here], keys.at[c], sems.at[0, c]),
                pltpu.make_async_copy(value_hbm.at[:, here], values.at[c], sems.at[1, c]),
            )
            for copy in pair:
                copy.start()
            copies.append(pair)
        for copy in small:
            copy.wait()
        mark = jnp.broadcast_to(seg_row[...].astype(f32) + 1.0, (size.dim, size.rows)).T
        mark_ref[...] = mark
        spans_ref[...] = jnp.broadcast_to(span_row[...], (size.dim, size.heads)).T
        last, first = mark[size.rows - 1 :, :], mark[:1, :]
        ahead = (size.rows - 1.0) - position(size)
        for c, (chunk, wave) in enumerate(pieces):
            for copy in copies[c]:
                copy.wait()
            for h, cols in wave_heads(size, wave):
                span = span_of(spans_ref, size, group[chunk], h)
                weight = jnp.where(mark == last, decay(ahead, span), 0.0)
                key = keys[c, :, cols]
                high, low = halves(values[c, :, cols].astype(f32) * weight)
                outs[c][cols, :] = dot(
                    jnp.concatenate([key, key], 0), jnp.concatenate([high, low], 0), 0, 0
                )
            outs[c][size.state :, :] = info_rows(last, first, size.dim)

    held = (n, size.rows, wide)
    outs = call(
        body, "states", (seg, decay_span.reshape(1, size.heads), key_rows, value_rows),
        [size.payload] * n + [
            jax.ShapeDtypeStruct((size.rows, size.dim), f32),
            jax.ShapeDtypeStruct((size.heads, size.dim), f32),
        ],
        n * size.each * 4 * size.rows * size.dim * size.dim, n * wide * size.rows * 8,
        [
            pltpu.VMEM((1, size.rows), jnp.int32),
            pltpu.VMEM((1, size.heads), f32),
            pltpu.VMEM(held, bf16),
            pltpu.VMEM(held, bf16),
            pltpu.SemaphoreType.DMA((3, max(n, 2))),
        ],
        [HBM] * 4, vmem=60,
    )
    return outs[:n], outs[n], outs[n + 1]


def nearby_attended(size, mark, spans, queries, key_rows, value_rows):
    def body(mark_ref, spans_ref, query_ref, key_ref, value_ref, out_ref):
        gap, live = pair_weight(mark_ref[...], size)
        for h in range(size.heads):
            cols = slice(h * size.dim, (h + 1) * size.dim)
            span = square_span(spans_ref[h : h + 1, :], size)
            weight = jnp.where(live, decay(gap, span), 0.0)
            query, key, value = query_ref[:, cols], key_ref[:, cols], value_ref[:, cols]
            high, low = halves(dot(query, key, 1, 1) * weight)
            out_ref[:, cols] = dot(
                jnp.concatenate([high, low], 1), jnp.concatenate([value, value], 0)
            )

    return call(
        body, "nearby", (mark, spans, queries, key_rows, value_rows), [size.block],
        size.heads * 6 * size.rows * size.dim * size.dim, size.features * size.rows * 10,
    )[0]


def group_total(size, backward, wave, spans, parts, riders=()):
    mark_row = size.state + (1 if backward else 0)

    def body(spans_ref, *refs):
        ins, out = refs[:GROUP], refs[GROUP + len(riders)]
        place = places(backward)
        marks = [ref[mark_row : mark_row + 1, :] for ref in ins]
        end = marks[0]
        for mark in marks[1:]:
            end = jnp.minimum(end, mark) if backward else jnp.maximum(end, mark)
        me = partners()[0]
        for h, cols in wave_heads(size, wave):
            span = span_of(spans_ref, size, me, h)
            total = None
            for k in range(GROUP):
                steps = ((GROUP - 1 - place[k]) * size.rows).astype(f32)
                factor = jnp.where(marks[k] == end, decay(steps, span), 0.0)
                term = factor * ins[k][cols, :]
                total = term if total is None else total + term
            out[cols, :] = total
        out[size.state :, :] = info_rows(end, end, size.dim)
        if riders:
            refs[-1][...] = refs[GROUP][...] + refs[GROUP + 1][...]

    outputs = [size.payload] + ([size.gains] if riders else [])
    return call(
        body, "total", (spans, *parts, *riders), outputs,
        size.state * size.dim * 8, size.state * size.dim * 20,
    )


def group_prefixes(size, backward, wave, spans, parts, entering, riders=()):
    mark_row = size.state + (1 if backward else 0)
    extra = sum(r.shape[0] for r in riders)

    def body(spans_ref, *refs):
        ins, enter = refs[:GROUP], refs[GROUP]
        rides, outs = refs[GROUP + 1 : GROUP + 1 + len(riders)], refs[GROUP + 1 + len(riders) :]
        place = places(backward)
        me = partners()[0]
        marks = [ref[mark_row : mark_row + 1, :] for ref in ins]
        block, members = lax.axis_index("seq"), lax.axis_size("seq")
        first = block >= members - GROUP if backward else block < GROUP
        outer = jnp.where(first, FAR if backward else 0.0, enter[size.state : size.state + 1, :])
        enters = jnp.where(first, 0.0, 1.0)
        carry = []
        for to in range(GROUP):
            now = outer
            for k in range(GROUP):
                if backward:
                    now = jnp.where(place[k] < place[to], jnp.minimum(now, marks[k]), now)
                else:
                    now = jnp.where(place[k] < place[to], jnp.maximum(now, marks[k]), now)
            carry.append(now)
            outs[to][size.state : size.state + INFO, :] = info_rows(now, now, size.dim)
            at = size.state + INFO
            for ride in rides:
                outs[to][at : at + ride.shape[0], :] = ride[...]
                at += ride.shape[0]
        for h, cols in wave_heads(size, wave):
            span = span_of(spans_ref, size, me, h)
            for to in range(GROUP):
                steps = (place[to] * size.rows).astype(f32)
                factor = jnp.where(outer == carry[to], enters * decay(steps, span), 0.0)
                total = factor * enter[cols, :]
                for k in range(GROUP):
                    if k == to:
                        continue
                    gap = place[to] - 1 - place[k]
                    steps = (jnp.maximum(gap, 0) * size.rows).astype(f32)
                    live = jnp.logical_and(marks[k] == carry[to], gap >= 0)
                    total += jnp.where(live, decay(steps, span), 0.0) * ins[k][cols, :]
                outs[to][cols, :] = total

    shape = jax.ShapeDtypeStruct((size.state + INFO + extra, size.dim), f32)
    return call(
        body, "prefixes", (spans, *parts, entering, *riders), [shape] * GROUP,
        size.state * size.dim * 40, size.state * size.dim * 36,
    )


def whole_attended(size, mark, spans, queries, out_grad, gain, near, entering):
    def body(mark_ref, spans_ref, query_ref, grad_ref, gain_ref, near_ref, *refs):
        states, (out_ref, sums_ref) = refs[:-2], refs[-2:]
        group = partners()
        mark = mark_ref[...]
        behind = position(size) + 1.0
        square = jnp.zeros((size.rows, size.dim), f32)
        cross = jnp.zeros((size.rows, size.dim), f32)
        live = mark == states[0][size.state : size.state + 1, :]
        for i, (c, wave) in enumerate(all_pieces(size)):
            for h, cols in wave_heads(size, wave):
                here = columns(size, group[c], h)
                span = span_of(spans_ref, size, group[c], h)
                weight = jnp.where(live, decay(behind, span), 0.0)
                query = query_ref[:, here]
                high, low = halves(states[i][cols, :])
                inter = dot(jnp.concatenate([query, query], 1), jnp.concatenate([high, low], 0))
                out = near_ref[:, here] + weight * inter
                out_ref[:, here] = out
                square += out * out
                cross += grad_ref[:, here].astype(f32) * gain_ref[:, here] * out
        square = jnp.sum(square.T, axis=0, keepdims=True)
        cross = jnp.sum(cross.T, axis=0, keepdims=True)
        index = lax.broadcasted_iota(jnp.int32, (8, size.rows), 0)
        sums_ref[...] = jnp.where(index == 0, square, jnp.where(index == 1, cross, 0.0))

    return call(
        body, "attended", (mark, spans, queries, out_grad, gain, near, *entering),
        [size.block, jax.ShapeDtypeStruct((8, size.rows), f32)],
        size.heads * 4 * size.rows * size.dim * size.dim, size.features * size.rows * 16,
    )


def output_grad_states(size, pieces, norm, mark, spans, queries, out_grad, gain, attended, sums, count=False):
    n = len(pieces)

    def body(mark_ref, spans_ref, query_ref, grad_ref, gain_ref, att_ref, sums_ref, *outs):
        group = partners()
        mark = mark_ref[...]
        last, first = mark[size.rows - 1 :, :], mark[:1, :]
        wide = (size.dim, size.rows)
        square = jnp.broadcast_to(sums_ref[0:1, :], wide).T
        cross = jnp.broadcast_to(sums_ref[1:2, :], wide).T
        inv = lax.rsqrt(square / norm + 1e-06)
        pull = inv * inv * inv * cross / norm
        gone = position(size)
        for c, (chunk, wave) in enumerate(pieces):
            back_ref, state_ref = outs[2 * c : 2 * c + 2]
            for h, cols in wave_heads(size, wave):
                here = columns(size, group[chunk], h)
                span = span_of(spans_ref, size, group[chunk], h)
                weight = jnp.where(mark == first, decay(gone, span), 0.0)
                grad = grad_ref[:, here].astype(f32) * inv
                att = att_ref[:, here]
                back = gain_ref[:, here] * grad - att * pull
                back_ref[:, cols] = back
                query = query_ref[:, here]
                high, low = halves(back * weight)
                state_ref[cols, :] = dot(
                    jnp.concatenate([query, query], 0), jnp.concatenate([high, low], 0), 0, 0
                )
            state_ref[size.state :, :] = info_rows(last, first, size.dim)
        if count:
            outs[2 * n][...] = jnp.zeros(size.gains.shape, f32)
            for chunk in range(GROUP):
                for h in range(size.per):
                    here = columns(size, group[chunk], h)
                    part = grad_ref[:, here].astype(f32) * inv * att_ref[:, here]
                    at = chunk * size.pad + h
                    outs[2 * n][at : at + 1, :] = jnp.sum(part, axis=0, keepdims=True)

    part = jax.ShapeDtypeStruct((size.rows, size.state), f32)
    outs = call(
        body, "back", (mark, spans, queries, out_grad, gain, attended, sums),
        [part, size.payload] * n + [size.gains] * count,
        n * size.each * 4 * size.rows * size.dim * size.dim, n * size.state * size.rows * 16,
    )
    return outs[0 : 2 * n : 2], outs[1 : 2 * n : 2], outs[2 * n :]


def local_gradients(size, mark, spans, queries, key_rows, value_rows, back, entering):
    def body(mark_ref, spans_ref, query_ref, key_ref, value_ref, *refs):
        n = GROUP * size.waves
        backs, states = refs[:n], refs[n : 2 * n]
        out_hbm, local_key, local_value, done, sems = refs[2 * n :]
        group = partners()
        mark = mark_ref[...]
        gap, pairs = pair_weight(mark, size)
        behind = position(size) + 1.0
        copies = []
        live = mark == states[0][size.state : size.state + 1, :]
        for c in range(GROUP):
            for h in range(size.per):
                here = columns(size, group[c], h)
                piece = c + GROUP * (h // size.each)
                cols = slice(h % size.each * size.dim, (h % size.each + 1) * size.dim)
                span = span_of(spans_ref, size, group[c], h)
                weight = jnp.where(pairs, decay(gap, square_span(span, size)), 0.0)
                query, key, value = query_ref[:, here], key_ref[:, here], value_ref[:, here]
                high, low = halves(backs[piece][:, cols])
                grads = dot(
                    jnp.concatenate([high, low], 1), jnp.concatenate([value, value], 1), 1, 1
                )
                grads_high, grads_low = halves(grads * weight)
                part = dot(
                    jnp.concatenate([grads_high, grads_low], 1), jnp.concatenate([key, key], 0)
                )
                state_high, state_low = halves(states[piece][cols, :])
                inter = dot(
                    jnp.concatenate([high, high, low], 1),
                    jnp.concatenate([state_high, state_low, state_high], 1),
                    1, 1,
                )
                into = jnp.where(live, decay(behind, span), 0.0)
                done[c, :, h * size.dim : (h + 1) * size.dim] = (part + into * inter).astype(bf16)
                local_key[:, here] = dot(
                    jnp.concatenate([grads_high, grads_low], 0),
                    jnp.concatenate([query, query], 0),
                    0, 0,
                )
                score_high, score_low = halves(dot(query, key, 1, 1) * weight)
                local_value[:, here] = dot(
                    jnp.concatenate([score_high, score_high, score_low], 0),
                    jnp.concatenate([high, low, high], 0),
                    0, 0,
                )
            copies.append(
                pltpu.make_async_copy(
                    done.at[c], out_hbm.at[:, columns(size, group[c])], sems.at[c]
                )
            )
            copies[c].start()
        for copy in copies:
            copy.wait()

    return call(
        body, "gradients", (mark, spans, queries, key_rows, value_rows, *back, *entering),
        [jax.ShapeDtypeStruct((size.rows, size.features), bf16), size.block, size.block],
        size.heads * 26 * size.rows * size.dim * size.dim, size.features * size.rows * 24,
        [pltpu.VMEM((GROUP, size.rows, size.wide), bf16), pltpu.SemaphoreType.DMA((GROUP,))],
        None, [HBM, VMEM, VMEM],
    )


def final_gradients(size, mark, spans, key_rows, value_rows, local_key, local_value, entering):
    def body(mark_ref, spans_ref, key_ref, value_ref, local_key_ref, local_value_ref, *refs):
        n = GROUP * size.waves
        states, (keys_hbm, values_hbm, gain_hbm) = refs[:n], refs[n : n + 3]
        keys, values, gains, sems = refs[n + 3 :]
        group = partners()
        mark = mark_ref[...]
        left = size.rows - position(size)
        for c in range(GROUP):
            for h in range(size.per):
                total = None
                for k in range(GROUP):
                    at = size.state + INFO + (k ^ c) * size.pad + h
                    row = states[n - GROUP + k][at : at + 1, :]
                    total = row if total is None else total + row
                gains[:, columns(size, group[c], h)] = total
        copies = [pltpu.make_async_copy(gains, gain_hbm, sems.at[2, 0])]
        copies[0].start()
        live = mark == states[0][size.state : size.state + 1, :]
        for c in range(GROUP):
            for h in range(size.per):
                here = columns(size, group[c], h)
                piece = c + GROUP * (h // size.each)
                at = slice(h % size.each * size.dim, (h % size.each + 1) * size.dim)
                cols = slice(h * size.dim, (h + 1) * size.dim)
                span = span_of(spans_ref, size, group[c], h)
                weight = jnp.where(live, decay(left, span), 0.0)
                key, value = key_ref[:, here], value_ref[:, here]
                high, low = halves(states[piece][at, :])
                from_values = dot(
                    jnp.concatenate([value, value], 1), jnp.concatenate([high, low], 1), 1, 1
                )
                from_keys = dot(jnp.concatenate([key, key], 1), jnp.concatenate([high, low], 0))
                keys[c, :, cols] = (local_key_ref[:, here] + weight * from_values).astype(bf16)
                values[c, :, cols] = (local_value_ref[:, here] + weight * from_keys).astype(bf16)
            here = columns(size, group[c])
            for copy in (
                pltpu.make_async_copy(keys.at[c], keys_hbm.at[:, here], sems.at[0, c]),
                pltpu.make_async_copy(values.at[c], values_hbm.at[:, here], sems.at[1, c]),
            ):
                copy.start()
                copies.append(copy)
        for copy in copies:
            copy.wait()

    shape = jax.ShapeDtypeStruct((size.rows, size.features), bf16)
    held = pltpu.VMEM((GROUP, size.rows, size.wide), bf16)
    return call(
        body, "final", (mark, spans, key_rows, value_rows, local_key, local_value, *entering),
        [shape, shape, jax.ShapeDtypeStruct((1, size.features), f32)],
        size.heads * 8 * size.rows * size.dim * size.dim, size.features * size.rows * 24,
        [held, held, pltpu.VMEM((1, size.features), f32), pltpu.SemaphoreType.DMA((3, GROUP))],
        None, [HBM] * 3,
    )


def swap(array, distance):
    members = lax.axis_size("seq")
    return lax.ppermute(array, "seq", [(i, i ^ distance) for i in range(members)])


def exchange(payloads):
    return [payloads[0]] + [swap(payloads[k], k) for k in range(1, GROUP)]


def shifted(array, by):
    members = lax.axis_size("seq")
    pairs = [(i, i + by) for i in range(members) if 0 <= i + by < members]
    return lax.ppermute(array, "seq", pairs)


def from_other_groups(size, backward, wave, decay_span, total):
    members = lax.axis_size("seq")
    tokens = GROUP * size.rows
    longest = members * size.rows // 4
    needed = max(longest - 2, 0) // tokens + 1
    way = -GROUP if backward else GROUP
    if needed == 1:
        pairs = [(i, (i + way) % members) for i in range(members)]
        return lax.ppermute(total, "seq", pairs)
    result = shifted(total, way)
    reach = 1
    start = partners()[0] * size.per + wave * size.each
    mine = lax.dynamic_slice(decay_span, (start,), (size.each,))
    while reach < needed:
        incoming = shifted(result, way * reach)
        passes = incoming[size.state, 0] == result[size.state, 0]
        factor = jnp.where(passes, jnp.exp(-(reach * tokens) / mine), 0.0)
        factor = jnp.repeat(factor, size.dim)[:, None]
        result = result.at[: size.state].add(factor * incoming[: size.state])
        reach *= 2
    return result


def local(queries, key_rows, value_rows, segment_ids, decay_span, norm_gain, out_grad):
    size = Sizes(queries, decay_span)
    norm = size.features * lax.axis_size("head")
    members = lax.axis_size("seq")
    seg = segment_ids.reshape(1, size.rows)
    gain = norm_gain.reshape(1, size.features)
    waves = range(size.waves)
    sent = [[(chunk, wave) for chunk in (3, 1, 2)] for wave in waves]
    kept = [(0, wave) for wave in waves]
    every = all_pieces(size)

    states = {}
    for pieces in [*sent, kept]:
        outs, mark, spans = key_value_states(size, pieces, seg, decay_span, key_rows, value_rows)
        states |= zip(pieces, outs)
        if pieces is sent[0]:
            common = (mark, spans)
    spans = common[1]
    near = nearby_attended(size, *common, queries, key_rows, value_rows)
    entering = {}
    parts = {w: exchange({k: states[k, w] for k in range(GROUP)}) for w in waves}
    totals = {w: group_total(size, False, w, spans, parts[w])[0] for w in waves}
    outer = {w: from_other_groups(size, False, w, decay_span, totals[w]) for w in waves}
    for w in waves:
        outs = exchange(group_prefixes(size, False, w, spans, parts[w], outer[w]))
        entering |= {(k, w): outs[k] for k in range(GROUP)}
    entering = [entering[piece] for piece in every]

    attended, sums = whole_attended(size, *common, queries, out_grad, gain, near, entering)
    sums = lax.psum(sums, "head")
    back, states, gains = {}, {}, []
    for pieces in [*sent, kept]:
        backs, payloads, rows = output_grad_states(
            size, pieces, norm, *common, queries, out_grad, gain, attended, sums, pieces is sent[-1]
        )
        back |= zip(pieces, backs)
        states |= zip(pieces, payloads)
        gains += rows
    back = [back[piece] for piece in every]

    parts = {w: exchange({k: states[k, w] for k in range(GROUP)}) for w in waves}
    gains, distance = gains[0], GROUP
    while distance << size.waves < members:
        gains = gains + swap(gains, distance)
        distance *= 2
    leaving, totals = {}, {}
    for w in waves:
        riders = (gains, swap(gains, distance)) if distance < members else ()
        totals[w], *rows = group_total(size, True, w, spans, parts[w], riders)
        gains = rows[0] if rows else gains
        distance *= 2
    riders = {w: (gains,) if w == size.waves - 1 else () for w in waves}
    outer = {w: from_other_groups(size, True, w, decay_span, totals[w]) for w in waves}
    for w in waves:
        outs = exchange(group_prefixes(size, True, w, spans, parts[w], outer[w], riders[w]))
        leaving |= {(k, w): outs[k] for k in range(GROUP)}
    leaving = [leaving[piece] for piece in every]

    query_grad, local_key, local_value = local_gradients(
        size, *common, queries, key_rows, value_rows, back, entering
    )
    key_grad, value_grad, gain_grad = final_gradients(
        size, *common, key_rows, value_rows, local_key, local_value, leaving
    )
    return query_grad, key_grad, value_grad, gain_grad.reshape(size.features)


def solution(mesh):
    rows = P("seq", "head")
    in_specs = (rows, rows, rows, P("seq"), P("head"), P("head"), rows)
    return jax.shard_map(
        local, mesh=mesh, in_specs=in_specs, out_specs=(rows, rows, rows, P("head")), check_vma=False
    )
```

```python
import jax
import jax.numpy as jnp
from jax import lax
from jax.experimental import pallas as pl
from jax.experimental.pallas import tpu as pltpu
from jax.sharding import PartitionSpec as P

GROUP = 4
INFO = 8
FAR = 1e9
NEVER = 1e30
f32 = jnp.float32
bf16 = jnp.bfloat16
HBM = pl.BlockSpec(memory_space=pltpu.HBM)
VMEM = pl.BlockSpec(memory_space=pltpu.VMEM)


def dot(a, b, over_a=1, over_b=0):
    return lax.dot_general(a, b, (((over_a,), (over_b,)), ((), ())), preferred_element_type=f32)


def halves(x):
    high = x.astype(bf16)
    return high, (x - high.astype(f32)).astype(bf16)


def decay(steps, rate):
    return jnp.exp(steps * rate)


class Sizes:
    def __init__(self, queries, decay_span):
        self.rows = queries.shape[0]
        self.heads = decay_span.shape[0]
        self.features = queries.shape[1]
        self.dim = self.features // self.heads
        self.per = self.heads // GROUP
        self.wide = self.per * self.dim
        self.pad = -(-self.heads // 8) * 8
        self.waves = 2 if self.per % 2 == 0 else 1
        self.each = self.per // self.waves
        self.state = self.each * self.dim
        self.payload = jax.ShapeDtypeStruct((self.state + INFO, self.dim), f32)
        self.block = jax.ShapeDtypeStruct((self.rows, self.features), f32)
        self.gains = jax.ShapeDtypeStruct((self.pad, self.dim), f32)


def position(size):
    return lax.broadcasted_iota(jnp.int32, (size.rows, size.dim), 0).astype(f32)


def steps_if(live, steps):
    return jnp.where(live, steps, NEVER)


def pair_steps(mark, size, earlier=1):
    shape = (size.rows, size.rows)
    here = mark if size.rows == size.dim else jnp.broadcast_to(mark[:, :1], shape)
    later = lax.broadcasted_iota(jnp.int32, shape, 1 - earlier)
    gap = later - lax.broadcasted_iota(jnp.int32, shape, earlier)
    return steps_if(jnp.logical_and(gap >= 0, here == here.T), gap.astype(f32))


def token_product(a, high, low):
    turned = a.T
    return dot(jnp.concatenate([turned, turned], 1), jnp.concatenate([high, low], 0))


def info_rows(first_row, second_row, dim):
    index = lax.broadcasted_iota(jnp.int32, (INFO, dim), 0)
    return jnp.where(index == 0, first_row, jnp.where(index == 1, second_row, 0.0))


def partners():
    me = jnp.bitwise_and(lax.axis_index("seq"), GROUP - 1)
    return [jnp.bitwise_xor(me, k) for k in range(GROUP)]


def places(backward):
    return [GROUP - 1 - p for p in partners()] if backward else partners()


def columns(size, group, h=None):
    if h is None:
        return pl.ds(pl.multiple_of(group * size.wide, size.wide), size.wide)
    return pl.ds(pl.multiple_of(group * size.wide + h * size.dim, size.dim), size.dim)


def wave_heads(size, wave):
    return [(wave * size.each + i, slice(i * size.dim, (i + 1) * size.dim)) for i in range(size.each)]


def all_pieces(size):
    return [(chunk, wave) for wave in range(size.waves) for chunk in range(GROUP)]


def rate_of(rates_ref, size, group, h):
    return rates_ref[pl.ds(group * size.per + h, 1), :]


def square_rate(rate, size):
    return rate[:, :1] if size.rows != size.dim else rate


def call(body, name, inputs, outputs, flops, moved, scratch=(), in_specs=None, out_specs=None, vmem=16):
    return pl.pallas_call(
        body,
        out_shape=outputs,
        in_specs=in_specs if in_specs is not None else [VMEM] * len(inputs),
        out_specs=out_specs if out_specs is not None else [VMEM] * len(outputs),
        scratch_shapes=list(scratch),
        compiler_params=pltpu.CompilerParams(vmem_limit_bytes=vmem * 1024 * 1024),
        cost_estimate=pl.CostEstimate(flops=flops, bytes_accessed=moved, transcendentals=0),
        name=name,
    )(*inputs)


def state_payloads(size, pieces, mark, rates_ref, group, outs, key_of, value_of):
    last, first = mark[size.rows - 1 :, :], mark[:1, :]
    ahead = steps_if(mark == last, (size.rows - 1.0) - position(size))
    for c, (chunk, wave) in enumerate(pieces):
        for h, cols in wave_heads(size, wave):
            weight = decay(ahead, rate_of(rates_ref, size, group[chunk], h))
            high, low = halves(value_of(c, h, cols).astype(f32) * weight)
            outs[c][cols, :] = token_product(key_of(c, h, cols), high, low)
        outs[c][size.state :, :] = info_rows(last, first, size.dim)


def first_states(size, pieces, seg, decay_span, key_rows, value_rows):
    n = len(pieces)
    wide = size.each * size.dim

    def body(seg_hbm, span_hbm, key_hbm, value_hbm, *refs):
        outs, mark_ref, rates_ref = refs[:n], refs[n], refs[n + 1]
        seg_row, span_row, keys, values, sems = refs[n + 2 :]
        group = partners()
        small = (
            pltpu.make_async_copy(seg_hbm, seg_row, sems.at[2, 0]),
            pltpu.make_async_copy(span_hbm, span_row, sems.at[2, 1]),
        )
        copies = []
        for copy in small:
            copy.start()
        for c, (chunk, wave) in enumerate(pieces):
            here = pl.ds(pl.multiple_of(group[chunk] * size.wide + wave * wide, wide), wide)
            copies += [
                pltpu.make_async_copy(key_hbm.at[:, here], keys.at[c], sems.at[0, c]),
                pltpu.make_async_copy(value_hbm.at[:, here], values.at[c], sems.at[1, c]),
            ]
        for copy in copies:
            copy.start()
        for copy in small:
            copy.wait()
        mark = jnp.broadcast_to(seg_row[...].astype(f32) + 1.0, (size.dim, size.rows)).T
        mark_ref[...] = mark
        rates_ref[...] = jnp.broadcast_to(-1.0 / span_row[...], (size.dim, size.heads)).T
        for copy in copies:
            copy.wait()
        state_payloads(
            size, pieces, mark, rates_ref, group, outs,
            lambda c, h, cols: keys[c, :, cols], lambda c, h, cols: values[c, :, cols],
        )

    held = (n, size.rows, wide)
    outs = call(
        body, "states", (seg, decay_span.reshape(1, size.heads), key_rows, value_rows),
        [size.payload] * n + [
            jax.ShapeDtypeStruct((size.rows, size.dim), f32),
            jax.ShapeDtypeStruct((size.heads, size.dim), f32),
        ],
        n * size.each * 4 * size.rows * size.dim * size.dim, n * wide * size.rows * 8,
        [
            pltpu.VMEM((1, size.rows), jnp.int32),
            pltpu.VMEM((1, size.heads), f32),
            pltpu.VMEM(held, bf16),
            pltpu.VMEM(held, bf16),
            pltpu.SemaphoreType.DMA((3, max(n, 2))),
        ],
        [HBM] * 4, vmem=60,
    )
    return outs[:n], outs[n], outs[n + 1]


def more_states(size, pieces, mark, rates, key_rows, value_rows):
    def body(mark_ref, rates_ref, key_ref, value_ref, *outs):
        group = partners()

        def head(ref):
            return lambda c, h, cols: ref[:, columns(size, group[pieces[c][0]], h)]

        state_payloads(
            size, pieces, mark_ref[...], rates_ref, group, outs, head(key_ref), head(value_ref)
        )

    n = len(pieces)
    return call(
        body, "states", (mark, rates, key_rows, value_rows), [size.payload] * n,
        n * size.each * 4 * size.rows * size.dim * size.dim, n * size.state * size.rows * 8,
    )


def nearby_attended(size, mark, rates, queries, key_rows, value_rows):
    def body(mark_ref, rates_ref, query_ref, key_ref, value_ref, out_ref):
        gap = pair_steps(mark_ref[...], size)
        for h in range(size.heads):
            cols = slice(h * size.dim, (h + 1) * size.dim)
            rate = square_rate(rates_ref[h : h + 1, :], size)
            weight = decay(gap, rate)
            query, key, value = query_ref[:, cols], key_ref[:, cols], value_ref[:, cols]
            high, low = halves(dot(query, key, 1, 1) * weight)
            out_ref[:, cols] = dot(
                jnp.concatenate([high, low], 1), jnp.concatenate([value, value], 0)
            )

    return call(
        body, "nearby", (mark, rates, queries, key_rows, value_rows), [size.block],
        size.heads * 6 * size.rows * size.dim * size.dim, size.features * size.rows * 10,
    )[0]


def put_rows(ref, at, rows):
    ref[at : at + rows.shape[0], :] = rows


def group_total(size, backward, wave, rates, parts, extra=0, riders=()):
    mark_row = size.state + (1 if backward else 0)

    def body(rates_ref, *refs):
        ins, out = refs[:GROUP], refs[-1]
        place = places(backward)
        marks = [ref[mark_row : mark_row + 1, :] for ref in ins]
        end = marks[0]
        for mark in marks[1:]:
            end = jnp.minimum(end, mark) if backward else jnp.maximum(end, mark)
        steps = [
            steps_if(marks[k] == end, ((GROUP - 1 - place[k]) * size.rows).astype(f32))
            for k in range(GROUP)
        ]
        me = partners()[0]
        for h, cols in wave_heads(size, wave):
            rate = rate_of(rates_ref, size, me, h)
            total = None
            for k in range(GROUP):
                term = decay(steps[k], rate) * ins[k][cols, :]
                total = term if total is None else total + term
            out[cols, :] = total
        put_rows(out, size.state, info_rows(end, end, size.dim))
        if extra:
            rows = refs[GROUP][...] if riders else jnp.zeros((extra, size.dim), f32)
            put_rows(out, size.state + INFO, rows)

    return call(
        body, "total", (rates, *parts, *riders),
        [jax.ShapeDtypeStruct((size.state + INFO + extra, size.dim), f32)],
        size.state * size.dim * 8, size.state * size.dim * 20,
    )[0]


def group_prefixes(size, backward, wave, rates, parts, entering, extra=0, riders=(), collect=()):
    mark_row = size.state + (1 if backward else 0)

    def body(rates_ref, *refs):
        ins, enter = refs[:GROUP], refs[GROUP]
        rides, outs = refs[GROUP + 1 : GROUP + 1 + len(riders)], refs[GROUP + 1 + len(riders) :]
        if collect:
            outs[-1][...] = outs[0][...] + enter[size.state + INFO :, :]
            outs = outs[1:-1]
        place = places(backward)
        me = partners()[0]
        marks = [ref[mark_row : mark_row + 1, :] for ref in ins]
        block, members = lax.axis_index("seq"), lax.axis_size("seq")
        first = block >= members - GROUP if backward else block < GROUP
        outer = jnp.where(first, FAR if backward else 0.0, enter[size.state : size.state + 1, :])
        steps = []
        for to in range(GROUP):
            now = outer
            for k in range(GROUP):
                if backward:
                    now = jnp.where(place[k] < place[to], jnp.minimum(now, marks[k]), now)
                else:
                    now = jnp.where(place[k] < place[to], jnp.maximum(now, marks[k]), now)
            put_rows(outs[to], size.state, info_rows(now, now, size.dim))
            if extra:
                total = jnp.zeros((extra, size.dim), f32)
                for ride in rides:
                    total = total + ride[...]
                put_rows(outs[to], size.state + INFO, total)
            far = (place[to] * size.rows).astype(f32)
            steps.append([steps_if(jnp.logical_and(outer == now, jnp.logical_not(first)), far)])
            for k in range(GROUP):
                gap = place[to] - 1 - place[k]
                live = jnp.logical_and(marks[k] == now, gap >= 0)
                steps[to].append(steps_if(live, (gap * size.rows).astype(f32)))
        for h, cols in wave_heads(size, wave):
            rate = rate_of(rates_ref, size, me, h)
            for to in range(GROUP):
                total = decay(steps[to][0], rate) * enter[cols, :]
                for k in range(GROUP):
                    if k != to:
                        total += decay(steps[to][1 + k], rate) * ins[k][cols, :]
                outs[to][cols, :] = total

    shape = jax.ShapeDtypeStruct((size.state + INFO + extra, size.dim), f32)
    return call(
        body, "prefixes", (rates, *parts, entering, *riders, *collect),
        [shape] * GROUP + [size.gains] * len(collect),
        size.state * size.dim * 40, size.state * size.dim * 36,
    )


def whole_attended(size, mark, rates, queries, out_grad, gain, near, entering):
    def body(mark_ref, rates_ref, query_ref, grad_ref, gain_ref, near_ref, *refs):
        states, (out_ref, sums_ref) = refs[:-2], refs[-2:]
        group = partners()
        mark = mark_ref[...]
        behind = steps_if(mark == states[0][size.state : size.state + 1, :], position(size) + 1.0)
        square = jnp.zeros((size.rows, size.dim), f32)
        cross = jnp.zeros((size.rows, size.dim), f32)
        for i, (c, wave) in enumerate(all_pieces(size)):
            for h, cols in wave_heads(size, wave):
                here = columns(size, group[c], h)
                rate = rate_of(rates_ref, size, group[c], h)
                weight = decay(behind, rate)
                query = query_ref[:, here]
                high, low = halves(states[i][cols, :])
                inter = dot(jnp.concatenate([query, query], 1), jnp.concatenate([high, low], 0))
                out = near_ref[:, here] + weight * inter
                out_ref[:, here] = out
                square += out * out
                cross += grad_ref[:, here].astype(f32) * gain_ref[:, here] * out
        square = jnp.sum(square.T, axis=0, keepdims=True)
        cross = jnp.sum(cross.T, axis=0, keepdims=True)
        index = lax.broadcasted_iota(jnp.int32, (8, size.rows), 0)
        sums_ref[...] = jnp.where(index == 0, square, jnp.where(index == 1, cross, 0.0))

    return call(
        body, "attended", (mark, rates, queries, out_grad, gain, near, *entering),
        [size.block, jax.ShapeDtypeStruct((8, size.rows), f32)],
        size.heads * 4 * size.rows * size.dim * size.dim, size.features * size.rows * 16,
    )


def output_grad_states(size, pieces, norm, mark, rates, queries, out_grad, gain, attended, sums, count=False):
    n = len(pieces)

    def body(mark_ref, rates_ref, query_ref, grad_ref, gain_ref, att_ref, sums_ref, *outs):
        group = partners()
        mark = mark_ref[...]
        last, first = mark[size.rows - 1 :, :], mark[:1, :]
        wide = (size.dim, size.rows)
        square = jnp.broadcast_to(sums_ref[0:1, :], wide).T
        cross = jnp.broadcast_to(sums_ref[1:2, :], wide).T
        inv = lax.rsqrt(square / norm + 1e-06)
        pull = inv * inv * inv * cross / norm
        gone = steps_if(mark == first, position(size))
        for c, (chunk, wave) in enumerate(pieces):
            back_ref, state_ref = outs[2 * c : 2 * c + 2]
            for h, cols in wave_heads(size, wave):
                here = columns(size, group[chunk], h)
                rate = rate_of(rates_ref, size, group[chunk], h)
                weight = decay(gone, rate)
                grad = grad_ref[:, here].astype(f32) * inv
                att = att_ref[:, here]
                back = gain_ref[:, here] * grad - att * pull
                back_ref[:, cols] = back
                high, low = halves(back * weight)
                state_ref[cols, :] = token_product(query_ref[:, here], high, low)
            put_rows(state_ref, size.state, info_rows(last, first, size.dim))
            put_rows(state_ref, size.state + INFO, jnp.zeros((size.pad, size.dim), f32))
        if count:
            outs[2 * n][...] = jnp.zeros(size.gains.shape, f32)
            for chunk in range(GROUP):
                for h in range(size.per):
                    here = columns(size, group[chunk], h)
                    part = grad_ref[:, here].astype(f32) * inv * att_ref[:, here]
                    at = chunk * size.per + h
                    outs[2 * n][at : at + 1, :] = jnp.sum(part, axis=0, keepdims=True)

    part = jax.ShapeDtypeStruct((size.rows, size.state), f32)
    outs = call(
        body, "back", (mark, rates, queries, out_grad, gain, attended, sums),
        [part, jax.ShapeDtypeStruct((size.state + INFO + size.pad, size.dim), f32)] * n + [size.gains] * count,
        n * size.each * 4 * size.rows * size.dim * size.dim, n * size.state * size.rows * 16,
    )
    return outs[0 : 2 * n : 2], outs[1 : 2 * n : 2], outs[2 * n :]


def local_gradients(size, mark, rates, queries, key_rows, value_rows, back, entering):
    def body(mark_ref, rates_ref, query_ref, key_ref, value_ref, *refs):
        n = GROUP * size.waves
        backs, states = refs[:n], refs[n : 2 * n]
        out_hbm, local_key, local_value, done, sems = refs[2 * n :]
        group = partners()
        mark = mark_ref[...]
        gap, turned_gap = pair_steps(mark, size), pair_steps(mark, size, 0)
        behind = steps_if(mark == states[0][size.state : size.state + 1, :], position(size) + 1.0)
        copies = []
        for c in range(GROUP):
            for h in range(size.per):
                here = columns(size, group[c], h)
                piece = c + GROUP * (h // size.each)
                cols = slice(h % size.each * size.dim, (h % size.each + 1) * size.dim)
                rate = rate_of(rates_ref, size, group[c], h)
                rows_rate = square_rate(rate, size)
                weight, turned_weight = decay(gap, rows_rate), decay(turned_gap, rows_rate)
                query, key, value = query_ref[:, here], key_ref[:, here], value_ref[:, here]
                high, low = halves(backs[piece][:, cols])
                both, values = jnp.concatenate([high, low], 1), jnp.concatenate([value, value], 1)
                grads_high, grads_low = halves(dot(both, values, 1, 1) * weight)
                part = dot(
                    jnp.concatenate([grads_high, grads_low], 1), jnp.concatenate([key, key], 0)
                )
                state_high, state_low = halves(states[piece][cols, :])
                inter = dot(
                    jnp.concatenate([high, high, low], 1),
                    jnp.concatenate([state_high, state_low, state_high], 1),
                    1, 1,
                )
                done[c, :, h * size.dim : (h + 1) * size.dim] = (
                    part + decay(behind, rate) * inter
                ).astype(bf16)
                grads_high, grads_low = halves(dot(values, both, 1, 1) * turned_weight)
                local_key[:, here] = dot(
                    jnp.concatenate([grads_high, grads_low], 1),
                    jnp.concatenate([query, query], 0),
                )
                score_high, score_low = halves(dot(key, query, 1, 1) * turned_weight)
                local_value[:, here] = dot(
                    jnp.concatenate([score_high, score_high, score_low], 1),
                    jnp.concatenate([high, low, high], 0),
                )
            copies.append(
                pltpu.make_async_copy(
                    done.at[c], out_hbm.at[:, columns(size, group[c])], sems.at[c]
                )
            )
            copies[c].start()
        for copy in copies:
            copy.wait()

    return call(
        body, "gradients", (mark, rates, queries, key_rows, value_rows, *back, *entering),
        [jax.ShapeDtypeStruct((size.rows, size.features), bf16), size.block, size.block],
        size.heads * 26 * size.rows * size.dim * size.dim, size.features * size.rows * 24,
        [pltpu.VMEM((GROUP, size.rows, size.wide), bf16), pltpu.SemaphoreType.DMA((GROUP,))],
        None, [HBM, VMEM, VMEM],
    )


def final_gradients(size, mark, rates, key_rows, value_rows, local_key, local_value, entering):
    def body(mark_ref, rates_ref, key_ref, value_ref, local_key_ref, local_value_ref, *refs):
        n = GROUP * size.waves
        states, (keys_hbm, values_hbm, gain_hbm) = refs[:n], refs[n : n + 3]
        keys, values, gains, sems = refs[n + 3 :]
        group = partners()
        mark = mark_ref[...]
        left = steps_if(mark == states[0][size.state : size.state + 1, :], size.rows - position(size))
        for c in range(GROUP):
            for h in range(size.per):
                total = None
                for k in range(GROUP):
                    at = size.state + INFO + (k ^ c) * size.per + h
                    row = states[n - GROUP + k][at : at + 1, :]
                    total = row if total is None else total + row
                gains[:, columns(size, group[c], h)] = total
        copies = [pltpu.make_async_copy(gains, gain_hbm, sems.at[2, 0])]
        copies[0].start()
        for c in range(GROUP):
            for h in range(size.per):
                here = columns(size, group[c], h)
                piece = c + GROUP * (h // size.each)
                at = slice(h % size.each * size.dim, (h % size.each + 1) * size.dim)
                cols = slice(h * size.dim, (h + 1) * size.dim)
                rate = rate_of(rates_ref, size, group[c], h)
                weight = decay(left, rate)
                key, value = key_ref[:, here], value_ref[:, here]
                high, low = halves(states[piece][at, :])
                from_values = dot(
                    jnp.concatenate([value, value], 1), jnp.concatenate([high, low], 1), 1, 1
                )
                from_keys = dot(jnp.concatenate([key, key], 1), jnp.concatenate([high, low], 0))
                keys[c, :, cols] = (local_key_ref[:, here] + weight * from_values).astype(bf16)
                values[c, :, cols] = (local_value_ref[:, here] + weight * from_keys).astype(bf16)
            here = columns(size, group[c])
            for copy in (
                pltpu.make_async_copy(keys.at[c], keys_hbm.at[:, here], sems.at[0, c]),
                pltpu.make_async_copy(values.at[c], values_hbm.at[:, here], sems.at[1, c]),
            ):
                copy.start()
                copies.append(copy)
        for copy in copies:
            copy.wait()

    shape = jax.ShapeDtypeStruct((size.rows, size.features), bf16)
    held = pltpu.VMEM((GROUP, size.rows, size.wide), bf16)
    return call(
        body, "final", (mark, rates, key_rows, value_rows, local_key, local_value, *entering),
        [shape, shape, jax.ShapeDtypeStruct((1, size.features), f32)],
        size.heads * 8 * size.rows * size.dim * size.dim, size.features * size.rows * 24,
        [held, held, pltpu.VMEM((1, size.features), f32), pltpu.SemaphoreType.DMA((3, GROUP))],
        None, [HBM] * 3,
    )


def swap(array, distance):
    members = lax.axis_size("seq")
    return lax.ppermute(array, "seq", [(i, i ^ distance) for i in range(members)])


def exchange(payloads):
    return [payloads[0]] + [swap(payloads[k], k) for k in range(1, GROUP)]


def shifted(array, by):
    members = lax.axis_size("seq")
    pairs = [(i, i + by) for i in range(members) if 0 <= i + by < members]
    return lax.ppermute(array, "seq", pairs)


def cyclic(array, by):
    members = lax.axis_size("seq")
    return lax.ppermute(array, "seq", [(i, (i + by) % members) for i in range(members)])


def reach_of_documents(size):
    longest = lax.axis_size("seq") * size.rows // 4
    return max(longest - 2, 0) // (GROUP * size.rows) + 1


def from_other_groups(size, backward, wave, decay_span, total):
    needed = reach_of_documents(size)
    way = -GROUP if backward else GROUP
    if needed == 1:
        return cyclic(total, way)
    result = shifted(total, way)
    reach = 1
    start = partners()[0] * size.per + wave * size.each
    mine = lax.dynamic_slice(decay_span, (start,), (size.each,))
    while reach < needed:
        incoming = shifted(result, way * reach)
        passes = incoming[size.state, 0] == result[size.state, 0]
        factor = jnp.where(passes, jnp.exp(-(reach * GROUP * size.rows) / mine), 0.0)
        factor = jnp.repeat(factor, size.dim)[:, None]
        result = result.at[: size.state].add(factor * incoming[: size.state])
        reach *= 2
    return result


def local(queries, key_rows, value_rows, segment_ids, decay_span, norm_gain, out_grad):
    size = Sizes(queries, decay_span)
    norm = size.features * lax.axis_size("head")
    members = lax.axis_size("seq")
    seg = segment_ids.reshape(1, size.rows)
    gain = norm_gain.reshape(1, size.features)
    waves = range(size.waves)
    sent = [[(chunk, wave) for chunk in (3, 1, 2)] for wave in waves]
    kept = [(0, wave) for wave in waves]
    every = all_pieces(size)
    calls = [sent[0], sum(sent[1:], []) + kept]

    outs, mark, rates = first_states(size, calls[0], seg, decay_span, key_rows, value_rows)
    common = (mark, rates)
    states = dict(zip(calls[0], outs))
    states |= zip(calls[1], more_states(size, calls[1], *common, key_rows, value_rows))
    near = nearby_attended(size, *common, queries, key_rows, value_rows)
    entering = {}
    parts = {w: exchange({k: states[k, w] for k in range(GROUP)}) for w in waves}
    totals = {w: group_total(size, False, w, rates, parts[w]) for w in waves}
    outer = {w: from_other_groups(size, False, w, decay_span, totals[w]) for w in waves}
    for w in waves:
        outs = exchange(group_prefixes(size, False, w, rates, parts[w], outer[w]))
        entering |= {(k, w): outs[k] for k in range(GROUP)}
    entering = [entering[piece] for piece in every]

    attended, sums = whole_attended(size, *common, queries, out_grad, gain, near, entering)
    sums = lax.psum(sums, "head")
    back, states = {}, {}
    for pieces in calls:
        backs, payloads, gains = output_grad_states(
            size, pieces, norm, *common, queries, out_grad, gain, attended, sums, pieces is calls[1]
        )
        back |= zip(pieces, backs)
        states |= zip(pieces, payloads)
    back = [back[piece] for piece in every]

    parts = {w: exchange({k: states[k, w] for k in range(GROUP)}) for w in waves}
    leaving, summed = {}, 1
    rides = size.waves > 1 and reach_of_documents(size) == 1 and members > GROUP
    totals = {}
    for w in waves:
        riders = gains if rides and w == 0 else ()
        totals[w] = group_total(size, True, w, rates, parts[w], size.pad * rides, riders)
    outer = {w: from_other_groups(size, True, w, decay_span, totals[w]) for w in waves}
    for w in waves:
        if w < size.waves - 1:
            riders, collect = (), (gains if rides and w == 0 else ())
        else:
            while summed * GROUP < members:
                gains = [sum(gains), cyclic(sum(gains), -summed * GROUP)]
                summed *= 2
            riders, collect = gains, ()
        outs = group_prefixes(
            size, True, w, rates, parts[w], outer[w], size.pad, riders, collect
        )
        if collect:
            gains, summed = outs[GROUP:], 2
        outs = exchange(outs[:GROUP])
        leaving |= {(k, w): outs[k] for k in range(GROUP)}
    leaving = [leaving[piece] for piece in every]

    query_grad, local_key, local_value = local_gradients(
        size, *common, queries, key_rows, value_rows, back, entering
    )
    key_grad, value_grad, gain_grad = final_gradients(
        size, *common, key_rows, value_rows, local_key, local_value, leaving
    )
    return query_grad, key_grad, value_grad, gain_grad.reshape(size.features)


def solution(mesh):
    rows = P("seq", "head")
    in_specs = (rows, rows, rows, P("seq"), P("head"), P("head"), rows)
    return jax.shard_map(
        local, mesh=mesh, in_specs=in_specs, out_specs=(rows, rows, rows, P("head")), check_vma=False
    )
```

```python
import jax
import jax.numpy as jnp
from jax import lax
from jax.experimental import pallas as pl
from jax.experimental.pallas import tpu as pltpu
from jax.sharding import PartitionSpec as P

GROUP = 4
MARKS = 2
FAR = 1e9
NEVER = 1e30
f32 = jnp.float32
bf16 = jnp.bfloat16
HBM = pl.BlockSpec(memory_space=pltpu.HBM)
VMEM = pl.BlockSpec(memory_space=pltpu.VMEM)


def dot(a, b, over_a=1, over_b=0):
    return lax.dot_general(a, b, (((over_a,), (over_b,)), ((), ())), preferred_element_type=f32)


def halves(x):
    high = x.astype(bf16)
    return high, (x - high.astype(f32)).astype(bf16)


def decay(steps, rate):
    return jnp.exp(steps * rate)


class Sizes:
    def __init__(self, queries, decay_span):
        self.rows = queries.shape[0]
        self.heads = decay_span.shape[0]
        self.features = queries.shape[1]
        self.dim = self.features // self.heads
        self.per = self.heads // GROUP
        self.wide = self.per * self.dim
        self.info = -(-(MARKS + self.per) // 8) * 8
        self.waves = 2 if self.per % 2 == 0 else 1
        self.each = self.per // self.waves
        self.state = self.each * self.dim
        self.payload = jax.ShapeDtypeStruct((self.state + self.info, self.dim), f32)
        self.block = jax.ShapeDtypeStruct((self.rows, self.features), f32)
        self.rows_of_gain = jax.ShapeDtypeStruct((self.info, self.dim), f32)


def position(size):
    return lax.broadcasted_iota(jnp.int32, (size.rows, size.dim), 0).astype(f32)


def steps_if(live, steps):
    return jnp.where(live, steps, NEVER)


def pair_steps(mark, size, earlier=1):
    shape = (size.rows, size.rows)
    here = mark if size.rows == size.dim else jnp.broadcast_to(mark[:, :1], shape)
    later = lax.broadcasted_iota(jnp.int32, shape, 1 - earlier)
    gap = later - lax.broadcasted_iota(jnp.int32, shape, earlier)
    return steps_if(jnp.logical_and(gap >= 0, here == here.T), gap.astype(f32))


def token_product(a, high, low):
    turned = a.T
    return dot(jnp.concatenate([turned, turned], 1), jnp.concatenate([high, low], 0))


def info_rows(size, last, first, more=()):
    index = lax.broadcasted_iota(jnp.int32, (size.info, size.dim), 0)
    rows = jnp.zeros((size.info, size.dim), f32)
    for i, row in enumerate((last, first, *more)):
        rows = jnp.where(index == i, row, rows)
    return rows


def with_marks(size, last, first, rows):
    index = lax.broadcasted_iota(jnp.int32, (size.info, size.dim), 0)
    return jnp.where(index == 0, last, jnp.where(index == 1, first, rows))


def partners():
    me = jnp.bitwise_and(lax.axis_index("seq"), GROUP - 1)
    return [jnp.bitwise_xor(me, k) for k in range(GROUP)]


def places(backward):
    return [GROUP - 1 - p for p in partners()] if backward else partners()


def columns(size, group, h=None):
    if h is None:
        return pl.ds(pl.multiple_of(group * size.wide, size.wide), size.wide)
    return pl.ds(pl.multiple_of(group * size.wide + h * size.dim, size.dim), size.dim)


def wave_heads(size, wave):
    return [(wave * size.each + i, slice(i * size.dim, (i + 1) * size.dim)) for i in range(size.each)]


def wave_columns(size, h):
    return slice(h % size.each * size.dim, (h % size.each + 1) * size.dim)


def all_pieces(size):
    return [(chunk, wave) for wave in range(size.waves) for chunk in range(GROUP)]


def rate_of(rates_ref, size, group, h):
    return rates_ref[pl.ds(group * size.per + h, 1), :]


def square_rate(rate, size):
    return rate[:, :1] if size.rows != size.dim else rate


def call(body, name, inputs, outputs, flops, moved, scratch=(), in_specs=None, out_specs=None, vmem=16):
    return pl.pallas_call(
        body,
        out_shape=outputs,
        in_specs=in_specs if in_specs is not None else [VMEM] * len(inputs),
        out_specs=out_specs if out_specs is not None else [VMEM] * len(outputs),
        scratch_shapes=list(scratch),
        compiler_params=pltpu.CompilerParams(vmem_limit_bytes=vmem * 1024 * 1024),
        cost_estimate=pl.CostEstimate(flops=flops, bytes_accessed=moved, transcendentals=0),
        name=name,
    )(*inputs)


def state_payloads(size, pieces, mark, rates_ref, group, outs, key_of, value_of):
    last, first = mark[size.rows - 1 :, :], mark[:1, :]
    ahead = steps_if(mark == last, (size.rows - 1.0) - position(size))
    for c, (chunk, wave) in enumerate(pieces):
        for h, cols in wave_heads(size, wave):
            weight = decay(ahead, rate_of(rates_ref, size, group[chunk], h))
            high, low = halves(value_of(c, h, cols).astype(f32) * weight)
            outs[c][cols, :] = token_product(key_of(c, h, cols), high, low)
        outs[c][size.state :, :] = info_rows(size, last, first)


def first_states(size, pieces, seg, decay_span, key_rows, value_rows):
    n = len(pieces)
    wide = size.each * size.dim

    def body(seg_hbm, span_hbm, key_hbm, value_hbm, *refs):
        outs, mark_ref, rates_ref = refs[:n], refs[n], refs[n + 1]
        seg_row, span_row, keys, values, sems = refs[n + 2 :]
        group = partners()
        small = (
            pltpu.make_async_copy(seg_hbm, seg_row, sems.at[2, 0]),
            pltpu.make_async_copy(span_hbm, span_row, sems.at[2, 1]),
        )
        copies = []
        for copy in small:
            copy.start()
        for c, (chunk, wave) in enumerate(pieces):
            here = pl.ds(pl.multiple_of(group[chunk] * size.wide + wave * wide, wide), wide)
            copies += [
                pltpu.make_async_copy(key_hbm.at[:, here], keys.at[c], sems.at[0, c]),
                pltpu.make_async_copy(value_hbm.at[:, here], values.at[c], sems.at[1, c]),
            ]
        for copy in copies:
            copy.start()
        for copy in small:
            copy.wait()
        mark = jnp.broadcast_to(seg_row[...].astype(f32) + 1.0, (size.dim, size.rows)).T
        mark_ref[...] = mark
        rates_ref[...] = jnp.broadcast_to(-1.0 / span_row[...], (size.dim, size.heads)).T
        for copy in copies:
            copy.wait()
        state_payloads(
            size, pieces, mark, rates_ref, group, outs,
            lambda c, h, cols: keys[c, :, cols], lambda c, h, cols: values[c, :, cols],
        )

    held = (n, size.rows, wide)
    outs = call(
        body, "states", (seg, decay_span.reshape(1, size.heads), key_rows, value_rows),
        [size.payload] * n + [
            jax.ShapeDtypeStruct((size.rows, size.dim), f32),
            jax.ShapeDtypeStruct((size.heads, size.dim), f32),
        ],
        n * size.each * 4 * size.rows * size.dim * size.dim, n * wide * size.rows * 8,
        [
            pltpu.VMEM((1, size.rows), jnp.int32),
            pltpu.VMEM((1, size.heads), f32),
            pltpu.VMEM(held, bf16),
            pltpu.VMEM(held, bf16),
            pltpu.SemaphoreType.DMA((3, max(n, 2))),
        ],
        [HBM] * 4, vmem=60,
    )
    return outs[:n], outs[n], outs[n + 1]


def more_states(size, pieces, mark, rates, key_rows, value_rows):
    def body(mark_ref, rates_ref, key_ref, value_ref, *outs):
        group = partners()

        def head(ref):
            return lambda c, h, cols: ref[:, columns(size, group[pieces[c][0]], h)]

        state_payloads(
            size, pieces, mark_ref[...], rates_ref, group, outs, head(key_ref), head(value_ref)
        )

    n = len(pieces)
    return call(
        body, "states", (mark, rates, key_rows, value_rows), [size.payload] * n,
        n * size.each * 4 * size.rows * size.dim * size.dim, n * size.state * size.rows * 8,
    )


def nearby_attended(size, mark, rates, queries, key_rows, value_rows):
    def body(mark_ref, rates_ref, query_ref, key_ref, value_ref, out_ref):
        gap = pair_steps(mark_ref[...], size)
        for h in range(size.heads):
            cols = slice(h * size.dim, (h + 1) * size.dim)
            rate = square_rate(rates_ref[h : h + 1, :], size)
            weight = decay(gap, rate)
            query, key, value = query_ref[:, cols], key_ref[:, cols], value_ref[:, cols]
            high, low = halves(dot(query, key, 1, 1) * weight)
            out_ref[:, cols] = dot(
                jnp.concatenate([high, low], 1), jnp.concatenate([value, value], 0)
            )

    return call(
        body, "nearby", (mark, rates, queries, key_rows, value_rows), [size.block],
        size.heads * 6 * size.rows * size.dim * size.dim, size.features * size.rows * 10,
    )[0]


def put_rows(ref, at, rows):
    ref[at : at + rows.shape[0], :] = rows


def group_total(size, backward, wave, rates, parts):
    mark_row = size.state + (1 if backward else 0)

    def body(rates_ref, *refs):
        ins, out = refs[:GROUP], refs[GROUP]
        place = places(backward)
        marks = [ref[mark_row : mark_row + 1, :] for ref in ins]
        end = marks[0]
        for mark in marks[1:]:
            end = jnp.minimum(end, mark) if backward else jnp.maximum(end, mark)
        steps = [
            steps_if(marks[k] == end, ((GROUP - 1 - place[k]) * size.rows).astype(f32))
            for k in range(GROUP)
        ]
        me = partners()[0]
        for h, cols in wave_heads(size, wave):
            rate = rate_of(rates_ref, size, me, h)
            total = None
            for k in range(GROUP):
                term = decay(steps[k], rate) * ins[k][cols, :]
                total = term if total is None else total + term
            out[cols, :] = total
        gains = ins[0][size.state :, :]
        for k in range(1, GROUP):
            gains = gains + ins[k][size.state :, :]
        put_rows(out, size.state, with_marks(size, end, end, gains))

    return call(
        body, "total", (rates, *parts), [size.payload],
        size.state * size.dim * 8, size.state * size.dim * 20,
    )[0]


def group_prefixes(size, backward, wave, rates, parts, entering, riders=(), collect=()):
    mark_row = size.state + (1 if backward else 0)

    def body(rates_ref, *refs):
        ins, enter = refs[:GROUP], refs[GROUP]
        rides, outs = refs[GROUP + 1 : GROUP + 1 + len(riders)], refs[GROUP + 1 + len(riders) :]
        if collect:
            put_rows(outs[-1], 0, outs[0][size.state :, :] + enter[size.state :, :])
            outs = outs[1:-1]
        gains = jnp.zeros((size.info, size.dim), f32)
        for ride in rides:
            gains = gains + ride[: size.info, :]
        place = places(backward)
        me = partners()[0]
        marks = [ref[mark_row : mark_row + 1, :] for ref in ins]
        block, members = lax.axis_index("seq"), lax.axis_size("seq")
        first = block >= members - GROUP if backward else block < GROUP
        outer = jnp.where(first, FAR if backward else 0.0, enter[size.state : size.state + 1, :])
        steps = []
        for to in range(GROUP):
            now = outer
            for k in range(GROUP):
                if backward:
                    now = jnp.where(place[k] < place[to], jnp.minimum(now, marks[k]), now)
                else:
                    now = jnp.where(place[k] < place[to], jnp.maximum(now, marks[k]), now)
            put_rows(outs[to], size.state, with_marks(size, now, now, gains))
            far = (place[to] * size.rows).astype(f32)
            steps.append([steps_if(jnp.logical_and(outer == now, jnp.logical_not(first)), far)])
            for k in range(GROUP):
                gap = place[to] - 1 - place[k]
                live = jnp.logical_and(marks[k] == now, gap >= 0)
                steps[to].append(steps_if(live, (gap * size.rows).astype(f32)))
        for h, cols in wave_heads(size, wave):
            rate = rate_of(rates_ref, size, me, h)
            for to in range(GROUP):
                total = decay(steps[to][0], rate) * enter[cols, :]
                for k in range(GROUP):
                    if k != to:
                        total += decay(steps[to][1 + k], rate) * ins[k][cols, :]
                outs[to][cols, :] = total

    return call(
        body, "prefixes", (rates, *parts, entering, *riders, *collect),
        [size.payload] * GROUP + [size.rows_of_gain] * len(collect),
        size.state * size.dim * 40, size.state * size.dim * 36,
    )


def whole_attended(size, mark, rates, queries, out_grad, gain, near, entering):
    def body(mark_ref, rates_ref, query_ref, grad_ref, gain_ref, near_ref, *refs):
        states, (out_ref, sums_ref) = refs[:-2], refs[-2:]
        group = partners()
        mark = mark_ref[...]
        behind = steps_if(mark == states[0][size.state : size.state + 1, :], position(size) + 1.0)
        square = jnp.zeros((size.rows, size.dim), f32)
        cross = jnp.zeros((size.rows, size.dim), f32)
        for i, (c, wave) in enumerate(all_pieces(size)):
            for h, cols in wave_heads(size, wave):
                here = columns(size, group[c], h)
                rate = rate_of(rates_ref, size, group[c], h)
                weight = decay(behind, rate)
                query = query_ref[:, here]
                high, low = halves(states[i][cols, :])
                inter = dot(jnp.concatenate([query, query], 1), jnp.concatenate([high, low], 0))
                out = near_ref[:, here] + weight * inter
                out_ref[:, here] = out
                square += out * out
                cross += grad_ref[:, here].astype(f32) * gain_ref[:, here] * out
        square = jnp.sum(square.T, axis=0, keepdims=True)
        cross = jnp.sum(cross.T, axis=0, keepdims=True)
        index = lax.broadcasted_iota(jnp.int32, (8, size.rows), 0)
        sums_ref[...] = jnp.where(index == 0, square, jnp.where(index == 1, cross, 0.0))

    return call(
        body, "attended", (mark, rates, queries, out_grad, gain, near, *entering),
        [size.block, jax.ShapeDtypeStruct((8, size.rows), f32)],
        size.heads * 4 * size.rows * size.dim * size.dim, size.features * size.rows * 16,
    )


def output_grad_states(size, pieces, norm, mark, rates, queries, out_grad, gain, sums, attended):
    n = len(pieces)

    def body(mark_ref, rates_ref, query_ref, grad_ref, gain_ref, sums_ref, att_ref, *outs):
        group = partners()
        mark = mark_ref[...]
        last, first = mark[size.rows - 1 :, :], mark[:1, :]
        wide = (size.dim, size.rows)
        square = jnp.broadcast_to(sums_ref[0:1, :], wide).T
        cross = jnp.broadcast_to(sums_ref[1:2, :], wide).T
        inv = lax.rsqrt(square / norm + 1e-06)
        pull = inv * inv * inv * cross / norm
        gone = steps_if(mark == first, position(size))
        for c, (chunk, wave) in enumerate(pieces):
            back_ref, state_ref = outs[2 * c : 2 * c + 2]
            gains = []
            for h in range(size.per):
                if wave > 0 and h // size.each != wave:
                    continue
                here, cols = columns(size, group[chunk], h), wave_columns(size, h)
                grad = grad_ref[:, here].astype(f32) * inv
                att = att_ref[:, here]
                if wave == 0:
                    gains.append(jnp.sum(grad * att, axis=0, keepdims=True))
                if h // size.each == wave:
                    weight = decay(gone, rate_of(rates_ref, size, group[chunk], h))
                    back = gain_ref[:, here] * grad - att * pull
                    back_ref[:, cols] = back
                    high, low = halves(back * weight)
                    state_ref[cols, :] = token_product(query_ref[:, here], high, low)
            put_rows(state_ref, size.state, info_rows(size, last, first, gains))

    part = jax.ShapeDtypeStruct((size.rows, size.state), f32)
    outs = call(
        body, "back", (mark, rates, queries, out_grad, gain, sums, attended),
        [part, size.payload] * n,
        n * size.each * 4 * size.rows * size.dim * size.dim, n * size.state * size.rows * 16,
    )
    return outs[0::2], outs[1::2]


def local_gradients(size, mark, rates, queries, key_rows, value_rows, back, entering):
    def body(mark_ref, rates_ref, query_ref, key_ref, value_ref, *refs):
        n = GROUP * size.waves
        backs, states = refs[:n], refs[n : 2 * n]
        out_hbm, local_key, local_value, done, sems = refs[2 * n :]
        group = partners()
        mark = mark_ref[...]
        gap, turned_gap = pair_steps(mark, size), pair_steps(mark, size, 0)
        behind = steps_if(mark == states[0][size.state : size.state + 1, :], position(size) + 1.0)
        copies = []
        for c in range(GROUP):
            for h in range(size.per):
                here = columns(size, group[c], h)
                piece = c + GROUP * (h // size.each)
                cols = slice(h % size.each * size.dim, (h % size.each + 1) * size.dim)
                rate = rate_of(rates_ref, size, group[c], h)
                rows_rate = square_rate(rate, size)
                weight, turned_weight = decay(gap, rows_rate), decay(turned_gap, rows_rate)
                query, key, value = query_ref[:, here], key_ref[:, here], value_ref[:, here]
                high, low = halves(backs[piece][:, cols])
                both, values = jnp.concatenate([high, low], 1), jnp.concatenate([value, value], 1)
                grads_high, grads_low = halves(dot(both, values, 1, 1) * weight)
                part = dot(
                    jnp.concatenate([grads_high, grads_low], 1), jnp.concatenate([key, key], 0)
                )
                state_high, state_low = halves(states[piece][cols, :])
                inter = dot(
                    jnp.concatenate([high, high, low], 1),
                    jnp.concatenate([state_high, state_low, state_high], 1),
                    1, 1,
                )
                done[c, :, h * size.dim : (h + 1) * size.dim] = (
                    part + decay(behind, rate) * inter
                ).astype(bf16)
                grads_high, grads_low = halves(dot(values, both, 1, 1) * turned_weight)
                local_key[:, here] = dot(
                    jnp.concatenate([grads_high, grads_low], 1),
                    jnp.concatenate([query, query], 0),
                )
                score_high, score_low = halves(dot(key, query, 1, 1) * turned_weight)
                local_value[:, here] = dot(
                    jnp.concatenate([score_high, score_high, score_low], 1),
                    jnp.concatenate([high, low, high], 0),
                )
            copies.append(
                pltpu.make_async_copy(
                    done.at[c], out_hbm.at[:, columns(size, group[c])], sems.at[c]
                )
            )
            copies[c].start()
        for copy in copies:
            copy.wait()

    return call(
        body, "gradients", (mark, rates, queries, key_rows, value_rows, *back, *entering),
        [jax.ShapeDtypeStruct((size.rows, size.features), bf16), size.block, size.block],
        size.heads * 26 * size.rows * size.dim * size.dim, size.features * size.rows * 24,
        [pltpu.VMEM((GROUP, size.rows, size.wide), bf16), pltpu.SemaphoreType.DMA((GROUP,))],
        None, [HBM, VMEM, VMEM],
    )


def final_gradients(size, mark, rates, key_rows, value_rows, local_key, local_value, entering):
    def body(mark_ref, rates_ref, key_ref, value_ref, local_key_ref, local_value_ref, *refs):
        n = GROUP * size.waves
        states, (keys_hbm, values_hbm, gain_hbm) = refs[:n], refs[n : n + 3]
        keys, values, gains, sems = refs[n + 3 :]
        group = partners()
        mark = mark_ref[...]
        left = steps_if(mark == states[0][size.state : size.state + 1, :], size.rows - position(size))
        for c in range(GROUP):
            for h in range(size.per):
                at = size.state + MARKS + h
                gains[:, columns(size, group[c], h)] = states[n - GROUP + c][at : at + 1, :]
        copies = [pltpu.make_async_copy(gains, gain_hbm, sems.at[2, 0])]
        copies[0].start()
        for c in range(GROUP):
            for h in range(size.per):
                here = columns(size, group[c], h)
                piece = c + GROUP * (h // size.each)
                at = slice(h % size.each * size.dim, (h % size.each + 1) * size.dim)
                cols = slice(h * size.dim, (h + 1) * size.dim)
                rate = rate_of(rates_ref, size, group[c], h)
                weight = decay(left, rate)
                key, value = key_ref[:, here], value_ref[:, here]
                high, low = halves(states[piece][at, :])
                from_values = dot(
                    jnp.concatenate([value, value], 1), jnp.concatenate([high, low], 1), 1, 1
                )
                from_keys = dot(jnp.concatenate([key, key], 1), jnp.concatenate([high, low], 0))
                keys[c, :, cols] = (local_key_ref[:, here] + weight * from_values).astype(bf16)
                values[c, :, cols] = (local_value_ref[:, here] + weight * from_keys).astype(bf16)
            here = columns(size, group[c])
            for copy in (
                pltpu.make_async_copy(keys.at[c], keys_hbm.at[:, here], sems.at[0, c]),
                pltpu.make_async_copy(values.at[c], values_hbm.at[:, here], sems.at[1, c]),
            ):
                copy.start()
                copies.append(copy)
        for copy in copies:
            copy.wait()

    shape = jax.ShapeDtypeStruct((size.rows, size.features), bf16)
    held = pltpu.VMEM((GROUP, size.rows, size.wide), bf16)
    return call(
        body, "final", (mark, rates, key_rows, value_rows, local_key, local_value, *entering),
        [shape, shape, jax.ShapeDtypeStruct((1, size.features), f32)],
        size.heads * 8 * size.rows * size.dim * size.dim, size.features * size.rows * 24,
        [held, held, pltpu.VMEM((1, size.features), f32), pltpu.SemaphoreType.DMA((3, GROUP))],
        None, [HBM] * 3,
    )


def swap(array, distance):
    members = lax.axis_size("seq")
    return lax.ppermute(array, "seq", [(i, i ^ distance) for i in range(members)])


def exchange(payloads):
    return [payloads[0]] + [swap(payloads[k], k) for k in range(1, GROUP)]


def shifted(array, by):
    members = lax.axis_size("seq")
    pairs = [(i, i + by) for i in range(members) if 0 <= i + by < members]
    return lax.ppermute(array, "seq", pairs)


def cyclic(array, by):
    members = lax.axis_size("seq")
    return lax.ppermute(array, "seq", [(i, (i + by) % members) for i in range(members)])


def reach_of_documents(size):
    longest = lax.axis_size("seq") * size.rows // 4
    return max(longest - 2, 0) // (GROUP * size.rows) + 1


def from_other_groups(size, backward, wave, decay_span, total):
    needed = reach_of_documents(size)
    way = -GROUP if backward else GROUP
    if needed == 1:
        return cyclic(total, way)
    result = shifted(total, way)
    reach = 1
    start = partners()[0] * size.per + wave * size.each
    mine = lax.dynamic_slice(decay_span, (start,), (size.each,))
    while reach < needed:
        incoming = shifted(result, way * reach)
        passes = incoming[size.state, 0] == result[size.state, 0]
        factor = jnp.where(passes, jnp.exp(-(reach * GROUP * size.rows) / mine), 0.0)
        factor = jnp.repeat(factor, size.dim)[:, None]
        result = result.at[: size.state].add(factor * incoming[: size.state])
        reach *= 2
    return result


def local(queries, key_rows, value_rows, segment_ids, decay_span, norm_gain, out_grad):
    size = Sizes(queries, decay_span)
    norm = size.features * lax.axis_size("head")
    members = lax.axis_size("seq")
    seg = segment_ids.reshape(1, size.rows)
    gain = norm_gain.reshape(1, size.features)
    waves = range(size.waves)
    sent = [[(chunk, wave) for chunk in (3, 1, 2)] for wave in waves]
    kept = [(0, wave) for wave in waves]
    every = all_pieces(size)

    outs, mark, rates = first_states(size, sent[0], seg, decay_span, key_rows, value_rows)
    common = (mark, rates)
    states = dict(zip(sent[0], outs))
    later = sum(sent[1:], []) + kept
    states |= zip(later, more_states(size, later, *common, key_rows, value_rows))
    near = nearby_attended(size, *common, queries, key_rows, value_rows)
    parts = {w: exchange({k: states[k, w] for k in range(GROUP)}) for w in waves}
    totals = {w: group_total(size, False, w, rates, parts[w]) for w in waves}
    outer = {w: from_other_groups(size, False, w, decay_span, totals[w]) for w in waves}
    entering = {}
    for w in waves:
        entering[w] = exchange(group_prefixes(size, False, w, rates, parts[w], outer[w]))

    entering = sum([entering[w] for w in waves], [])
    attended, sums = whole_attended(size, *common, queries, out_grad, gain, near, entering)
    sums = lax.psum(sums, "head")
    back, states = {}, {}
    for pieces in [*sent, kept]:
        backs, payloads = output_grad_states(
            size, pieces, norm, *common, queries, out_grad, gain, sums, attended
        )
        back |= zip(pieces, backs)
        states |= zip(pieces, payloads)

    parts = {w: exchange({k: states[k, w] for k in range(GROUP)}) for w in waves}
    totals = {w: group_total(size, True, w, rates, parts[w]) for w in waves}
    outer = {w: from_other_groups(size, True, w, decay_span, totals[w]) for w in waves}
    rides = size.waves > 1 and reach_of_documents(size) == 1 and members > GROUP
    gains, summed, leaving = [totals[0][size.state :, :]], 1, []
    for w in waves:
        if w < size.waves - 1:
            riders, collect = (), ((totals[0],) if rides and w == 0 else ())
        else:
            while summed * GROUP < members:
                gains = [sum(gains), cyclic(sum(gains), -summed * GROUP)]
                summed *= 2
            riders, collect = gains, ()
        outs = group_prefixes(size, True, w, rates, parts[w], outer[w], riders, collect)
        if collect:
            gains, summed = outs[GROUP:], 2
        leaving += exchange(outs[:GROUP])

    query_grad, local_key, local_value = local_gradients(
        size, *common, queries, key_rows, value_rows, [back[piece] for piece in every], entering
    )
    key_grad, value_grad, gain_grad = final_gradients(
        size, *common, key_rows, value_rows, local_key, local_value, leaving
    )
    return query_grad, key_grad, value_grad, gain_grad.reshape(size.features)


def solution(mesh):
    rows = P("seq", "head")
    in_specs = (rows, rows, rows, P("seq"), P("head"), P("head"), rows)
    return jax.shard_map(
        local, mesh=mesh, in_specs=in_specs, out_specs=(rows, rows, rows, P("head")), check_vma=False
    )
```

```python
import jax
import jax.numpy as jnp
from jax import lax
from jax.experimental import pallas as pl
from jax.experimental.pallas import tpu as pltpu
from jax.sharding import PartitionSpec as P

GROUP = 4
MARKS = 2
FAR = 1e9
NEVER = 1e30
f32 = jnp.float32
bf16 = jnp.bfloat16
HBM = pl.BlockSpec(memory_space=pltpu.HBM)
VMEM = pl.BlockSpec(memory_space=pltpu.VMEM)


def dot(a, b, over_a=1, over_b=0):
    return lax.dot_general(a, b, (((over_a,), (over_b,)), ((), ())), preferred_element_type=f32)


def halves(x):
    high = x.astype(bf16)
    return high, (x - high.astype(f32)).astype(bf16)


def decay(steps, rate):
    return jnp.exp(steps * rate)


class Sizes:
    def __init__(self, queries, decay_span):
        self.rows = queries.shape[0]
        self.heads = decay_span.shape[0]
        self.features = queries.shape[1]
        self.dim = self.features // self.heads
        self.per = self.heads // GROUP
        self.wide = self.per * self.dim
        self.info = -(-(MARKS + self.per) // 8) * 8
        self.waves = 2 if self.per % 2 == 0 else 1
        self.each = self.per // self.waves
        self.state = self.each * self.dim
        self.payload = jax.ShapeDtypeStruct((self.state + self.info, self.dim), f32)
        self.block = jax.ShapeDtypeStruct((self.rows, self.features), f32)
        self.rows_of_gain = jax.ShapeDtypeStruct((self.info, self.dim), f32)


def position(size):
    return lax.broadcasted_iota(jnp.int32, (size.rows, size.dim), 0).astype(f32)


def steps_if(live, steps):
    return jnp.where(live, steps, NEVER)


def pair_steps(mark, size, earlier=1):
    shape = (size.rows, size.rows)
    here = mark if size.rows == size.dim else jnp.broadcast_to(mark[:, :1], shape)
    later = lax.broadcasted_iota(jnp.int32, shape, 1 - earlier)
    gap = later - lax.broadcasted_iota(jnp.int32, shape, earlier)
    return steps_if(jnp.logical_and(gap >= 0, here == here.T), gap.astype(f32))


def token_product(a, high, low):
    turned = a.T
    return dot(jnp.concatenate([turned, turned], 1), jnp.concatenate([high, low], 0))


def info_rows(size, last, first, more=()):
    index = lax.broadcasted_iota(jnp.int32, (size.info, size.dim), 0)
    rows = jnp.zeros((size.info, size.dim), f32)
    for i, row in enumerate((last, first, *more)):
        rows = jnp.where(index == i, row, rows)
    return rows


def with_marks(size, last, first, rows):
    index = lax.broadcasted_iota(jnp.int32, (size.info, size.dim), 0)
    return jnp.where(index == 0, last, jnp.where(index == 1, first, rows))


def partners():
    me = jnp.bitwise_and(lax.axis_index("seq"), GROUP - 1)
    return [jnp.bitwise_xor(me, k) for k in range(GROUP)]


def places(backward):
    return [GROUP - 1 - p for p in partners()] if backward else partners()


def columns(size, group, h=None):
    if h is None:
        return pl.ds(pl.multiple_of(group * size.wide, size.wide), size.wide)
    return pl.ds(pl.multiple_of(group * size.wide + h * size.dim, size.dim), size.dim)


def wave_heads(size, wave):
    return [(wave * size.each + i, slice(i * size.dim, (i + 1) * size.dim)) for i in range(size.each)]


def wave_columns(size, h):
    return slice(h % size.each * size.dim, (h % size.each + 1) * size.dim)


def all_pieces(size):
    return [(chunk, wave) for wave in range(size.waves) for chunk in range(GROUP)]


def last_order(size):
    usual = list(range(GROUP * (size.waves - 1)))
    return usual + [GROUP * (size.waves - 1) + k for k in reversed(range(GROUP))]


def rate_of(rates_ref, size, group, h):
    return rates_ref[pl.ds(group * size.per + h, 1), :]


def square_rate(rate, size):
    return rate[:, :1] if size.rows != size.dim else rate


def call(body, name, inputs, outputs, flops, moved, scratch=(), in_specs=None, out_specs=None, vmem=16, aliases=None):
    return pl.pallas_call(
        body,
        out_shape=outputs,
        in_specs=in_specs if in_specs is not None else [VMEM] * len(inputs),
        out_specs=out_specs if out_specs is not None else [VMEM] * len(outputs),
        scratch_shapes=list(scratch),
        input_output_aliases=aliases or {},
        compiler_params=pltpu.CompilerParams(vmem_limit_bytes=vmem * 1024 * 1024),
        cost_estimate=pl.CostEstimate(flops=flops, bytes_accessed=moved, transcendentals=0),
        name=name,
    )(*inputs)


def state_payloads(size, pieces, mark, rates_ref, group, outs, key_of, value_of):
    last, first = mark[size.rows - 1 :, :], mark[:1, :]
    ahead = steps_if(mark == last, (size.rows - 1.0) - position(size))
    for c, (chunk, wave) in enumerate(pieces):
        for h, cols in wave_heads(size, wave):
            weight = decay(ahead, rate_of(rates_ref, size, group[chunk], h))
            high, low = halves(value_of(c, h, cols).astype(f32) * weight)
            outs[c][cols, :] = token_product(key_of(c, h, cols), high, low)
        outs[c][size.state :, :] = info_rows(size, last, first)


def first_states(size, pieces, seg, decay_span, key_rows, value_rows):
    n = len(pieces)
    wide = size.each * size.dim

    def body(seg_hbm, span_hbm, key_hbm, value_hbm, *refs):
        outs, mark_ref, rates_ref = refs[:n], refs[n], refs[n + 1]
        seg_row, span_row, keys, values, sems = refs[n + 2 :]
        group = partners()
        small = (
            pltpu.make_async_copy(seg_hbm, seg_row, sems.at[2, 0]),
            pltpu.make_async_copy(span_hbm, span_row, sems.at[2, 1]),
        )
        copies = []
        for copy in small:
            copy.start()
        for c, (chunk, wave) in enumerate(pieces):
            here = pl.ds(pl.multiple_of(group[chunk] * size.wide + wave * wide, wide), wide)
            copies += [
                pltpu.make_async_copy(key_hbm.at[:, here], keys.at[c], sems.at[0, c]),
                pltpu.make_async_copy(value_hbm.at[:, here], values.at[c], sems.at[1, c]),
            ]
        for copy in copies:
            copy.start()
        for copy in small:
            copy.wait()
        mark = jnp.broadcast_to(seg_row[...].astype(f32) + 1.0, (size.dim, size.rows)).T
        mark_ref[...] = mark
        rates_ref[...] = jnp.broadcast_to(-1.0 / span_row[...], (size.dim, size.heads)).T
        for copy in copies:
            copy.wait()
        state_payloads(
            size, pieces, mark, rates_ref, group, outs,
            lambda c, h, cols: keys[c, :, cols], lambda c, h, cols: values[c, :, cols],
        )

    held = (n, size.rows, wide)
    outs = call(
        body, "states", (seg, decay_span.reshape(1, size.heads), key_rows, value_rows),
        [size.payload] * n + [
            jax.ShapeDtypeStruct((size.rows, size.dim), f32),
            jax.ShapeDtypeStruct((size.heads, size.dim), f32),
        ],
        n * size.each * 4 * size.rows * size.dim * size.dim, n * wide * size.rows * 8,
        [
            pltpu.VMEM((1, size.rows), jnp.int32),
            pltpu.VMEM((1, size.heads), f32),
            pltpu.VMEM(held, bf16),
            pltpu.VMEM(held, bf16),
            pltpu.SemaphoreType.DMA((3, max(n, 2))),
        ],
        [HBM] * 4, vmem=60,
    )
    return outs[:n], outs[n], outs[n + 1]


def more_states(size, pieces, mark, rates, key_rows, value_rows):
    def body(mark_ref, rates_ref, key_ref, value_ref, *outs):
        group = partners()

        def head(ref):
            return lambda c, h, cols: ref[:, columns(size, group[pieces[c][0]], h)]

        state_payloads(
            size, pieces, mark_ref[...], rates_ref, group, outs, head(key_ref), head(value_ref)
        )

    n = len(pieces)
    return call(
        body, "states", (mark, rates, key_rows, value_rows), [size.payload] * n,
        n * size.each * 4 * size.rows * size.dim * size.dim, n * size.state * size.rows * 8,
    )


def nearby_attended(size, mark, rates, queries, key_rows, value_rows):
    def body(mark_ref, rates_ref, query_ref, key_ref, value_ref, out_ref):
        gap = pair_steps(mark_ref[...], size)
        for h in range(size.heads):
            cols = slice(h * size.dim, (h + 1) * size.dim)
            rate = square_rate(rates_ref[h : h + 1, :], size)
            weight = decay(gap, rate)
            query, key, value = query_ref[:, cols], key_ref[:, cols], value_ref[:, cols]
            high, low = halves(dot(query, key, 1, 1) * weight)
            out_ref[:, cols] = dot(
                jnp.concatenate([high, low], 1), jnp.concatenate([value, value], 0)
            )

    return call(
        body, "nearby", (mark, rates, queries, key_rows, value_rows), [size.block],
        size.heads * 6 * size.rows * size.dim * size.dim, size.features * size.rows * 10,
    )[0]


def put_rows(ref, at, rows):
    ref[at : at + rows.shape[0], :] = rows


def group_total(size, backward, wave, rates, parts, riders=(), count=False):
    mark_row = size.state + (1 if backward else 0)

    def body(rates_ref, *refs):
        ins, rides = refs[:GROUP], refs[GROUP : GROUP + len(riders)]
        outs = refs[GROUP + len(riders) :]
        place = places(backward)
        marks = [ref[mark_row : mark_row + 1, :] for ref in ins]
        end = marks[0]
        for mark in marks[1:]:
            end = jnp.minimum(end, mark) if backward else jnp.maximum(end, mark)
        steps = [
            steps_if(marks[k] == end, ((GROUP - 1 - place[k]) * size.rows).astype(f32))
            for k in range(GROUP)
        ]
        me = partners()[0]
        for h, cols in wave_heads(size, wave):
            rate = rate_of(rates_ref, size, me, h)
            total = None
            for k in range(GROUP):
                term = decay(steps[k], rate) * ins[k][cols, :]
                total = term if total is None else total + term
            outs[0][cols, :] = total
        rows = [ride[...] for ride in rides] or [ref[size.state :, :] for ref in ins]
        put_rows(outs[0], size.state, with_marks(size, end, end, sum(rows)))
        if count:
            outs[1][...] = sum(rows)

    return call(
        body, "total", (rates, *parts, *riders), [size.payload] + [size.rows_of_gain] * count,
        size.state * size.dim * 8, size.state * size.dim * 20,
    )


def group_prefixes(size, backward, wave, rates, parts, entering, riders=(), own=()):
    mark_row = size.state + (1 if backward else 0)

    def body(rates_ref, *refs):
        ins, enter, refs = refs[:GROUP], refs[GROUP], refs[GROUP + 1 :]
        rows = [ref[...] for ref in refs[: len(riders)]]
        rows += [ref[size.state :, :] for ref in refs[len(riders) : len(riders) + len(own)]]
        outs = refs[len(riders) + len(own) :]
        gains = sum(rows) + enter[size.state :, :] if own else sum(rows)
        if not rows:
            gains = jnp.zeros((size.info, size.dim), f32)
        place = places(backward)
        me = partners()[0]
        marks = [ref[mark_row : mark_row + 1, :] for ref in ins]
        block, members = lax.axis_index("seq"), lax.axis_size("seq")
        first = block >= members - GROUP if backward else block < GROUP
        outer = jnp.where(first, FAR if backward else 0.0, enter[size.state : size.state + 1, :])
        steps = []
        for to in range(GROUP):
            now = outer
            for k in range(GROUP):
                if backward:
                    now = jnp.where(place[k] < place[to], jnp.minimum(now, marks[k]), now)
                else:
                    now = jnp.where(place[k] < place[to], jnp.maximum(now, marks[k]), now)
            put_rows(outs[to], size.state, with_marks(size, now, now, gains))
            far = (place[to] * size.rows).astype(f32)
            steps.append([steps_if(jnp.logical_and(outer == now, jnp.logical_not(first)), far)])
            for k in range(GROUP):
                gap = place[to] - 1 - place[k]
                live = jnp.logical_and(marks[k] == now, gap >= 0)
                steps[to].append(steps_if(live, (gap * size.rows).astype(f32)))
        for h, cols in wave_heads(size, wave):
            rate = rate_of(rates_ref, size, me, h)
            for to in range(GROUP):
                total = decay(steps[to][0], rate) * enter[cols, :]
                for k in range(GROUP):
                    if k != to:
                        total += decay(steps[to][1 + k], rate) * ins[k][cols, :]
                outs[to][cols, :] = total

    return call(
        body, "prefixes", (rates, *parts, entering, *riders, *own), [size.payload] * GROUP,
        size.state * size.dim * 40, size.state * size.dim * 36,
    )


def whole_attended(size, wave, mark, rates, queries, out_grad, gain, near, entering, before=()):
    last = wave == size.waves - 1

    def body(mark_ref, rates_ref, query_ref, grad_ref, gain_ref, near_ref, *refs):
        states, earlier, outs = refs[:GROUP], refs[GROUP : GROUP + len(before)], refs[GROUP + len(before) :]
        group = partners()
        mark = mark_ref[...]
        behind = steps_if(mark == states[0][size.state : size.state + 1, :], position(size) + 1.0)
        square = earlier[1][...] if before else jnp.zeros((size.rows, size.dim), f32)
        cross = earlier[2][...] if before else jnp.zeros((size.rows, size.dim), f32)
        for c in range(GROUP):
            for h, cols in wave_heads(size, wave):
                here = columns(size, group[c], h)
                weight = decay(behind, rate_of(rates_ref, size, group[c], h))
                query = query_ref[:, here]
                high, low = halves(states[c][cols, :])
                inter = dot(jnp.concatenate([query, query], 1), jnp.concatenate([high, low], 0))
                out = near_ref[:, here] + weight * inter
                outs[0][:, here] = out
                square += out * out
                cross += grad_ref[:, here].astype(f32) * gain_ref[:, here] * out
        if last:
            square = jnp.sum(square.T, axis=0, keepdims=True)
            cross = jnp.sum(cross.T, axis=0, keepdims=True)
            index = lax.broadcasted_iota(jnp.int32, (8, size.rows), 0)
            outs[1][...] = jnp.where(index == 0, square, jnp.where(index == 1, cross, 0.0))
        else:
            outs[1][...], outs[2][...] = square, cross

    if last:
        sums = [jax.ShapeDtypeStruct((8, size.rows), f32)]
    else:
        sums = [jax.ShapeDtypeStruct((size.rows, size.dim), f32)] * 2
    inputs = (mark, rates, queries, out_grad, gain, near, *entering, *before)
    return call(
        body, "attended", inputs, [size.block] + sums,
        GROUP * size.each * 4 * size.rows * size.dim * size.dim, GROUP * size.state * size.rows * 16,
        aliases={len(inputs) - len(before): 0} if before else {},
    )


def output_grad_states(size, pieces, norm, mark, rates, queries, out_grad, gain, sums, attended):
    n = len(pieces)

    def body(mark_ref, rates_ref, query_ref, grad_ref, gain_ref, sums_ref, att_ref, *outs):
        group = partners()
        mark = mark_ref[...]
        last, first = mark[size.rows - 1 :, :], mark[:1, :]
        wide = (size.dim, size.rows)
        square = jnp.broadcast_to(sums_ref[0:1, :], wide).T
        cross = jnp.broadcast_to(sums_ref[1:2, :], wide).T
        inv = lax.rsqrt(square / norm + 1e-06)
        pull = inv * inv * inv * cross / norm
        gone = steps_if(mark == first, position(size))
        for c, (chunk, wave) in enumerate(pieces):
            back_ref, state_ref = outs[2 * c : 2 * c + 2]
            gains = []
            for h in range(size.per):
                if wave > 0 and h // size.each != wave:
                    continue
                here, cols = columns(size, group[chunk], h), wave_columns(size, h)
                grad = grad_ref[:, here].astype(f32) * inv
                att = att_ref[:, here]
                if wave == 0:
                    gains.append(jnp.sum(grad * att, axis=0, keepdims=True))
                if h // size.each == wave:
                    weight = decay(gone, rate_of(rates_ref, size, group[chunk], h))
                    back = gain_ref[:, here] * grad - att * pull
                    back_ref[:, cols] = back
                    high, low = halves(back * weight)
                    state_ref[cols, :] = token_product(query_ref[:, here], high, low)
            put_rows(state_ref, size.state, info_rows(size, last, first, gains))

    part = jax.ShapeDtypeStruct((size.rows, size.state), f32)
    outs = call(
        body, "back", (mark, rates, queries, out_grad, gain, sums, attended),
        [part, size.payload] * n,
        n * size.each * 4 * size.rows * size.dim * size.dim, n * size.state * size.rows * 16,
    )
    return outs[0::2], outs[1::2]


def local_gradients(size, mark, rates, queries, key_rows, value_rows, back, entering):
    pieces = all_pieces(size)
    n = len(pieces)

    def body(mark_ref, rates_ref, query_ref, key_ref, value_ref, *refs):
        backs, states = refs[:n], refs[n : 2 * n]
        out_hbm, local_key, local_value, done, sems = refs[2 * n :]
        group = partners()
        mark = mark_ref[...]
        gap, turned_gap = pair_steps(mark, size), pair_steps(mark, size, 0)
        behind = steps_if(mark == states[0][size.state : size.state + 1, :], position(size) + 1.0)
        copies = []
        for c in range(GROUP):
            for h in range(size.per):
                here = columns(size, group[c], h)
                piece = pieces.index((c, h // size.each))
                near = slice(c * size.wide + h * size.dim, c * size.wide + (h + 1) * size.dim)
                cols = slice(h % size.each * size.dim, (h % size.each + 1) * size.dim)
                rate = rate_of(rates_ref, size, group[c], h)
                rows_rate = square_rate(rate, size)
                weight, turned_weight = decay(gap, rows_rate), decay(turned_gap, rows_rate)
                query, key, value = query_ref[:, here], key_ref[:, here], value_ref[:, here]
                high, low = halves(backs[piece][:, cols])
                both, values = jnp.concatenate([high, low], 1), jnp.concatenate([value, value], 1)
                grads_high, grads_low = halves(dot(both, values, 1, 1) * weight)
                part = dot(
                    jnp.concatenate([grads_high, grads_low], 1), jnp.concatenate([key, key], 0)
                )
                state_high, state_low = halves(states[piece][cols, :])
                inter = dot(
                    jnp.concatenate([high, high, low], 1),
                    jnp.concatenate([state_high, state_low, state_high], 1),
                    1, 1,
                )
                done[c, :, h * size.dim : (h + 1) * size.dim] = (
                    part + decay(behind, rate) * inter
                ).astype(bf16)
                grads_high, grads_low = halves(dot(values, both, 1, 1) * turned_weight)
                local_key[:, near] = dot(
                    jnp.concatenate([grads_high, grads_low], 1),
                    jnp.concatenate([query, query], 0),
                )
                score_high, score_low = halves(dot(key, query, 1, 1) * turned_weight)
                local_value[:, near] = dot(
                    jnp.concatenate([score_high, score_high, score_low], 1),
                    jnp.concatenate([high, low, high], 0),
                )
            copies.append(
                pltpu.make_async_copy(
                    done.at[c], out_hbm.at[:, columns(size, group[c])], sems.at[c]
                )
            )
            copies[c].start()
        for copy in copies:
            copy.wait()

    return call(
        body, "gradients", (mark, rates, queries, key_rows, value_rows, *back, *entering),
        [jax.ShapeDtypeStruct((size.rows, size.features), bf16), size.block, size.block],
        size.heads * 26 * size.rows * size.dim * size.dim, size.features * size.rows * 24,
        [pltpu.VMEM((GROUP, size.rows, size.wide), bf16), pltpu.SemaphoreType.DMA((GROUP,))],
        None, [HBM, VMEM, VMEM],
    )


def final_gradients(size, mark, rates, key_rows, value_rows, local_key, local_value, entering):
    def body(mark_ref, rates_ref, key_ref, value_ref, local_key_ref, local_value_ref, *refs):
        n = GROUP * size.waves
        states, (keys_hbm, values_hbm, gain_hbm) = refs[:n], refs[n : n + 3]
        states = [states[last_order(size).index(i)] for i in range(n)]
        keys, values, gains, sems = refs[n + 3 :]
        group = partners()
        mark = mark_ref[...]
        left = steps_if(mark == states[0][size.state : size.state + 1, :], size.rows - position(size))
        for c in range(GROUP):
            for h in range(size.per):
                at = size.state + MARKS + h
                gains[:, columns(size, group[c], h)] = states[n - GROUP + c][at : at + 1, :]
        copies = [pltpu.make_async_copy(gains, gain_hbm, sems.at[2, 0])]
        copies[0].start()
        for c in range(GROUP):
            for h in range(size.per):
                here = columns(size, group[c], h)
                piece = c + GROUP * (h // size.each)
                at = slice(h % size.each * size.dim, (h % size.each + 1) * size.dim)
                cols = slice(h * size.dim, (h + 1) * size.dim)
                rate = rate_of(rates_ref, size, group[c], h)
                weight = decay(left, rate)
                key, value = key_ref[:, here], value_ref[:, here]
                high, low = halves(states[piece][at, :])
                from_values = dot(
                    jnp.concatenate([value, value], 1), jnp.concatenate([high, low], 1), 1, 1
                )
                from_keys = dot(jnp.concatenate([key, key], 1), jnp.concatenate([high, low], 0))
                near = slice(c * size.wide + h * size.dim, c * size.wide + (h + 1) * size.dim)
                keys[c, :, cols] = (local_key_ref[:, near] + weight * from_values).astype(bf16)
                values[c, :, cols] = (local_value_ref[:, near] + weight * from_keys).astype(bf16)
            here = columns(size, group[c])
            for copy in (
                pltpu.make_async_copy(keys.at[c], keys_hbm.at[:, here], sems.at[0, c]),
                pltpu.make_async_copy(values.at[c], values_hbm.at[:, here], sems.at[1, c]),
            ):
                copy.start()
                copies.append(copy)
        for copy in copies:
            copy.wait()

    shape = jax.ShapeDtypeStruct((size.rows, size.features), bf16)
    held = pltpu.VMEM((GROUP, size.rows, size.wide), bf16)
    return call(
        body, "final",
        (
            mark, rates, key_rows, value_rows, local_key, local_value,
            *[entering[i] for i in last_order(size)],
        ),
        [shape, shape, jax.ShapeDtypeStruct((1, size.features), f32)],
        size.heads * 8 * size.rows * size.dim * size.dim, size.features * size.rows * 24,
        [held, held, pltpu.VMEM((1, size.features), f32), pltpu.SemaphoreType.DMA((3, GROUP))],
        None, [HBM] * 3,
    )


def swap(array, distance):
    members = lax.axis_size("seq")
    return lax.ppermute(array, "seq", [(i, i ^ distance) for i in range(members)])


def exchange(payloads):
    return [payloads[0]] + [swap(payloads[k], k) for k in range(1, GROUP)]


def shifted(array, by):
    members = lax.axis_size("seq")
    pairs = [(i, i + by) for i in range(members) if 0 <= i + by < members]
    return lax.ppermute(array, "seq", pairs)


def cyclic(array, by):
    members = lax.axis_size("seq")
    return lax.ppermute(array, "seq", [(i, (i + by) % members) for i in range(members)])


def reach_of_documents(size):
    longest = lax.axis_size("seq") * size.rows // 4
    return max(longest - 2, 0) // (GROUP * size.rows) + 1


def from_other_groups(size, backward, wave, decay_span, total):
    needed = reach_of_documents(size)
    way = -GROUP if backward else GROUP
    if needed == 1:
        return cyclic(total, way)
    result = shifted(total, way)
    reach = 1
    start = partners()[0] * size.per + wave * size.each
    mine = lax.dynamic_slice(decay_span, (start,), (size.each,))
    while reach < needed:
        incoming = shifted(result, way * reach)
        passes = incoming[size.state, 0] == result[size.state, 0]
        factor = jnp.where(passes, jnp.exp(-(reach * GROUP * size.rows) / mine), 0.0)
        factor = jnp.repeat(factor, size.dim)[:, None]
        result = result.at[: size.state].add(factor * incoming[: size.state])
        reach *= 2
    return result


def local(queries, key_rows, value_rows, segment_ids, decay_span, norm_gain, out_grad):
    size = Sizes(queries, decay_span)
    norm = size.features * lax.axis_size("head")
    members = lax.axis_size("seq")
    seg = segment_ids.reshape(1, size.rows)
    gain = norm_gain.reshape(1, size.features)
    waves = range(size.waves)
    sent = [[(chunk, wave) for chunk in (3, 1, 2)] for wave in waves]
    kept = [(0, wave) for wave in waves]
    every = all_pieces(size)

    outs, mark, rates = first_states(size, sent[0], seg, decay_span, key_rows, value_rows)
    common = (mark, rates)
    states = dict(zip(sent[0], outs))
    later = sum(sent[1:], []) + kept
    states |= zip(later, more_states(size, later, *common, key_rows, value_rows))
    near = nearby_attended(size, *common, queries, key_rows, value_rows)
    parts = {w: exchange({k: states[k, w] for k in range(GROUP)}) for w in waves}
    totals = {w: group_total(size, False, w, rates, parts[w])[0] for w in waves}
    outer = {w: from_other_groups(size, False, w, decay_span, totals[w]) for w in waves}
    entering = {}
    for w in waves:
        entering[w] = exchange(group_prefixes(size, False, w, rates, parts[w], outer[w]))

    entering = sum([entering[w] for w in waves], [])
    outs = ()
    for w in waves:
        states = entering[w * GROUP : (w + 1) * GROUP]
        outs = whole_attended(size, w, *common, queries, out_grad, gain, near, states, outs)
    attended, sums = outs
    sums = lax.psum(sums, "head")
    back, states = {}, {}
    for pieces in [*sent, kept]:
        backs, payloads = output_grad_states(
            size, pieces, norm, *common, queries, out_grad, gain, sums, attended
        )
        back |= zip(pieces, backs)
        states |= zip(pieces, payloads)

    parts = {w: exchange({k: states[k, w] for k in range(GROUP)}) for w in waves}
    back = [back[piece] for piece in every]
    totals, leaving, last = {}, [], size.waves - 1
    rides = size.waves > 1 and reach_of_documents(size) == 1 and members > GROUP
    totals[0], *gains = group_total(size, True, 0, rates, parts[0], (), True)
    apart = 2 if rides else 1
    while apart * GROUP < members:
        gains = [sum(gains), cyclic(sum(gains), -apart * GROUP)]
        apart *= 2
    for w in waves[1:]:
        riders = gains if rides and w == last else ()
        totals[w] = group_total(size, True, w, rates, parts[w], riders)[0]
    outer = {w: from_other_groups(size, True, w, decay_span, totals[w]) for w in waves}
    for w in waves:
        riders = gains if w == last and not rides else ()
        own = (totals[w],) if w == last and rides else ()
        leaving += exchange(
            group_prefixes(size, True, w, rates, parts[w], outer[w], riders, own)
        )

    query_grad, local_key, local_value = local_gradients(
        size, *common, queries, key_rows, value_rows, back, entering
    )
    key_grad, value_grad, gain_grad = final_gradients(
        size, *common, key_rows, value_rows, local_key, local_value, leaving
    )
    return query_grad, key_grad, value_grad, gain_grad.reshape(size.features)


def solution(mesh):
    rows = P("seq", "head")
    in_specs = (rows, rows, rows, P("seq"), P("head"), P("head"), rows)
    return jax.shard_map(
        local, mesh=mesh, in_specs=in_specs, out_specs=(rows, rows, rows, P("head")), check_vma=False
    )
```

```python
import jax
import jax.numpy as jnp
from jax import lax
from jax.experimental import pallas as pl
from jax.experimental.pallas import tpu as pltpu
from jax.sharding import PartitionSpec as P

GROUP = 4
MARKS = 2
FAR = 1e9
NEVER = 1e30
f32 = jnp.float32
bf16 = jnp.bfloat16
HBM = pl.BlockSpec(memory_space=pltpu.HBM)
VMEM = pl.BlockSpec(memory_space=pltpu.VMEM)


def dot(a, b, over_a=1, over_b=0):
    return lax.dot_general(a, b, (((over_a,), (over_b,)), ((), ())), preferred_element_type=f32)


def halves(x):
    high = x.astype(bf16)
    return high, (x - high.astype(f32)).astype(bf16)


def decay(steps, rate):
    return jnp.exp(steps * rate)


class Sizes:
    def __init__(self, queries, decay_span):
        self.rows = queries.shape[0]
        self.heads = decay_span.shape[0]
        self.features = queries.shape[1]
        self.dim = self.features // self.heads
        self.per = self.heads // GROUP
        self.wide = self.per * self.dim
        self.info = -(-(MARKS + self.per) // 8) * 8
        self.waves = 2 if self.per % 2 == 0 else 1
        self.each = self.per // self.waves
        self.state = self.each * self.dim
        self.payload = jax.ShapeDtypeStruct((self.state + self.info, self.dim), f32)
        self.block = jax.ShapeDtypeStruct((self.rows, self.features), f32)
        self.rows_of_gain = jax.ShapeDtypeStruct((self.info, self.dim), f32)


def position(size):
    return lax.broadcasted_iota(jnp.int32, (size.rows, size.dim), 0).astype(f32)


def steps_if(live, steps):
    return jnp.where(live, steps, NEVER)


def pair_steps(mark, size, earlier=1):
    shape = (size.rows, size.rows)
    here = mark if size.rows == size.dim else jnp.broadcast_to(mark[:, :1], shape)
    later = lax.broadcasted_iota(jnp.int32, shape, 1 - earlier)
    gap = later - lax.broadcasted_iota(jnp.int32, shape, earlier)
    return steps_if(jnp.logical_and(gap >= 0, here == here.T), gap.astype(f32))


def token_product(a, high, low):
    turned = a.T
    return dot(jnp.concatenate([turned, turned], 1), jnp.concatenate([high, low], 0))


def info_rows(size, last, first, more=()):
    index = lax.broadcasted_iota(jnp.int32, (size.info, size.dim), 0)
    rows = jnp.zeros((size.info, size.dim), f32)
    for i, row in enumerate((last, first, *more)):
        rows = jnp.where(index == i, row, rows)
    return rows


def with_marks(size, last, first, rows):
    index = lax.broadcasted_iota(jnp.int32, (size.info, size.dim), 0)
    return jnp.where(index == 0, last, jnp.where(index == 1, first, rows))


def partners():
    me = jnp.bitwise_and(lax.axis_index("seq"), GROUP - 1)
    return [jnp.bitwise_xor(me, k) for k in range(GROUP)]


def places(backward):
    return [GROUP - 1 - p for p in partners()] if backward else partners()


def columns(size, group, h=None):
    if h is None:
        return pl.ds(pl.multiple_of(group * size.wide, size.wide), size.wide)
    return pl.ds(pl.multiple_of(group * size.wide + h * size.dim, size.dim), size.dim)


def wave_heads(size, wave):
    return [(wave * size.each + i, slice(i * size.dim, (i + 1) * size.dim)) for i in range(size.each)]


def wave_columns(size, h):
    return slice(h % size.each * size.dim, (h % size.each + 1) * size.dim)


def all_pieces(size):
    return [(chunk, wave) for wave in range(size.waves) for chunk in range(GROUP)]


def last_order(size):
    usual = list(range(GROUP * (size.waves - 1)))
    return usual + [GROUP * (size.waves - 1) + k for k in reversed(range(GROUP))]


def rate_of(rates_ref, size, group, h):
    return rates_ref[pl.ds(group * size.per + h, 1), :]


def square_rate(rate, size):
    return rate[:, :1] if size.rows != size.dim else rate


def call(body, name, inputs, outputs, flops, moved, scratch=(), in_specs=None, out_specs=None, vmem=16, aliases=None):
    return pl.pallas_call(
        body,
        out_shape=outputs,
        in_specs=in_specs if in_specs is not None else [VMEM] * len(inputs),
        out_specs=out_specs if out_specs is not None else [VMEM] * len(outputs),
        scratch_shapes=list(scratch),
        input_output_aliases=aliases or {},
        compiler_params=pltpu.CompilerParams(vmem_limit_bytes=vmem * 1024 * 1024),
        cost_estimate=pl.CostEstimate(flops=flops, bytes_accessed=moved, transcendentals=0),
        name=name,
    )(*inputs)


def state_payloads(size, pieces, mark, rates_ref, group, outs, key_of, value_of):
    last, first = mark[size.rows - 1 :, :], mark[:1, :]
    ahead = steps_if(mark == last, (size.rows - 1.0) - position(size))
    for c, (chunk, wave) in enumerate(pieces):
        for h, cols in wave_heads(size, wave):
            weight = decay(ahead, rate_of(rates_ref, size, group[chunk], h))
            high, low = halves(value_of(c, h, cols).astype(f32) * weight)
            outs[c][cols, :] = token_product(key_of(c, h, cols), high, low)
        outs[c][size.state :, :] = info_rows(size, last, first)


def first_states(size, pieces, seg, decay_span, key_rows, value_rows):
    n = len(pieces)
    wide = size.each * size.dim

    def body(seg_hbm, span_hbm, key_hbm, value_hbm, *refs):
        outs, mark_ref, rates_ref = refs[:n], refs[n], refs[n + 1]
        seg_row, span_row, keys, values, sems = refs[n + 2 :]
        group = partners()
        small = (
            pltpu.make_async_copy(seg_hbm, seg_row, sems.at[2, 0]),
            pltpu.make_async_copy(span_hbm, span_row, sems.at[2, 1]),
        )
        copies = []
        for copy in small:
            copy.start()
        for c, (chunk, wave) in enumerate(pieces):
            here = pl.ds(pl.multiple_of(group[chunk] * size.wide + wave * wide, wide), wide)
            copies += [
                pltpu.make_async_copy(key_hbm.at[:, here], keys.at[c], sems.at[0, c]),
                pltpu.make_async_copy(value_hbm.at[:, here], values.at[c], sems.at[1, c]),
            ]
        for copy in copies:
            copy.start()
        for copy in small:
            copy.wait()
        mark = jnp.broadcast_to(seg_row[...].astype(f32) + 1.0, (size.dim, size.rows)).T
        mark_ref[...] = mark
        rates_ref[...] = jnp.broadcast_to(-1.0 / span_row[...], (size.dim, size.heads)).T
        for copy in copies:
            copy.wait()
        state_payloads(
            size, pieces, mark, rates_ref, group, outs,
            lambda c, h, cols: keys[c, :, cols], lambda c, h, cols: values[c, :, cols],
        )

    held = (n, size.rows, wide)
    outs = call(
        body, "states", (seg, decay_span.reshape(1, size.heads), key_rows, value_rows),
        [size.payload] * n + [
            jax.ShapeDtypeStruct((size.rows, size.dim), f32),
            jax.ShapeDtypeStruct((size.heads, size.dim), f32),
        ],
        n * size.each * 4 * size.rows * size.dim * size.dim, n * wide * size.rows * 8,
        [
            pltpu.VMEM((1, size.rows), jnp.int32),
            pltpu.VMEM((1, size.heads), f32),
            pltpu.VMEM(held, bf16),
            pltpu.VMEM(held, bf16),
            pltpu.SemaphoreType.DMA((3, max(n, 2))),
        ],
        [HBM] * 4, vmem=60,
    )
    return outs[:n], outs[n], outs[n + 1]


def more_states(size, pieces, mark, rates, key_rows, value_rows):
    def body(mark_ref, rates_ref, key_ref, value_ref, *outs):
        group = partners()

        def head(ref):
            return lambda c, h, cols: ref[:, columns(size, group[pieces[c][0]], h)]

        state_payloads(
            size, pieces, mark_ref[...], rates_ref, group, outs, head(key_ref), head(value_ref)
        )

    n = len(pieces)
    return call(
        body, "states", (mark, rates, key_rows, value_rows), [size.payload] * n,
        n * size.each * 4 * size.rows * size.dim * size.dim, n * size.state * size.rows * 8,
    )


def nearby_attended(size, mark, rates, queries, key_rows, value_rows):
    def body(mark_ref, rates_ref, query_ref, key_ref, value_ref, out_ref):
        gap = pair_steps(mark_ref[...], size)
        for h in range(size.heads):
            cols = slice(h * size.dim, (h + 1) * size.dim)
            rate = square_rate(rates_ref[h : h + 1, :], size)
            weight = decay(gap, rate)
            query, key, value = query_ref[:, cols], key_ref[:, cols], value_ref[:, cols]
            high, low = halves(dot(query, key, 1, 1) * weight)
            out_ref[:, cols] = dot(
                jnp.concatenate([high, low], 1), jnp.concatenate([value, value], 0)
            )

    return call(
        body, "nearby", (mark, rates, queries, key_rows, value_rows), [size.block],
        size.heads * 6 * size.rows * size.dim * size.dim, size.features * size.rows * 10,
    )[0]


def put_rows(ref, at, rows):
    ref[at : at + rows.shape[0], :] = rows


def group_total(size, backward, wave, rates, parts, riders=(), count=False):
    mark_row = size.state + (1 if backward else 0)

    def body(rates_ref, *refs):
        ins, rides = refs[:GROUP], refs[GROUP : GROUP + len(riders)]
        outs = refs[GROUP + len(riders) :]
        place = places(backward)
        marks = [ref[mark_row : mark_row + 1, :] for ref in ins]
        end = marks[0]
        for mark in marks[1:]:
            end = jnp.minimum(end, mark) if backward else jnp.maximum(end, mark)
        steps = [
            steps_if(marks[k] == end, ((GROUP - 1 - place[k]) * size.rows).astype(f32))
            for k in range(GROUP)
        ]
        me = partners()[0]
        for h, cols in wave_heads(size, wave):
            rate = rate_of(rates_ref, size, me, h)
            total = None
            for k in range(GROUP):
                term = decay(steps[k], rate) * ins[k][cols, :]
                total = term if total is None else total + term
            outs[0][cols, :] = total
        rows = [ride[...] for ride in rides] or [ref[size.state :, :] for ref in ins]
        put_rows(outs[0], size.state, with_marks(size, end, end, sum(rows)))
        if count:
            outs[1][...] = sum(rows)

    return call(
        body, "total", (rates, *parts, *riders), [size.payload] + [size.rows_of_gain] * count,
        size.state * size.dim * 8, size.state * size.dim * 20,
    )


def group_prefixes(size, backward, wave, rates, parts, entering, riders=(), own=()):
    mark_row = size.state + (1 if backward else 0)

    def body(rates_ref, *refs):
        ins, enter, refs = refs[:GROUP], refs[GROUP], refs[GROUP + 1 :]
        rows = [ref[...] for ref in refs[: len(riders)]]
        rows += [ref[size.state :, :] for ref in refs[len(riders) : len(riders) + len(own)]]
        outs = refs[len(riders) + len(own) :]
        gains = sum(rows) + enter[size.state :, :] if own else sum(rows)
        if not rows:
            gains = jnp.zeros((size.info, size.dim), f32)
        place = places(backward)
        me = partners()[0]
        marks = [ref[mark_row : mark_row + 1, :] for ref in ins]
        block, members = lax.axis_index("seq"), lax.axis_size("seq")
        first = block >= members - GROUP if backward else block < GROUP
        outer = jnp.where(first, FAR if backward else 0.0, enter[size.state : size.state + 1, :])
        steps = []
        for to in range(GROUP):
            now = outer
            for k in range(GROUP):
                if backward:
                    now = jnp.where(place[k] < place[to], jnp.minimum(now, marks[k]), now)
                else:
                    now = jnp.where(place[k] < place[to], jnp.maximum(now, marks[k]), now)
            put_rows(outs[to], size.state, with_marks(size, now, now, gains))
            far = (place[to] * size.rows).astype(f32)
            steps.append([steps_if(jnp.logical_and(outer == now, jnp.logical_not(first)), far)])
            for k in range(GROUP):
                gap = place[to] - 1 - place[k]
                live = jnp.logical_and(marks[k] == now, gap >= 0)
                steps[to].append(steps_if(live, (gap * size.rows).astype(f32)))
        for h, cols in wave_heads(size, wave):
            rate = rate_of(rates_ref, size, me, h)
            for to in range(GROUP):
                total = decay(steps[to][0], rate) * enter[cols, :]
                for k in range(GROUP):
                    if k != to:
                        total += decay(steps[to][1 + k], rate) * ins[k][cols, :]
                outs[to][cols, :] = total

    return call(
        body, "prefixes", (rates, *parts, entering, *riders, *own), [size.payload] * GROUP,
        size.state * size.dim * 40, size.state * size.dim * 36,
    )


def whole_attended(size, wave, mark, rates, queries, out_grad, gain, near, entering, before=()):
    last = wave == size.waves - 1

    def body(mark_ref, rates_ref, query_ref, grad_ref, gain_ref, near_ref, *refs):
        states, earlier, outs = refs[:GROUP], refs[GROUP : GROUP + len(before)], refs[GROUP + len(before) :]
        group = partners()
        mark = mark_ref[...]
        behind = steps_if(mark == states[0][size.state : size.state + 1, :], position(size) + 1.0)
        square = earlier[1][...] if before else jnp.zeros((size.rows, size.dim), f32)
        cross = earlier[2][...] if before else jnp.zeros((size.rows, size.dim), f32)
        for c in range(GROUP):
            for h, cols in wave_heads(size, wave):
                here = columns(size, group[c], h)
                weight = decay(behind, rate_of(rates_ref, size, group[c], h))
                query = query_ref[:, here]
                high, low = halves(states[c][cols, :])
                inter = dot(jnp.concatenate([query, query], 1), jnp.concatenate([high, low], 0))
                out = near_ref[:, here] + weight * inter
                outs[0][:, here] = out
                square += out * out
                cross += grad_ref[:, here].astype(f32) * gain_ref[:, here] * out
        if last:
            square = jnp.sum(square.T, axis=0, keepdims=True)
            cross = jnp.sum(cross.T, axis=0, keepdims=True)
            index = lax.broadcasted_iota(jnp.int32, (8, size.rows), 0)
            outs[1][...] = jnp.where(index == 0, square, jnp.where(index == 1, cross, 0.0))
        else:
            outs[1][...], outs[2][...] = square, cross

    if last:
        sums = [jax.ShapeDtypeStruct((8, size.rows), f32)]
    else:
        sums = [jax.ShapeDtypeStruct((size.rows, size.dim), f32)] * 2
    inputs = (mark, rates, queries, out_grad, gain, near, *entering, *before)
    return call(
        body, "attended", inputs, [size.block] + sums,
        GROUP * size.each * 4 * size.rows * size.dim * size.dim, GROUP * size.state * size.rows * 16,
        aliases={len(inputs) - len(before): 0} if before else {},
    )


def output_grad_states(size, pieces, norm, mark, rates, queries, out_grad, gain, sums, attended):
    n = len(pieces)

    def body(mark_ref, rates_ref, query_ref, grad_ref, gain_ref, att_ref, *refs):
        sums_refs, outs = refs[: len(sums)], refs[len(sums) :]
        group = partners()
        mark = mark_ref[...]
        last, first = mark[size.rows - 1 :, :], mark[:1, :]
        wide = (size.dim, size.rows)
        square = jnp.broadcast_to(sum(ref[0:1, :] for ref in sums_refs), wide).T
        cross = jnp.broadcast_to(sum(ref[1:2, :] for ref in sums_refs), wide).T
        inv = lax.rsqrt(square / norm + 1e-06)
        pull = inv * inv * inv * cross / norm
        gone = steps_if(mark == first, position(size))
        for c, (chunk, wave) in enumerate(pieces):
            back_ref, state_ref = outs[2 * c : 2 * c + 2]
            gains = []
            for h in range(size.per):
                if wave > 0 and h // size.each != wave:
                    continue
                here, cols = columns(size, group[chunk], h), wave_columns(size, h)
                grad = grad_ref[:, here].astype(f32) * inv
                att = att_ref[:, here]
                if wave == 0:
                    gains.append(jnp.sum(grad * att, axis=0, keepdims=True))
                if h // size.each == wave:
                    weight = decay(gone, rate_of(rates_ref, size, group[chunk], h))
                    back = gain_ref[:, here] * grad - att * pull
                    back_ref[:, cols] = back
                    high, low = halves(back * weight)
                    state_ref[cols, :] = token_product(query_ref[:, here], high, low)
            put_rows(state_ref, size.state, info_rows(size, last, first, gains))

    part = jax.ShapeDtypeStruct((size.rows, size.state), f32)
    outs = call(
        body, "back", (mark, rates, queries, out_grad, gain, attended, *sums),
        [part, size.payload] * n,
        n * size.each * 4 * size.rows * size.dim * size.dim, n * size.state * size.rows * 16,
    )
    return outs[0::2], outs[1::2]


def local_gradients(size, mark, rates, queries, key_rows, value_rows, back, entering):
    pieces = all_pieces(size)
    n = len(pieces)

    def body(mark_ref, rates_ref, query_ref, key_ref, value_ref, *refs):
        backs, states = refs[:n], refs[n : 2 * n]
        out_hbm, local_key, local_value, done, sems = refs[2 * n :]
        group = partners()
        mark = mark_ref[...]
        gap, turned_gap = pair_steps(mark, size), pair_steps(mark, size, 0)
        behind = steps_if(mark == states[0][size.state : size.state + 1, :], position(size) + 1.0)
        copies = []
        for c in range(GROUP):
            for h in range(size.per):
                here = columns(size, group[c], h)
                piece = pieces.index((c, h // size.each))
                near = slice(c * size.wide + h * size.dim, c * size.wide + (h + 1) * size.dim)
                cols = slice(h % size.each * size.dim, (h % size.each + 1) * size.dim)
                rate = rate_of(rates_ref, size, group[c], h)
                rows_rate = square_rate(rate, size)
                weight, turned_weight = decay(gap, rows_rate), decay(turned_gap, rows_rate)
                query, key, value = query_ref[:, here], key_ref[:, here], value_ref[:, here]
                high, low = halves(backs[piece][:, cols])
                both, values = jnp.concatenate([high, low], 1), jnp.concatenate([value, value], 1)
                grads_high, grads_low = halves(dot(both, values, 1, 1) * weight)
                part = dot(
                    jnp.concatenate([grads_high, grads_low], 1), jnp.concatenate([key, key], 0)
                )
                state_high, state_low = halves(states[piece][cols, :])
                inter = dot(
                    jnp.concatenate([high, high, low], 1),
                    jnp.concatenate([state_high, state_low, state_high], 1),
                    1, 1,
                )
                done[c, :, h * size.dim : (h + 1) * size.dim] = (
                    part + decay(behind, rate) * inter
                ).astype(bf16)
                grads_high, grads_low = halves(dot(values, both, 1, 1) * turned_weight)
                local_key[:, near] = dot(
                    jnp.concatenate([grads_high, grads_low], 1),
                    jnp.concatenate([query, query], 0),
                )
                score_high, score_low = halves(dot(key, query, 1, 1) * turned_weight)
                local_value[:, near] = dot(
                    jnp.concatenate([score_high, score_high, score_low], 1),
                    jnp.concatenate([high, low, high], 0),
                )
            copies.append(
                pltpu.make_async_copy(
                    done.at[c], out_hbm.at[:, columns(size, group[c])], sems.at[c]
                )
            )
            copies[c].start()
        for copy in copies:
            copy.wait()

    return call(
        body, "gradients", (mark, rates, queries, key_rows, value_rows, *back, *entering),
        [jax.ShapeDtypeStruct((size.rows, size.features), bf16), size.block, size.block],
        size.heads * 26 * size.rows * size.dim * size.dim, size.features * size.rows * 24,
        [pltpu.VMEM((GROUP, size.rows, size.wide), bf16), pltpu.SemaphoreType.DMA((GROUP,))],
        None, [HBM, VMEM, VMEM],
    )


def final_gradients(size, mark, rates, key_rows, value_rows, local_key, local_value, entering):
    def body(mark_ref, rates_ref, key_ref, value_ref, local_key_ref, local_value_ref, *refs):
        n = GROUP * size.waves
        states, (keys_hbm, values_hbm, gain_hbm) = refs[:n], refs[n : n + 3]
        states = [states[last_order(size).index(i)] for i in range(n)]
        keys, values, gains, sems = refs[n + 3 :]
        group = partners()
        mark = mark_ref[...]
        left = steps_if(mark == states[0][size.state : size.state + 1, :], size.rows - position(size))
        for c in range(GROUP):
            for h in range(size.per):
                at = size.state + MARKS + h
                gains[:, columns(size, group[c], h)] = states[n - GROUP + c][at : at + 1, :]
        copies = [pltpu.make_async_copy(gains, gain_hbm, sems.at[2, 0])]
        copies[0].start()
        for c in range(GROUP):
            for h in range(size.per):
                here = columns(size, group[c], h)
                piece = c + GROUP * (h // size.each)
                at = slice(h % size.each * size.dim, (h % size.each + 1) * size.dim)
                cols = slice(h * size.dim, (h + 1) * size.dim)
                rate = rate_of(rates_ref, size, group[c], h)
                weight = decay(left, rate)
                key, value = key_ref[:, here], value_ref[:, here]
                high, low = halves(states[piece][at, :])
                from_values = dot(
                    jnp.concatenate([value, value], 1), jnp.concatenate([high, low], 1), 1, 1
                )
                from_keys = dot(jnp.concatenate([key, key], 1), jnp.concatenate([high, low], 0))
                near = slice(c * size.wide + h * size.dim, c * size.wide + (h + 1) * size.dim)
                keys[c, :, cols] = (local_key_ref[:, near] + weight * from_values).astype(bf16)
                values[c, :, cols] = (local_value_ref[:, near] + weight * from_keys).astype(bf16)
            here = columns(size, group[c])
            for copy in (
                pltpu.make_async_copy(keys.at[c], keys_hbm.at[:, here], sems.at[0, c]),
                pltpu.make_async_copy(values.at[c], values_hbm.at[:, here], sems.at[1, c]),
            ):
                copy.start()
                copies.append(copy)
        for copy in copies:
            copy.wait()

    shape = jax.ShapeDtypeStruct((size.rows, size.features), bf16)
    held = pltpu.VMEM((GROUP, size.rows, size.wide), bf16)
    return call(
        body, "final",
        (
            mark, rates, key_rows, value_rows, local_key, local_value,
            *[entering[i] for i in last_order(size)],
        ),
        [shape, shape, jax.ShapeDtypeStruct((1, size.features), f32)],
        size.heads * 8 * size.rows * size.dim * size.dim, size.features * size.rows * 24,
        [held, held, pltpu.VMEM((1, size.features), f32), pltpu.SemaphoreType.DMA((3, GROUP))],
        None, [HBM] * 3,
    )


def swap(array, distance):
    members = lax.axis_size("seq")
    return lax.ppermute(array, "seq", [(i, i ^ distance) for i in range(members)])


def exchange(payloads):
    return [payloads[0]] + [swap(payloads[k], k) for k in range(1, GROUP)]


def shifted(array, by):
    members = lax.axis_size("seq")
    pairs = [(i, i + by) for i in range(members) if 0 <= i + by < members]
    return lax.ppermute(array, "seq", pairs)


def cyclic(array, by):
    members = lax.axis_size("seq")
    return lax.ppermute(array, "seq", [(i, (i + by) % members) for i in range(members)])


def reach_of_documents(size):
    longest = lax.axis_size("seq") * size.rows // 4
    return max(longest - 2, 0) // (GROUP * size.rows) + 1


def from_other_groups(size, backward, wave, decay_span, total):
    needed = reach_of_documents(size)
    way = -GROUP if backward else GROUP
    if needed == 1:
        return cyclic(total, way)
    result = shifted(total, way)
    reach = 1
    start = partners()[0] * size.per + wave * size.each
    mine = lax.dynamic_slice(decay_span, (start,), (size.each,))
    while reach < needed:
        incoming = shifted(result, way * reach)
        passes = incoming[size.state, 0] == result[size.state, 0]
        factor = jnp.where(passes, jnp.exp(-(reach * GROUP * size.rows) / mine), 0.0)
        factor = jnp.repeat(factor, size.dim)[:, None]
        result = result.at[: size.state].add(factor * incoming[: size.state])
        reach *= 2
    return result


def local(queries, key_rows, value_rows, segment_ids, decay_span, norm_gain, out_grad):
    size = Sizes(queries, decay_span)
    norm = size.features * lax.axis_size("head")
    members = lax.axis_size("seq")
    seg = segment_ids.reshape(1, size.rows)
    gain = norm_gain.reshape(1, size.features)
    waves = range(size.waves)
    sent = [[(chunk, wave) for chunk in (3, 1, 2)] for wave in waves]
    kept = [(0, wave) for wave in waves]
    every = all_pieces(size)

    outs, mark, rates = first_states(size, sent[0], seg, decay_span, key_rows, value_rows)
    common = (mark, rates)
    states = dict(zip(sent[0], outs))
    later = sum(sent[1:], []) + kept
    states |= zip(later, more_states(size, later, *common, key_rows, value_rows))
    near = nearby_attended(size, *common, queries, key_rows, value_rows)
    parts = {w: exchange({k: states[k, w] for k in range(GROUP)}) for w in waves}
    totals = {w: group_total(size, False, w, rates, parts[w])[0] for w in waves}
    outer = {w: from_other_groups(size, False, w, decay_span, totals[w]) for w in waves}
    entering = {}
    for w in waves:
        entering[w] = exchange(group_prefixes(size, False, w, rates, parts[w], outer[w]))

    entering = sum([entering[w] for w in waves], [])
    outs = ()
    for w in waves:
        states = entering[w * GROUP : (w + 1) * GROUP]
        outs = whole_attended(size, w, *common, queries, out_grad, gain, near, states, outs)
    attended, sums = outs
    if lax.axis_size("head") == 2:
        sums = (sums, lax.ppermute(sums, "head", [(0, 1), (1, 0)]))
    else:
        sums = (lax.psum(sums, "head"),)
    back, states = {}, {}
    for pieces in [*sent, kept]:
        backs, payloads = output_grad_states(
            size, pieces, norm, *common, queries, out_grad, gain, sums, attended
        )
        back |= zip(pieces, backs)
        states |= zip(pieces, payloads)

    parts = {w: exchange({k: states[k, w] for k in range(GROUP)}) for w in waves}
    back = [back[piece] for piece in every]
    totals, leaving, last = {}, [], size.waves - 1
    rides = size.waves > 1 and reach_of_documents(size) == 1 and members > GROUP
    totals[0], *gains = group_total(size, True, 0, rates, parts[0], (), True)
    apart = 2 if rides else 1
    while apart * GROUP < members:
        gains = [sum(gains), cyclic(sum(gains), -apart * GROUP)]
        apart *= 2
    for w in waves[1:]:
        riders = gains if rides and w == last else ()
        totals[w] = group_total(size, True, w, rates, parts[w], riders)[0]
    outer = {w: from_other_groups(size, True, w, decay_span, totals[w]) for w in waves}
    for w in waves:
        riders = gains if w == last and not rides else ()
        own = (totals[w],) if w == last and rides else ()
        leaving += exchange(
            group_prefixes(size, True, w, rates, parts[w], outer[w], riders, own)
        )

    query_grad, local_key, local_value = local_gradients(
        size, *common, queries, key_rows, value_rows, back, entering
    )
    key_grad, value_grad, gain_grad = final_gradients(
        size, *common, key_rows, value_rows, local_key, local_value, leaving
    )
    return query_grad, key_grad, value_grad, gain_grad.reshape(size.features)


def solution(mesh):
    rows = P("seq", "head")
    in_specs = (rows, rows, rows, P("seq"), P("head"), P("head"), rows)
    return jax.shard_map(
        local, mesh=mesh, in_specs=in_specs, out_specs=(rows, rows, rows, P("head")), check_vma=False
    )
```

```python
import jax
import jax.numpy as jnp
from jax import lax
from jax.experimental import pallas as pl
from jax.experimental.pallas import tpu as pltpu
from jax.sharding import PartitionSpec as P

GROUP = 4
MARKS = 2
FAR = 1e9
NEVER = 1e30
f32 = jnp.float32
bf16 = jnp.bfloat16
HBM = pl.BlockSpec(memory_space=pltpu.HBM)
VMEM = pl.BlockSpec(memory_space=pltpu.VMEM)


def dot(a, b, over_a=1, over_b=0):
    return lax.dot_general(a, b, (((over_a,), (over_b,)), ((), ())), preferred_element_type=f32)


def halves(x):
    high = x.astype(bf16)
    return high, (x - high.astype(f32)).astype(bf16)


def decay(steps, rate):
    return jnp.exp(steps * rate)


class Sizes:
    def __init__(self, queries, decay_span):
        self.rows = queries.shape[0]
        self.heads = decay_span.shape[0]
        self.features = queries.shape[1]
        self.dim = self.features // self.heads
        self.per = self.heads // GROUP
        self.wide = self.per * self.dim
        self.info = -(-(MARKS + self.per) // 8) * 8
        self.waves = 2 if self.per % 2 == 0 else 1
        self.each = self.per // self.waves
        self.state = self.each * self.dim
        self.payload = jax.ShapeDtypeStruct((self.state + self.info, self.dim), f32)
        self.block = jax.ShapeDtypeStruct((self.rows, self.features), f32)
        self.bare = jax.ShapeDtypeStruct((self.state, self.dim), f32)
        self.rows_of_gain = jax.ShapeDtypeStruct((self.info, self.dim), f32)


def position(size):
    return lax.broadcasted_iota(jnp.int32, (size.rows, size.dim), 0).astype(f32)


def steps_if(live, steps):
    return jnp.where(live, steps, NEVER)


def pair_steps(mark, size, earlier=1):
    shape = (size.rows, size.rows)
    here = mark if size.rows == size.dim else jnp.broadcast_to(mark[:, :1], shape)
    later = lax.broadcasted_iota(jnp.int32, shape, 1 - earlier)
    gap = later - lax.broadcasted_iota(jnp.int32, shape, earlier)
    return steps_if(jnp.logical_and(gap >= 0, here == here.T), gap.astype(f32))


def token_product(a, high, low):
    turned = a.T
    return dot(jnp.concatenate([turned, turned], 1), jnp.concatenate([high, low], 0))


def info_rows(size, last, first, more=()):
    index = lax.broadcasted_iota(jnp.int32, (size.info, size.dim), 0)
    rows = jnp.zeros((size.info, size.dim), f32)
    for i, row in enumerate((last, first, *more)):
        rows = jnp.where(index == i, row, rows)
    return rows


def with_marks(size, last, first, rows):
    index = lax.broadcasted_iota(jnp.int32, (size.info, size.dim), 0)
    return jnp.where(index == 0, last, jnp.where(index == 1, first, rows))


def partners():
    me = jnp.bitwise_and(lax.axis_index("seq"), GROUP - 1)
    return [jnp.bitwise_xor(me, k) for k in range(GROUP)]


def places(backward):
    return [GROUP - 1 - p for p in partners()] if backward else partners()


def columns(size, group, h=None):
    if h is None:
        return pl.ds(pl.multiple_of(group * size.wide, size.wide), size.wide)
    return pl.ds(pl.multiple_of(group * size.wide + h * size.dim, size.dim), size.dim)


def wave_heads(size, wave):
    return [(wave * size.each + i, slice(i * size.dim, (i + 1) * size.dim)) for i in range(size.each)]


def wave_columns(size, h):
    return slice(h % size.each * size.dim, (h % size.each + 1) * size.dim)


def all_pieces(size):
    return [(chunk, wave) for wave in range(size.waves) for chunk in range(GROUP)]


def last_order(size):
    usual = list(range(GROUP * (size.waves - 1)))
    return usual + [GROUP * (size.waves - 1) + k for k in reversed(range(GROUP))]


def rate_of(rates_ref, size, group, h):
    return rates_ref[pl.ds(group * size.per + h, 1), :]


def square_rate(rate, size):
    return rate[:, :1] if size.rows != size.dim else rate


def call(body, name, inputs, outputs, flops, moved, scratch=(), in_specs=None, out_specs=None, vmem=8, aliases=None):
    return pl.pallas_call(
        body,
        out_shape=outputs,
        in_specs=in_specs if in_specs is not None else [VMEM] * len(inputs),
        out_specs=out_specs if out_specs is not None else [VMEM] * len(outputs),
        scratch_shapes=list(scratch),
        input_output_aliases=aliases or {},
        compiler_params=pltpu.CompilerParams(vmem_limit_bytes=vmem * 1024 * 1024),
        cost_estimate=pl.CostEstimate(flops=flops, bytes_accessed=moved, transcendentals=0),
        name=name,
    )(*inputs)


def state_payloads(size, pieces, mark, rates_ref, group, outs, key_of, value_of):
    last, first = mark[size.rows - 1 :, :], mark[:1, :]
    ahead = steps_if(mark == last, (size.rows - 1.0) - position(size))
    for c, (chunk, wave) in enumerate(pieces):
        for h, cols in wave_heads(size, wave):
            weight = decay(ahead, rate_of(rates_ref, size, group[chunk], h))
            high, low = halves(value_of(c, h, cols).astype(f32) * weight)
            outs[c][cols, :] = token_product(key_of(c, h, cols), high, low)
        outs[c][size.state :, :] = info_rows(size, last, first)


def first_states(size, pieces, seg, decay_span, key_rows, value_rows):
    n = len(pieces)
    wide = size.each * size.dim

    def body(seg_hbm, span_hbm, key_hbm, value_hbm, *refs):
        outs, mark_ref, rates_ref = refs[:n], refs[n], refs[n + 1]
        seg_row, span_row, keys, values, sems = refs[n + 2 :]
        group = partners()
        small = (
            pltpu.make_async_copy(seg_hbm, seg_row, sems.at[2, 0]),
            pltpu.make_async_copy(span_hbm, span_row, sems.at[2, 1]),
        )
        copies = []
        for copy in small:
            copy.start()
        for c, (chunk, wave) in enumerate(pieces):
            here = pl.ds(pl.multiple_of(group[chunk] * size.wide + wave * wide, wide), wide)
            copies += [
                pltpu.make_async_copy(key_hbm.at[:, here], keys.at[c], sems.at[0, c]),
                pltpu.make_async_copy(value_hbm.at[:, here], values.at[c], sems.at[1, c]),
            ]
        for copy in copies:
            copy.start()
        for copy in small:
            copy.wait()
        mark = jnp.broadcast_to(seg_row[...].astype(f32) + 1.0, (size.dim, size.rows)).T
        mark_ref[...] = mark
        rates_ref[...] = jnp.broadcast_to(-1.0 / span_row[...], (size.dim, size.heads)).T
        for copy in copies:
            copy.wait()
        state_payloads(
            size, pieces, mark, rates_ref, group, outs,
            lambda c, h, cols: keys[c, :, cols], lambda c, h, cols: values[c, :, cols],
        )

    held = (n, size.rows, wide)
    outs = call(
        body, "states", (seg, decay_span.reshape(1, size.heads), key_rows, value_rows),
        [size.payload] * n + [
            jax.ShapeDtypeStruct((size.rows, size.dim), f32),
            jax.ShapeDtypeStruct((size.heads, size.dim), f32),
        ],
        n * size.each * 4 * size.rows * size.dim * size.dim, n * wide * size.rows * 8,
        [
            pltpu.VMEM((1, size.rows), jnp.int32),
            pltpu.VMEM((1, size.heads), f32),
            pltpu.VMEM(held, bf16),
            pltpu.VMEM(held, bf16),
            pltpu.SemaphoreType.DMA((3, max(n, 2))),
        ],
        [HBM] * 4, vmem=60,
    )
    return outs[:n], outs[n], outs[n + 1]


def more_states(size, pieces, mark, rates, key_rows, value_rows):
    def body(mark_ref, rates_ref, key_ref, value_ref, *outs):
        group = partners()

        def head(ref):
            return lambda c, h, cols: ref[:, columns(size, group[pieces[c][0]], h)]

        state_payloads(
            size, pieces, mark_ref[...], rates_ref, group, outs, head(key_ref), head(value_ref)
        )

    n = len(pieces)
    return call(
        body, "states", (mark, rates, key_rows, value_rows), [size.payload] * n,
        n * size.each * 4 * size.rows * size.dim * size.dim, n * size.state * size.rows * 8,
    )


def nearby_attended(size, mark, rates, queries, key_rows, value_rows):
    def body(mark_ref, rates_ref, query_ref, key_ref, value_ref, out_ref):
        gap = pair_steps(mark_ref[...], size)
        for h in range(size.heads):
            cols = slice(h * size.dim, (h + 1) * size.dim)
            rate = square_rate(rates_ref[h : h + 1, :], size)
            weight = decay(gap, rate)
            query, key, value = query_ref[:, cols], key_ref[:, cols], value_ref[:, cols]
            high, low = halves(dot(query, key, 1, 1) * weight)
            out_ref[:, cols] = dot(
                jnp.concatenate([high, low], 1), jnp.concatenate([value, value], 0)
            )

    return call(
        body, "nearby", (mark, rates, queries, key_rows, value_rows), [size.block],
        size.heads * 6 * size.rows * size.dim * size.dim, size.features * size.rows * 10,
    )[0]


def put_rows(ref, at, rows):
    ref[at : at + rows.shape[0], :] = rows


def group_total(size, backward, wave, rates, parts, riders=(), count=False):
    mark_row = size.state + (1 if backward else 0)

    def body(rates_ref, *refs):
        ins, rides = refs[:GROUP], refs[GROUP : GROUP + len(riders)]
        outs = refs[GROUP + len(riders) :]
        place = places(backward)
        marks = [ref[mark_row : mark_row + 1, :] for ref in ins]
        end = marks[0]
        for mark in marks[1:]:
            end = jnp.minimum(end, mark) if backward else jnp.maximum(end, mark)
        steps = [
            steps_if(marks[k] == end, ((GROUP - 1 - place[k]) * size.rows).astype(f32))
            for k in range(GROUP)
        ]
        me = partners()[0]
        for h, cols in wave_heads(size, wave):
            rate = rate_of(rates_ref, size, me, h)
            total = None
            for k in range(GROUP):
                term = decay(steps[k], rate) * ins[k][cols, :]
                total = term if total is None else total + term
            outs[0][cols, :] = total
        rows = [ride[...] for ride in rides] or [ref[size.state :, :] for ref in ins]
        put_rows(outs[0], size.state, with_marks(size, end, end, sum(rows)))
        if count:
            outs[1][...] = sum(rows)

    return call(
        body, "total", (rates, *parts, *riders), [size.payload] + [size.rows_of_gain] * count,
        size.state * size.dim * 8, size.state * size.dim * 20,
    )


def group_prefixes(size, backward, wave, rates, parts, entering, riders=(), own=()):
    mark_row = size.state + (1 if backward else 0)

    def body(rates_ref, *refs):
        ins, enter, refs = refs[:GROUP], refs[GROUP], refs[GROUP + 1 :]
        rows = [ref[...] for ref in refs[: len(riders)]]
        rows += [ref[size.state :, :] for ref in refs[len(riders) : len(riders) + len(own)]]
        outs = refs[len(riders) + len(own) :]
        gains = sum(rows) + enter[size.state :, :] if own else sum(rows)
        if not rows:
            gains = jnp.zeros((size.info, size.dim), f32)
        place = places(backward)
        me = partners()[0]
        marks = [ref[mark_row : mark_row + 1, :] for ref in ins]
        block, members = lax.axis_index("seq"), lax.axis_size("seq")
        first = block >= members - GROUP if backward else block < GROUP
        outer = jnp.where(first, FAR if backward else 0.0, enter[size.state : size.state + 1, :])
        steps = []
        for to in range(GROUP):
            now = outer
            for k in range(GROUP):
                if backward:
                    now = jnp.where(place[k] < place[to], jnp.minimum(now, marks[k]), now)
                else:
                    now = jnp.where(place[k] < place[to], jnp.maximum(now, marks[k]), now)
            if to == 0 or backward:
                put_rows(outs[to], size.state, with_marks(size, now, now, gains))
            far = (place[to] * size.rows).astype(f32)
            steps.append([steps_if(jnp.logical_and(outer == now, jnp.logical_not(first)), far)])
            for k in range(GROUP):
                gap = place[to] - 1 - place[k]
                live = jnp.logical_and(marks[k] == now, gap >= 0)
                steps[to].append(steps_if(live, (gap * size.rows).astype(f32)))
        for h, cols in wave_heads(size, wave):
            rate = rate_of(rates_ref, size, me, h)
            for to in range(GROUP):
                total = decay(steps[to][0], rate) * enter[cols, :]
                for k in range(GROUP):
                    if k != to:
                        total += decay(steps[to][1 + k], rate) * ins[k][cols, :]
                outs[to][cols, :] = total

    return call(
        body, "prefixes", (rates, *parts, entering, *riders, *own), [size.payload] + [size.payload if backward else size.bare] * (GROUP - 1),
        size.state * size.dim * 40, size.state * size.dim * 36,
    )


def whole_attended(size, wave, mark, rates, queries, out_grad, gain, near, entering, before=()):
    last = wave == size.waves - 1

    def body(mark_ref, rates_ref, query_ref, grad_ref, gain_ref, near_ref, *refs):
        states, earlier, outs = refs[:GROUP], refs[GROUP : GROUP + len(before)], refs[GROUP + len(before) :]
        group = partners()
        mark = mark_ref[...]
        behind = steps_if(mark == states[0][size.state : size.state + 1, :], position(size) + 1.0)
        square = earlier[1][...] if before else jnp.zeros((size.rows, size.dim), f32)
        cross = earlier[2][...] if before else jnp.zeros((size.rows, size.dim), f32)
        for c in range(GROUP):
            for h, cols in wave_heads(size, wave):
                here = columns(size, group[c], h)
                weight = decay(behind, rate_of(rates_ref, size, group[c], h))
                query = query_ref[:, here]
                high, low = halves(states[c][cols, :])
                inter = dot(jnp.concatenate([query, query], 1), jnp.concatenate([high, low], 0))
                out = near_ref[:, here] + weight * inter
                outs[0][:, here] = out
                square += out * out
                cross += grad_ref[:, here].astype(f32) * gain_ref[:, here] * out
        if last:
            square = jnp.sum(square.T, axis=0, keepdims=True)
            cross = jnp.sum(cross.T, axis=0, keepdims=True)
            index = lax.broadcasted_iota(jnp.int32, (8, size.rows), 0)
            outs[1][...] = jnp.where(index == 0, square, jnp.where(index == 1, cross, 0.0))
        else:
            outs[1][...], outs[2][...] = square, cross

    if last:
        sums = [jax.ShapeDtypeStruct((8, size.rows), f32)]
    else:
        sums = [jax.ShapeDtypeStruct((size.rows, size.dim), f32)] * 2
    inputs = (mark, rates, queries, out_grad, gain, near, *entering, *before)
    return call(
        body, "attended", inputs, [size.block] + sums,
        GROUP * size.each * 4 * size.rows * size.dim * size.dim, GROUP * size.state * size.rows * 16,
        aliases={len(inputs) - len(before): 0} if before else {},
    )


def output_grad_states(size, pieces, norm, mark, rates, queries, out_grad, gain, sums, attended):
    n = len(pieces)

    def body(mark_ref, rates_ref, query_ref, grad_ref, gain_ref, att_ref, *refs):
        sums_refs, outs = refs[: len(sums)], refs[len(sums) :]
        group = partners()
        mark = mark_ref[...]
        last, first = mark[size.rows - 1 :, :], mark[:1, :]
        wide = (size.dim, size.rows)
        square = jnp.broadcast_to(sum(ref[0:1, :] for ref in sums_refs), wide).T
        cross = jnp.broadcast_to(sum(ref[1:2, :] for ref in sums_refs), wide).T
        inv = lax.rsqrt(square / norm + 1e-06)
        pull = inv * inv * inv * cross / norm
        gone = steps_if(mark == first, position(size))
        for c, (chunk, wave) in enumerate(pieces):
            back_ref, state_ref = outs[2 * c : 2 * c + 2]
            gains = []
            for h in range(size.per):
                if wave > 0 and h // size.each != wave:
                    continue
                here, cols = columns(size, group[chunk], h), wave_columns(size, h)
                grad = grad_ref[:, here].astype(f32) * inv
                att = att_ref[:, here]
                if wave == 0:
                    gains.append(jnp.sum(grad * att, axis=0, keepdims=True))
                if h // size.each == wave:
                    weight = decay(gone, rate_of(rates_ref, size, group[chunk], h))
                    back = gain_ref[:, here] * grad - att * pull
                    back_ref[:, cols] = back
                    high, low = halves(back * weight)
                    state_ref[cols, :] = token_product(query_ref[:, here], high, low)
            put_rows(state_ref, size.state, info_rows(size, last, first, gains))

    part = jax.ShapeDtypeStruct((size.rows, size.state), f32)
    outs = call(
        body, "back", (mark, rates, queries, out_grad, gain, attended, *sums),
        [part, size.payload] * n,
        n * size.each * 4 * size.rows * size.dim * size.dim, n * size.state * size.rows * 16,
    )
    return outs[0::2], outs[1::2]


def local_gradients(size, mark, rates, queries, key_rows, value_rows, back, entering):
    pieces = all_pieces(size)
    n = len(pieces)

    def body(mark_ref, rates_ref, query_ref, key_ref, value_ref, *refs):
        backs, states = refs[:n], refs[n : 2 * n]
        out_hbm, local_key, local_value, done, sems = refs[2 * n :]
        group = partners()
        mark = mark_ref[...]
        gap, turned_gap = pair_steps(mark, size), pair_steps(mark, size, 0)
        behind = steps_if(mark == states[0][size.state : size.state + 1, :], position(size) + 1.0)
        copies = []
        for c in range(GROUP):
            for h in range(size.per):
                here = columns(size, group[c], h)
                piece = pieces.index((c, h // size.each))
                near = slice(c * size.wide + h * size.dim, c * size.wide + (h + 1) * size.dim)
                cols = slice(h % size.each * size.dim, (h % size.each + 1) * size.dim)
                rate = rate_of(rates_ref, size, group[c], h)
                rows_rate = square_rate(rate, size)
                weight, turned_weight = decay(gap, rows_rate), decay(turned_gap, rows_rate)
                query, key, value = query_ref[:, here], key_ref[:, here], value_ref[:, here]
                high, low = halves(backs[piece][:, cols])
                both, values = jnp.concatenate([high, low], 1), jnp.concatenate([value, value], 1)
                grads_high, grads_low = halves(dot(both, values, 1, 1) * weight)
                part = dot(
                    jnp.concatenate([grads_high, grads_low], 1), jnp.concatenate([key, key], 0)
                )
                state_high, state_low = halves(states[piece][cols, :])
                inter = dot(
                    jnp.concatenate([high, high, low], 1),
                    jnp.concatenate([state_high, state_low, state_high], 1),
                    1, 1,
                )
                done[c, :, h * size.dim : (h + 1) * size.dim] = (
                    part + decay(behind, rate) * inter
                ).astype(bf16)
                grads_high, grads_low = halves(dot(values, both, 1, 1) * turned_weight)
                local_key[:, near] = dot(
                    jnp.concatenate([grads_high, grads_low], 1),
                    jnp.concatenate([query, query], 0),
                )
                score_high, score_low = halves(dot(key, query, 1, 1) * turned_weight)
                local_value[:, near] = dot(
                    jnp.concatenate([score_high, score_high, score_low], 1),
                    jnp.concatenate([high, low, high], 0),
                )
            copies.append(
                pltpu.make_async_copy(
                    done.at[c], out_hbm.at[:, columns(size, group[c])], sems.at[c]
                )
            )
            copies[c].start()
        for copy in copies:
            copy.wait()

    return call(
        body, "gradients", (mark, rates, queries, key_rows, value_rows, *back, *entering),
        [jax.ShapeDtypeStruct((size.rows, size.features), bf16), size.block, size.block],
        size.heads * 26 * size.rows * size.dim * size.dim, size.features * size.rows * 24,
        [pltpu.VMEM((GROUP, size.rows, size.wide), bf16), pltpu.SemaphoreType.DMA((GROUP,))],
        None, [HBM, VMEM, VMEM],
    )


def final_gradients(size, mark, rates, key_rows, value_rows, local_key, local_value, entering):
    def body(mark_ref, rates_ref, key_ref, value_ref, local_key_ref, local_value_ref, *refs):
        n = GROUP * size.waves
        states, (keys_hbm, values_hbm, gain_hbm) = refs[:n], refs[n : n + 3]
        states = [states[last_order(size).index(i)] for i in range(n)]
        keys, values, gains, sems = refs[n + 3 :]
        group = partners()
        mark = mark_ref[...]
        left = steps_if(mark == states[0][size.state : size.state + 1, :], size.rows - position(size))
        for c in range(GROUP):
            for h in range(size.per):
                at = size.state + MARKS + h
                gains[:, columns(size, group[c], h)] = states[n - GROUP + c][at : at + 1, :]
        copies = [pltpu.make_async_copy(gains, gain_hbm, sems.at[2, 0])]
        copies[0].start()
        for c in range(GROUP):
            for h in range(size.per):
                here = columns(size, group[c], h)
                piece = c + GROUP * (h // size.each)
                at = slice(h % size.each * size.dim, (h % size.each + 1) * size.dim)
                cols = slice(h * size.dim, (h + 1) * size.dim)
                rate = rate_of(rates_ref, size, group[c], h)
                weight = decay(left, rate)
                key, value = key_ref[:, here], value_ref[:, here]
                high, low = halves(states[piece][at, :])
                from_values = dot(
                    jnp.concatenate([value, value], 1), jnp.concatenate([high, low], 1), 1, 1
                )
                from_keys = dot(jnp.concatenate([key, key], 1), jnp.concatenate([high, low], 0))
                near = slice(c * size.wide + h * size.dim, c * size.wide + (h + 1) * size.dim)
                keys[c, :, cols] = (local_key_ref[:, near] + weight * from_values).astype(bf16)
                values[c, :, cols] = (local_value_ref[:, near] + weight * from_keys).astype(bf16)
            here = columns(size, group[c])
            for copy in (
                pltpu.make_async_copy(keys.at[c], keys_hbm.at[:, here], sems.at[0, c]),
                pltpu.make_async_copy(values.at[c], values_hbm.at[:, here], sems.at[1, c]),
            ):
                copy.start()
                copies.append(copy)
        for copy in copies:
            copy.wait()

    shape = jax.ShapeDtypeStruct((size.rows, size.features), bf16)
    held = pltpu.VMEM((GROUP, size.rows, size.wide), bf16)
    return call(
        body, "final",
        (
            mark, rates, key_rows, value_rows, local_key, local_value,
            *[entering[i] for i in last_order(size)],
        ),
        [shape, shape, jax.ShapeDtypeStruct((1, size.features), f32)],
        size.heads * 8 * size.rows * size.dim * size.dim, size.features * size.rows * 24,
        [held, held, pltpu.VMEM((1, size.features), f32), pltpu.SemaphoreType.DMA((3, GROUP))],
        None, [HBM] * 3,
    )


def swap(array, distance):
    members = lax.axis_size("seq")
    return lax.ppermute(array, "seq", [(i, i ^ distance) for i in range(members)])


def exchange(payloads):
    return [payloads[0]] + [swap(payloads[k], k) for k in range(1, GROUP)]


def shifted(array, by):
    members = lax.axis_size("seq")
    pairs = [(i, i + by) for i in range(members) if 0 <= i + by < members]
    return lax.ppermute(array, "seq", pairs)


def cyclic(array, by):
    members = lax.axis_size("seq")
    return lax.ppermute(array, "seq", [(i, (i + by) % members) for i in range(members)])


def reach_of_documents(size):
    longest = lax.axis_size("seq") * size.rows // 4
    return max(longest - 2, 0) // (GROUP * size.rows) + 1


def from_other_groups(size, backward, wave, decay_span, total):
    needed = reach_of_documents(size)
    way = -GROUP if backward else GROUP
    if needed == 1:
        return cyclic(total, way)
    result = shifted(total, way)
    reach = 1
    start = partners()[0] * size.per + wave * size.each
    mine = lax.dynamic_slice(decay_span, (start,), (size.each,))
    while reach < needed:
        incoming = shifted(result, way * reach)
        passes = incoming[size.state, 0] == result[size.state, 0]
        factor = jnp.where(passes, jnp.exp(-(reach * GROUP * size.rows) / mine), 0.0)
        factor = jnp.repeat(factor, size.dim)[:, None]
        result = result.at[: size.state].add(factor * incoming[: size.state])
        reach *= 2
    return result


def local(queries, key_rows, value_rows, segment_ids, decay_span, norm_gain, out_grad):
    size = Sizes(queries, decay_span)
    norm = size.features * lax.axis_size("head")
    members = lax.axis_size("seq")
    seg = segment_ids.reshape(1, size.rows)
    gain = norm_gain.reshape(1, size.features)
    waves = range(size.waves)
    sent = [[(chunk, wave) for chunk in (3, 1, 2)] for wave in waves]
    kept = [(0, wave) for wave in waves]
    every = all_pieces(size)

    outs, mark, rates = first_states(size, sent[0], seg, decay_span, key_rows, value_rows)
    common = (mark, rates)
    states = dict(zip(sent[0], outs))
    later = sum(sent[1:], []) + kept
    states |= zip(later, more_states(size, later, *common, key_rows, value_rows))
    near = nearby_attended(size, *common, queries, key_rows, value_rows)
    parts = {w: exchange({k: states[k, w] for k in range(GROUP)}) for w in waves}
    totals = {w: group_total(size, False, w, rates, parts[w])[0] for w in waves}
    outer = {w: from_other_groups(size, False, w, decay_span, totals[w]) for w in waves}
    entering = {}
    for w in waves:
        entering[w] = exchange(group_prefixes(size, False, w, rates, parts[w], outer[w]))

    entering = sum([entering[w] for w in waves], [])
    outs = ()
    for w in waves:
        states = entering[w * GROUP : (w + 1) * GROUP]
        outs = whole_attended(size, w, *common, queries, out_grad, gain, near, states, outs)
    attended, sums = outs
    if lax.axis_size("head") == 2:
        sums = (sums, lax.ppermute(sums, "head", [(0, 1), (1, 0)]))
    else:
        sums = (lax.psum(sums, "head"),)
    back, states = {}, {}
    for pieces in [*sent, kept]:
        backs, payloads = output_grad_states(
            size, pieces, norm, *common, queries, out_grad, gain, sums, attended
        )
        back |= zip(pieces, backs)
        states |= zip(pieces, payloads)

    parts = {w: exchange({k: states[k, w] for k in range(GROUP)}) for w in waves}
    back = [back[piece] for piece in every]
    totals, leaving, last = {}, [], size.waves - 1
    rides = size.waves > 1 and reach_of_documents(size) == 1 and members > GROUP
    totals[0], *gains = group_total(size, True, 0, rates, parts[0], (), True)
    apart = 2 if rides else 1
    while apart * GROUP < members:
        gains = [sum(gains), cyclic(sum(gains), -apart * GROUP)]
        apart *= 2
    for w in waves[1:]:
        riders = gains if rides and w == last else ()
        totals[w] = group_total(size, True, w, rates, parts[w], riders)[0]
    outer = {w: from_other_groups(size, True, w, decay_span, totals[w]) for w in waves}
    for w in waves:
        riders = gains if w == last and not rides else ()
        own = (totals[w],) if w == last and rides else ()
        leaving += exchange(
            group_prefixes(size, True, w, rates, parts[w], outer[w], riders, own)
        )

    query_grad, local_key, local_value = local_gradients(
        size, *common, queries, key_rows, value_rows, back, entering
    )
    key_grad, value_grad, gain_grad = final_gradients(
        size, *common, key_rows, value_rows, local_key, local_value, leaving
    )
    return query_grad, key_grad, value_grad, gain_grad.reshape(size.features)


def solution(mesh):
    rows = P("seq", "head")
    in_specs = (rows, rows, rows, P("seq"), P("head"), P("head"), rows)
    return jax.shard_map(
        local, mesh=mesh, in_specs=in_specs, out_specs=(rows, rows, rows, P("head")), check_vma=False
    )
```

```python
import jax
import jax.numpy as jnp
from jax import lax
from jax.experimental import pallas as pl
from jax.experimental.pallas import tpu as pltpu
from jax.sharding import PartitionSpec as P

GROUP = 4
MARKS = 2
FAR = 1e9
NEVER = 1e30
f32 = jnp.float32
bf16 = jnp.bfloat16
HBM = pl.BlockSpec(memory_space=pltpu.HBM)
VMEM = pl.BlockSpec(memory_space=pltpu.VMEM)


def dot(a, b, over_a=1, over_b=0):
    return lax.dot_general(a, b, (((over_a,), (over_b,)), ((), ())), preferred_element_type=f32)


def halves(x):
    high = x.astype(bf16)
    return high, (x - high.astype(f32)).astype(bf16)


def decay(steps, rate):
    return jnp.exp(steps * rate)


class Sizes:
    def __init__(self, queries, decay_span):
        self.rows = queries.shape[0]
        self.heads = decay_span.shape[0]
        self.features = queries.shape[1]
        self.dim = self.features // self.heads
        self.per = self.heads // GROUP
        self.wide = self.per * self.dim
        self.info = -(-(MARKS + self.per) // 8) * 8
        self.waves = 2 if self.per % 2 == 0 else 1
        self.each = self.per // self.waves
        self.state = self.each * self.dim
        self.payload = jax.ShapeDtypeStruct((self.state + self.info, self.dim), f32)
        self.block = jax.ShapeDtypeStruct((self.rows, self.features), f32)
        self.bare = jax.ShapeDtypeStruct((self.state, self.dim), f32)
        self.rows_of_gain = jax.ShapeDtypeStruct((self.info, self.dim), f32)


def position(size):
    return lax.broadcasted_iota(jnp.int32, (size.rows, size.dim), 0).astype(f32)


def steps_if(live, steps):
    return jnp.where(live, steps, NEVER)


def pair_steps(mark, size, earlier=1):
    shape = (size.rows, size.rows)
    here = mark if size.rows == size.dim else jnp.broadcast_to(mark[:, :1], shape)
    later = lax.broadcasted_iota(jnp.int32, shape, 1 - earlier)
    gap = later - lax.broadcasted_iota(jnp.int32, shape, earlier)
    return steps_if(jnp.logical_and(gap >= 0, here == here.T), gap.astype(f32))


def token_product(a, high, low):
    turned = a.T
    return dot(jnp.concatenate([turned, turned], 1), jnp.concatenate([high, low], 0))


def info_rows(size, last, first, more=()):
    index = lax.broadcasted_iota(jnp.int32, (size.info, size.dim), 0)
    rows = jnp.zeros((size.info, size.dim), f32)
    for i, row in enumerate((last, first, *more)):
        rows = jnp.where(index == i, row, rows)
    return rows


def with_marks(size, last, first, rows):
    index = lax.broadcasted_iota(jnp.int32, (size.info, size.dim), 0)
    return jnp.where(index == 0, last, jnp.where(index == 1, first, rows))


def partners():
    me = jnp.bitwise_and(lax.axis_index("seq"), GROUP - 1)
    return [jnp.bitwise_xor(me, k) for k in range(GROUP)]


def places(backward):
    return [GROUP - 1 - p for p in partners()] if backward else partners()


def columns(size, group, h=None):
    if h is None:
        return pl.ds(pl.multiple_of(group * size.wide, size.wide), size.wide)
    return pl.ds(pl.multiple_of(group * size.wide + h * size.dim, size.dim), size.dim)


def wave_heads(size, wave):
    return [(wave * size.each + i, slice(i * size.dim, (i + 1) * size.dim)) for i in range(size.each)]


def wave_columns(size, h):
    return slice(h % size.each * size.dim, (h % size.each + 1) * size.dim)


def all_pieces(size):
    return [(chunk, wave) for wave in range(size.waves) for chunk in range(GROUP)]


def last_order(size):
    usual = list(range(GROUP * (size.waves - 1)))
    return usual + [GROUP * (size.waves - 1) + k for k in reversed(range(GROUP))]


def rate_of(rates_ref, size, group, h):
    return rates_ref[pl.ds(group * size.per + h, 1), :]


def square_rate(rate, size):
    return rate[:, :1] if size.rows != size.dim else rate


def call(body, name, inputs, outputs, flops, moved, scratch=(), in_specs=None, out_specs=None, vmem=8, aliases=None):
    return pl.pallas_call(
        body,
        out_shape=outputs,
        in_specs=in_specs if in_specs is not None else [VMEM] * len(inputs),
        out_specs=out_specs if out_specs is not None else [VMEM] * len(outputs),
        scratch_shapes=list(scratch),
        input_output_aliases=aliases or {},
        compiler_params=pltpu.CompilerParams(vmem_limit_bytes=vmem * 1024 * 1024),
        cost_estimate=pl.CostEstimate(flops=flops, bytes_accessed=moved, transcendentals=0),
        name=name,
    )(*inputs)


def state_payloads(size, pieces, mark, rates_ref, group, outs, key_of, value_of):
    last, first = mark[size.rows - 1 :, :], mark[:1, :]
    ahead = steps_if(mark == last, (size.rows - 1.0) - position(size))
    for c, (chunk, wave) in enumerate(pieces):
        for h, cols in wave_heads(size, wave):
            weight = decay(ahead, rate_of(rates_ref, size, group[chunk], h))
            high, low = halves(value_of(c, h, cols).astype(f32) * weight)
            outs[c][cols, :] = token_product(key_of(c, h, cols), high, low)
        outs[c][size.state :, :] = info_rows(size, last, first)


def first_states(size, pieces, seg, decay_span, key_rows, value_rows):
    n = len(pieces)
    wide = size.each * size.dim

    def body(seg_hbm, span_hbm, key_hbm, value_hbm, *refs):
        outs, mark_ref, rates_ref = refs[:n], refs[n], refs[n + 1]
        seg_row, span_row, keys, values, sems = refs[n + 2 :]
        group = partners()
        small = (
            pltpu.make_async_copy(seg_hbm, seg_row, sems.at[2, 0]),
            pltpu.make_async_copy(span_hbm, span_row, sems.at[2, 1]),
        )
        copies = []
        for copy in small:
            copy.start()
        for c, (chunk, wave) in enumerate(pieces):
            here = pl.ds(pl.multiple_of(group[chunk] * size.wide + wave * wide, wide), wide)
            copies += [
                pltpu.make_async_copy(key_hbm.at[:, here], keys.at[c], sems.at[0, c]),
                pltpu.make_async_copy(value_hbm.at[:, here], values.at[c], sems.at[1, c]),
            ]
        for copy in copies:
            copy.start()
        for copy in small:
            copy.wait()
        mark = jnp.broadcast_to(seg_row[...].astype(f32) + 1.0, (size.dim, size.rows)).T
        mark_ref[...] = mark
        rates_ref[...] = jnp.broadcast_to(-1.0 / span_row[...], (size.dim, size.heads)).T
        for copy in copies:
            copy.wait()
        state_payloads(
            size, pieces, mark, rates_ref, group, outs,
            lambda c, h, cols: keys[c, :, cols], lambda c, h, cols: values[c, :, cols],
        )

    held = (n, size.rows, wide)
    outs = call(
        body, "states", (seg, decay_span.reshape(1, size.heads), key_rows, value_rows),
        [size.payload] * n + [
            jax.ShapeDtypeStruct((size.rows, size.dim), f32),
            jax.ShapeDtypeStruct((size.heads, size.dim), f32),
        ],
        n * size.each * 4 * size.rows * size.dim * size.dim, n * wide * size.rows * 8,
        [
            pltpu.VMEM((1, size.rows), jnp.int32),
            pltpu.VMEM((1, size.heads), f32),
            pltpu.VMEM(held, bf16),
            pltpu.VMEM(held, bf16),
            pltpu.SemaphoreType.DMA((3, max(n, 2))),
        ],
        [HBM] * 4, vmem=60,
    )
    return outs[:n], outs[n], outs[n + 1]


def more_states(size, pieces, mark, rates, key_rows, value_rows):
    def body(mark_ref, rates_ref, key_ref, value_ref, *outs):
        group = partners()

        def head(ref):
            return lambda c, h, cols: ref[:, columns(size, group[pieces[c][0]], h)]

        state_payloads(
            size, pieces, mark_ref[...], rates_ref, group, outs, head(key_ref), head(value_ref)
        )

    n = len(pieces)
    return call(
        body, "states", (mark, rates, key_rows, value_rows), [size.payload] * n,
        n * size.each * 4 * size.rows * size.dim * size.dim, n * size.state * size.rows * 8,
    )


def nearby_attended(size, mark, rates, queries, key_rows, value_rows):
    def body(mark_ref, rates_ref, query_ref, key_ref, value_ref, out_ref):
        gap = pair_steps(mark_ref[...], size)
        for h in range(size.heads):
            cols = slice(h * size.dim, (h + 1) * size.dim)
            rate = square_rate(rates_ref[h : h + 1, :], size)
            weight = decay(gap, rate)
            query, key, value = query_ref[:, cols], key_ref[:, cols], value_ref[:, cols]
            high, low = halves(dot(query, key, 1, 1) * weight)
            out_ref[:, cols] = dot(
                jnp.concatenate([high, low], 1), jnp.concatenate([value, value], 0)
            )

    return call(
        body, "nearby", (mark, rates, queries, key_rows, value_rows), [size.block],
        size.heads * 6 * size.rows * size.dim * size.dim, size.features * size.rows * 10,
    )[0]


def put_rows(ref, at, rows):
    ref[at : at + rows.shape[0], :] = rows


def group_total(size, backward, wave, rates, parts, riders=(), count=False):
    mark_row = size.state + (1 if backward else 0)

    def body(rates_ref, *refs):
        ins, rides = refs[:GROUP], refs[GROUP : GROUP + len(riders)]
        outs = refs[GROUP + len(riders) :]
        place = places(backward)
        marks = [ref[mark_row : mark_row + 1, :] for ref in ins]
        end = marks[0]
        for mark in marks[1:]:
            end = jnp.minimum(end, mark) if backward else jnp.maximum(end, mark)
        steps = [
            steps_if(marks[k] == end, ((GROUP - 1 - place[k]) * size.rows).astype(f32))
            for k in range(GROUP)
        ]
        me = partners()[0]
        for h, cols in wave_heads(size, wave):
            rate = rate_of(rates_ref, size, me, h)
            total = None
            for k in range(GROUP):
                term = decay(steps[k], rate) * ins[k][cols, :]
                total = term if total is None else total + term
            outs[0][cols, :] = total
        rows = [ride[...] for ride in rides] or [ref[size.state :, :] for ref in ins]
        put_rows(outs[0], size.state, with_marks(size, end, end, sum(rows)))
        if count:
            outs[1][...] = sum(rows)

    return call(
        body, "total", (rates, *parts, *riders), [size.payload] + [size.rows_of_gain] * count,
        size.state * size.dim * 8, size.state * size.dim * 20,
    )


def group_prefixes(size, backward, wave, rates, parts, entering, riders=(), own=()):
    mark_row = size.state + (1 if backward else 0)

    def body(rates_ref, *refs):
        ins, enter, refs = refs[:GROUP], refs[GROUP], refs[GROUP + 1 :]
        rows = [ref[...] for ref in refs[: len(riders)]]
        rows += [ref[size.state :, :] for ref in refs[len(riders) : len(riders) + len(own)]]
        outs = refs[len(riders) + len(own) :]
        gains = sum(rows) + enter[size.state :, :] if own else sum(rows)
        if not rows:
            gains = jnp.zeros((size.info, size.dim), f32)
        place = places(backward)
        me = partners()[0]
        marks = [ref[mark_row : mark_row + 1, :] for ref in ins]
        block, members = lax.axis_index("seq"), lax.axis_size("seq")
        first = block >= members - GROUP if backward else block < GROUP
        outer = jnp.where(first, FAR if backward else 0.0, enter[size.state : size.state + 1, :])
        steps = []
        for to in range(GROUP):
            now = outer
            for k in range(GROUP):
                if backward:
                    now = jnp.where(place[k] < place[to], jnp.minimum(now, marks[k]), now)
                else:
                    now = jnp.where(place[k] < place[to], jnp.maximum(now, marks[k]), now)
            if to == 0 or backward:
                put_rows(outs[to], size.state, with_marks(size, now, now, gains))
            far = (place[to] * size.rows).astype(f32)
            steps.append([steps_if(jnp.logical_and(outer == now, jnp.logical_not(first)), far)])
            for k in range(GROUP):
                gap = place[to] - 1 - place[k]
                live = jnp.logical_and(marks[k] == now, gap >= 0)
                steps[to].append(steps_if(live, (gap * size.rows).astype(f32)))
        for h, cols in wave_heads(size, wave):
            rate = rate_of(rates_ref, size, me, h)
            for to in range(GROUP):
                total = decay(steps[to][0], rate) * enter[cols, :]
                for k in range(GROUP):
                    if k != to:
                        total += decay(steps[to][1 + k], rate) * ins[k][cols, :]
                outs[to][cols, :] = total

    return call(
        body, "prefixes", (rates, *parts, entering, *riders, *own), [size.payload] + [size.payload if backward else size.bare] * (GROUP - 1),
        size.state * size.dim * 40, size.state * size.dim * 36,
    )


def whole_attended(size, wave, mark, rates, queries, out_grad, gain, near, entering, before=()):
    last = wave == size.waves - 1

    def body(mark_ref, rates_ref, query_ref, grad_ref, gain_ref, near_ref, *refs):
        states, earlier, outs = refs[:GROUP], refs[GROUP : GROUP + len(before)], refs[GROUP + len(before) :]
        group = partners()
        mark = mark_ref[...]
        behind = steps_if(mark == states[0][size.state : size.state + 1, :], position(size) + 1.0)
        if before:
            for c in range(GROUP):
                for h in range(wave * size.each):
                    here = columns(size, group[c], h)
                    outs[0][:, here] = earlier[0][:, here]
        square = earlier[1][...] if before else jnp.zeros((size.rows, size.dim), f32)
        cross = earlier[2][...] if before else jnp.zeros((size.rows, size.dim), f32)
        for c in range(GROUP):
            for h, cols in wave_heads(size, wave):
                here = columns(size, group[c], h)
                weight = decay(behind, rate_of(rates_ref, size, group[c], h))
                query = query_ref[:, here]
                high, low = halves(states[c][cols, :])
                inter = dot(jnp.concatenate([query, query], 1), jnp.concatenate([high, low], 0))
                out = near_ref[:, here] + weight * inter
                outs[0][:, here] = out
                square += out * out
                cross += grad_ref[:, here].astype(f32) * gain_ref[:, here] * out
        if last:
            square = jnp.sum(square.T, axis=0, keepdims=True)
            cross = jnp.sum(cross.T, axis=0, keepdims=True)
            index = lax.broadcasted_iota(jnp.int32, (8, size.rows), 0)
            outs[1][...] = jnp.where(index == 0, square, jnp.where(index == 1, cross, 0.0))
        else:
            outs[1][...], outs[2][...] = square, cross

    if last:
        sums = [jax.ShapeDtypeStruct((8, size.rows), f32)]
    else:
        sums = [jax.ShapeDtypeStruct((size.rows, size.dim), f32)] * 2
    inputs = (mark, rates, queries, out_grad, gain, near, *entering, *before)
    return call(
        body, "attended", inputs, [size.block] + sums,
        GROUP * size.each * 4 * size.rows * size.dim * size.dim, GROUP * size.state * size.rows * 16,
        aliases={len(inputs) - len(before): 0} if before else {},
    )


def output_grad_states(size, pieces, norm, mark, rates, queries, out_grad, gain, sums, attended):
    n = len(pieces)

    def body(mark_ref, rates_ref, query_ref, grad_ref, gain_ref, att_ref, *refs):
        sums_refs, outs = refs[: len(sums)], refs[len(sums) :]
        group = partners()
        mark = mark_ref[...]
        last, first = mark[size.rows - 1 :, :], mark[:1, :]
        wide = (size.dim, size.rows)
        square = jnp.broadcast_to(sum(ref[0:1, :] for ref in sums_refs), wide).T
        cross = jnp.broadcast_to(sum(ref[1:2, :] for ref in sums_refs), wide).T
        inv = lax.rsqrt(square / norm + 1e-06)
        pull = inv * inv * inv * cross / norm
        gone = steps_if(mark == first, position(size))
        for c, (chunk, wave) in enumerate(pieces):
            back_ref, state_ref = outs[2 * c : 2 * c + 2]
            gains = []
            for h in range(size.per):
                if wave > 0 and h // size.each != wave:
                    continue
                here, cols = columns(size, group[chunk], h), wave_columns(size, h)
                grad = grad_ref[:, here].astype(f32) * inv
                att = att_ref[:, here]
                if wave == 0:
                    gains.append(jnp.sum(grad * att, axis=0, keepdims=True))
                if h // size.each == wave:
                    weight = decay(gone, rate_of(rates_ref, size, group[chunk], h))
                    back = gain_ref[:, here] * grad - att * pull
                    back_ref[:, cols] = back
                    high, low = halves(back * weight)
                    state_ref[cols, :] = token_product(query_ref[:, here], high, low)
            put_rows(state_ref, size.state, info_rows(size, last, first, gains))

    part = jax.ShapeDtypeStruct((size.rows, size.state), f32)
    outs = call(
        body, "back", (mark, rates, queries, out_grad, gain, attended, *sums),
        [part, size.payload] * n,
        n * size.each * 4 * size.rows * size.dim * size.dim, n * size.state * size.rows * 16,
    )
    return outs[0::2], outs[1::2]


def local_gradients(size, mark, rates, queries, key_rows, value_rows, back, entering):
    pieces = all_pieces(size)
    n = len(pieces)

    def body(mark_ref, rates_ref, query_ref, key_ref, value_ref, *refs):
        backs, states = refs[:n], refs[n : 2 * n]
        out_hbm, local_key, local_value, done, sems = refs[2 * n :]
        group = partners()
        mark = mark_ref[...]
        gap, turned_gap = pair_steps(mark, size), pair_steps(mark, size, 0)
        behind = steps_if(mark == states[0][size.state : size.state + 1, :], position(size) + 1.0)
        copies = []
        for c in range(GROUP):
            for h in range(size.per):
                here = columns(size, group[c], h)
                piece = pieces.index((c, h // size.each))
                near = slice(c * size.wide + h * size.dim, c * size.wide + (h + 1) * size.dim)
                cols = slice(h % size.each * size.dim, (h % size.each + 1) * size.dim)
                rate = rate_of(rates_ref, size, group[c], h)
                rows_rate = square_rate(rate, size)
                weight, turned_weight = decay(gap, rows_rate), decay(turned_gap, rows_rate)
                query, key, value = query_ref[:, here], key_ref[:, here], value_ref[:, here]
                high, low = halves(backs[piece][:, cols])
                both, values = jnp.concatenate([high, low], 1), jnp.concatenate([value, value], 1)
                grads_high, grads_low = halves(dot(both, values, 1, 1) * weight)
                part = dot(
                    jnp.concatenate([grads_high, grads_low], 1), jnp.concatenate([key, key], 0)
                )
                state_high, state_low = halves(states[piece][cols, :])
                inter = dot(
                    jnp.concatenate([high, high, low], 1),
                    jnp.concatenate([state_high, state_low, state_high], 1),
                    1, 1,
                )
                done[c, :, h * size.dim : (h + 1) * size.dim] = (
                    part + decay(behind, rate) * inter
                ).astype(bf16)
                grads_high, grads_low = halves(dot(values, both, 1, 1) * turned_weight)
                local_key[:, near] = dot(
                    jnp.concatenate([grads_high, grads_low], 1),
                    jnp.concatenate([query, query], 0),
                )
                score_high, score_low = halves(dot(key, query, 1, 1) * turned_weight)
                local_value[:, near] = dot(
                    jnp.concatenate([score_high, score_high, score_low], 1),
                    jnp.concatenate([high, low, high], 0),
                )
            copies.append(
                pltpu.make_async_copy(
                    done.at[c], out_hbm.at[:, columns(size, group[c])], sems.at[c]
                )
            )
            copies[c].start()
        for copy in copies:
            copy.wait()

    return call(
        body, "gradients", (mark, rates, queries, key_rows, value_rows, *back, *entering),
        [jax.ShapeDtypeStruct((size.rows, size.features), bf16), size.block, size.block],
        size.heads * 26 * size.rows * size.dim * size.dim, size.features * size.rows * 24,
        [pltpu.VMEM((GROUP, size.rows, size.wide), bf16), pltpu.SemaphoreType.DMA((GROUP,))],
        None, [HBM, VMEM, VMEM],
    )


def final_gradients(size, mark, rates, key_rows, value_rows, local_key, local_value, entering):
    def body(mark_ref, rates_ref, key_ref, value_ref, local_key_ref, local_value_ref, *refs):
        n = GROUP * size.waves
        states, (keys_hbm, values_hbm, gain_hbm) = refs[:n], refs[n : n + 3]
        states = [states[last_order(size).index(i)] for i in range(n)]
        keys, values, gains, sems = refs[n + 3 :]
        group = partners()
        mark = mark_ref[...]
        left = steps_if(mark == states[0][size.state : size.state + 1, :], size.rows - position(size))
        for c in range(GROUP):
            for h in range(size.per):
                at = size.state + MARKS + h
                gains[:, columns(size, group[c], h)] = states[n - GROUP + c][at : at + 1, :]
        copies = [pltpu.make_async_copy(gains, gain_hbm, sems.at[2, 0])]
        copies[0].start()
        for c in range(GROUP):
            for h in range(size.per):
                here = columns(size, group[c], h)
                piece = c + GROUP * (h // size.each)
                at = slice(h % size.each * size.dim, (h % size.each + 1) * size.dim)
                cols = slice(h * size.dim, (h + 1) * size.dim)
                rate = rate_of(rates_ref, size, group[c], h)
                weight = decay(left, rate)
                key, value = key_ref[:, here], value_ref[:, here]
                high, low = halves(states[piece][at, :])
                from_values = dot(
                    jnp.concatenate([value, value], 1), jnp.concatenate([high, low], 1), 1, 1
                )
                from_keys = dot(jnp.concatenate([key, key], 1), jnp.concatenate([high, low], 0))
                near = slice(c * size.wide + h * size.dim, c * size.wide + (h + 1) * size.dim)
                keys[c, :, cols] = (local_key_ref[:, near] + weight * from_values).astype(bf16)
                values[c, :, cols] = (local_value_ref[:, near] + weight * from_keys).astype(bf16)
            here = columns(size, group[c])
            for copy in (
                pltpu.make_async_copy(keys.at[c], keys_hbm.at[:, here], sems.at[0, c]),
                pltpu.make_async_copy(values.at[c], values_hbm.at[:, here], sems.at[1, c]),
            ):
                copy.start()
                copies.append(copy)
        for copy in copies:
            copy.wait()

    shape = jax.ShapeDtypeStruct((size.rows, size.features), bf16)
    held = pltpu.VMEM((GROUP, size.rows, size.wide), bf16)
    return call(
        body, "final",
        (
            mark, rates, key_rows, value_rows, local_key, local_value,
            *[entering[i] for i in last_order(size)],
        ),
        [shape, shape, jax.ShapeDtypeStruct((1, size.features), f32)],
        size.heads * 8 * size.rows * size.dim * size.dim, size.features * size.rows * 24,
        [held, held, pltpu.VMEM((1, size.features), f32), pltpu.SemaphoreType.DMA((3, GROUP))],
        None, [HBM] * 3,
    )


def swap(array, distance):
    members = lax.axis_size("seq")
    return lax.ppermute(array, "seq", [(i, i ^ distance) for i in range(members)])


def exchange(payloads):
    return [payloads[0]] + [swap(payloads[k], k) for k in range(1, GROUP)]


def shifted(array, by):
    members = lax.axis_size("seq")
    pairs = [(i, i + by) for i in range(members) if 0 <= i + by < members]
    return lax.ppermute(array, "seq", pairs)


def cyclic(array, by):
    members = lax.axis_size("seq")
    return lax.ppermute(array, "seq", [(i, (i + by) % members) for i in range(members)])


def reach_of_documents(size):
    longest = lax.axis_size("seq") * size.rows // 4
    return max(longest - 2, 0) // (GROUP * size.rows) + 1


def from_other_groups(size, backward, wave, decay_span, total):
    needed = reach_of_documents(size)
    way = -GROUP if backward else GROUP
    if needed == 1:
        return cyclic(total, way)
    result = shifted(total, way)
    reach = 1
    start = partners()[0] * size.per + wave * size.each
    mine = lax.dynamic_slice(decay_span, (start,), (size.each,))
    while reach < needed:
        incoming = shifted(result, way * reach)
        passes = incoming[size.state, 0] == result[size.state, 0]
        factor = jnp.where(passes, jnp.exp(-(reach * GROUP * size.rows) / mine), 0.0)
        factor = jnp.repeat(factor, size.dim)[:, None]
        result = result.at[: size.state].add(factor * incoming[: size.state])
        reach *= 2
    return result


def local(queries, key_rows, value_rows, segment_ids, decay_span, norm_gain, out_grad):
    size = Sizes(queries, decay_span)
    norm = size.features * lax.axis_size("head")
    members = lax.axis_size("seq")
    seg = segment_ids.reshape(1, size.rows)
    gain = norm_gain.reshape(1, size.features)
    waves = range(size.waves)
    sent = [[(chunk, wave) for chunk in (3, 1, 2)] for wave in waves]
    kept = [(0, wave) for wave in waves]
    every = all_pieces(size)

    outs, mark, rates = first_states(size, sent[0], seg, decay_span, key_rows, value_rows)
    common = (mark, rates)
    states = dict(zip(sent[0], outs))
    later = sum(sent[1:], []) + kept
    states |= zip(later, more_states(size, later, *common, key_rows, value_rows))
    near = nearby_attended(size, *common, queries, key_rows, value_rows)
    parts = {w: exchange({k: states[k, w] for k in range(GROUP)}) for w in waves}
    totals = {w: group_total(size, False, w, rates, parts[w])[0] for w in waves}
    outer = {w: from_other_groups(size, False, w, decay_span, totals[w]) for w in waves}
    entering = {}
    for w in waves:
        entering[w] = exchange(group_prefixes(size, False, w, rates, parts[w], outer[w]))

    entering = sum([entering[w] for w in waves], [])
    outs = ()
    for w in waves:
        states = entering[w * GROUP : (w + 1) * GROUP]
        outs = whole_attended(size, w, *common, queries, out_grad, gain, near, states, outs)
    attended, sums = outs
    if lax.axis_size("head") == 2:
        sums = (sums, lax.ppermute(sums, "head", [(0, 1), (1, 0)]))
    else:
        sums = (lax.psum(sums, "head"),)
    back, states = {}, {}
    for pieces in [*sent, kept]:
        backs, payloads = output_grad_states(
            size, pieces, norm, *common, queries, out_grad, gain, sums, attended
        )
        back |= zip(pieces, backs)
        states |= zip(pieces, payloads)

    parts = {w: exchange({k: states[k, w] for k in range(GROUP)}) for w in waves}
    back = [back[piece] for piece in every]
    totals, leaving, last = {}, [], size.waves - 1
    rides = size.waves > 1 and reach_of_documents(size) == 1 and members > GROUP
    totals[0], *gains = group_total(size, True, 0, rates, parts[0], (), True)
    apart = 2 if rides else 1
    while apart * GROUP < members:
        gains = [sum(gains), cyclic(sum(gains), -apart * GROUP)]
        apart *= 2
    for w in waves[1:]:
        riders = gains if rides and w == last else ()
        totals[w] = group_total(size, True, w, rates, parts[w], riders)[0]
    outer = {w: from_other_groups(size, True, w, decay_span, totals[w]) for w in waves}
    for w in waves:
        riders = gains if w == last and not rides else ()
        own = (totals[w],) if w == last and rides else ()
        leaving += exchange(
            group_prefixes(size, True, w, rates, parts[w], outer[w], riders, own)
        )

    query_grad, local_key, local_value = local_gradients(
        size, *common, queries, key_rows, value_rows, back, entering
    )
    key_grad, value_grad, gain_grad = final_gradients(
        size, *common, key_rows, value_rows, local_key, local_value, leaving
    )
    return query_grad, key_grad, value_grad, gain_grad.reshape(size.features)


def solution(mesh):
    rows = P("seq", "head")
    in_specs = (rows, rows, rows, P("seq"), P("head"), P("head"), rows)
    return jax.shard_map(
        local, mesh=mesh, in_specs=in_specs, out_specs=(rows, rows, rows, P("head")), check_vma=False
    )
```

```python
import jax
import jax.numpy as jnp
from jax import lax
from jax.experimental import pallas as pl
from jax.experimental.pallas import tpu as pltpu
from jax.sharding import PartitionSpec as P

GROUP = 4
MARKS = 2
FAR = 1e9
NEVER = 1e30
f32 = jnp.float32
bf16 = jnp.bfloat16
HBM = pl.BlockSpec(memory_space=pltpu.HBM)
VMEM = pl.BlockSpec(memory_space=pltpu.VMEM)


def dot(a, b, over_a=1, over_b=0):
    return lax.dot_general(a, b, (((over_a,), (over_b,)), ((), ())), preferred_element_type=f32)


def halves(x):
    high = x.astype(bf16)
    return high, (x - high.astype(f32)).astype(bf16)


def decay(steps, rate):
    return jnp.exp(steps * rate)


class Sizes:
    def __init__(self, queries, decay_span):
        self.rows = queries.shape[0]
        self.heads = decay_span.shape[0]
        self.features = queries.shape[1]
        self.dim = self.features // self.heads
        self.per = self.heads // GROUP
        self.wide = self.per * self.dim
        self.info = -(-(MARKS + self.per) // 8) * 8
        self.waves = 2 if self.per % 2 == 0 else 1
        self.each = self.per // self.waves
        self.state = self.each * self.dim
        self.payload = jax.ShapeDtypeStruct((self.state + self.info, self.dim), f32)
        self.block = jax.ShapeDtypeStruct((self.rows, self.features), f32)
        self.bare = jax.ShapeDtypeStruct((self.state, self.dim), f32)
        self.rows_of_gain = jax.ShapeDtypeStruct((self.info, self.dim), f32)


def position(size):
    return lax.broadcasted_iota(jnp.int32, (size.rows, size.dim), 0).astype(f32)


def steps_if(live, steps):
    return jnp.where(live, steps, NEVER)


def pair_steps(mark, size, earlier=1):
    shape = (size.rows, size.rows)
    here = mark if size.rows == size.dim else jnp.broadcast_to(mark[:, :1], shape)
    later = lax.broadcasted_iota(jnp.int32, shape, 1 - earlier)
    gap = later - lax.broadcasted_iota(jnp.int32, shape, earlier)
    return steps_if(jnp.logical_and(gap >= 0, here == here.T), gap.astype(f32))


def token_product(a, high, low):
    turned = a.T
    return dot(jnp.concatenate([turned, turned], 1), jnp.concatenate([high, low], 0))


def info_rows(size, last, first, more=()):
    index = lax.broadcasted_iota(jnp.int32, (size.info, size.dim), 0)
    rows = jnp.zeros((size.info, size.dim), f32)
    for i, row in enumerate((last, first, *more)):
        rows = jnp.where(index == i, row, rows)
    return rows


def with_marks(size, last, first, rows):
    index = lax.broadcasted_iota(jnp.int32, (size.info, size.dim), 0)
    return jnp.where(index == 0, last, jnp.where(index == 1, first, rows))


def partners():
    me = jnp.bitwise_and(lax.axis_index("seq"), GROUP - 1)
    return [jnp.bitwise_xor(me, k) for k in range(GROUP)]


def places(backward):
    return [GROUP - 1 - p for p in partners()] if backward else partners()


def columns(size, group, h=None):
    if h is None:
        return pl.ds(pl.multiple_of(group * size.wide, size.wide), size.wide)
    return pl.ds(pl.multiple_of(group * size.wide + h * size.dim, size.dim), size.dim)


def wave_heads(size, wave):
    return [(wave * size.each + i, slice(i * size.dim, (i + 1) * size.dim)) for i in range(size.each)]


def wave_columns(size, h):
    return slice(h % size.each * size.dim, (h % size.each + 1) * size.dim)


def all_pieces(size):
    return [(chunk, wave) for wave in range(size.waves) for chunk in range(GROUP)]


def last_order(size):
    usual = list(range(GROUP * (size.waves - 1)))
    return usual + [GROUP * (size.waves - 1) + k for k in reversed(range(GROUP))]


def rate_of(rates_ref, size, group, h):
    return rates_ref[pl.ds(group * size.per + h, 1), :]


def square_rate(rate, size):
    return rate[:, :1] if size.rows != size.dim else rate


def call(body, name, inputs, outputs, flops, moved, scratch=(), in_specs=None, out_specs=None, vmem=8, aliases=None):
    return pl.pallas_call(
        body,
        out_shape=outputs,
        in_specs=in_specs if in_specs is not None else [VMEM] * len(inputs),
        out_specs=out_specs if out_specs is not None else [VMEM] * len(outputs),
        scratch_shapes=list(scratch),
        input_output_aliases=aliases or {},
        compiler_params=pltpu.CompilerParams(vmem_limit_bytes=vmem * 1024 * 1024),
        cost_estimate=pl.CostEstimate(flops=flops, bytes_accessed=moved, transcendentals=0),
        name=name,
    )(*inputs)


def state_payloads(size, pieces, mark, rates_ref, group, outs, key_of, value_of):
    last, first = mark[size.rows - 1 :, :], mark[:1, :]
    ahead = steps_if(mark == last, (size.rows - 1.0) - position(size))
    for c, (chunk, wave) in enumerate(pieces):
        for h, cols in wave_heads(size, wave):
            weight = decay(ahead, rate_of(rates_ref, size, group[chunk], h))
            high, low = halves(value_of(c, h, cols).astype(f32) * weight)
            outs[c][cols, :] = token_product(key_of(c, h, cols), high, low)
        outs[c][size.state :, :] = info_rows(size, last, first)


def first_states(size, pieces, seg, decay_span, key_rows, value_rows):
    n = len(pieces)
    wide = size.each * size.dim

    def body(seg_hbm, span_hbm, key_hbm, value_hbm, *refs):
        outs, mark_ref, rates_ref = refs[:n], refs[n], refs[n + 1]
        seg_row, span_row, keys, values, sems = refs[n + 2 :]
        group = partners()
        small = (
            pltpu.make_async_copy(seg_hbm, seg_row, sems.at[2, 0]),
            pltpu.make_async_copy(span_hbm, span_row, sems.at[2, 1]),
        )
        copies = []
        for copy in small:
            copy.start()
        for c, (chunk, wave) in enumerate(pieces):
            here = pl.ds(pl.multiple_of(group[chunk] * size.wide + wave * wide, wide), wide)
            copies += [
                pltpu.make_async_copy(key_hbm.at[:, here], keys.at[c], sems.at[0, c]),
                pltpu.make_async_copy(value_hbm.at[:, here], values.at[c], sems.at[1, c]),
            ]
        for copy in copies:
            copy.start()
        for copy in small:
            copy.wait()
        mark = jnp.broadcast_to(seg_row[...].astype(f32) + 1.0, (size.dim, size.rows)).T
        mark_ref[...] = mark
        rates_ref[...] = jnp.broadcast_to(-1.0 / span_row[...], (size.dim, size.heads)).T
        for copy in copies:
            copy.wait()
        state_payloads(
            size, pieces, mark, rates_ref, group, outs,
            lambda c, h, cols: keys[c, :, cols], lambda c, h, cols: values[c, :, cols],
        )

    held = (n, size.rows, wide)
    outs = call(
        body, "states", (seg, decay_span.reshape(1, size.heads), key_rows, value_rows),
        [size.payload] * n + [
            jax.ShapeDtypeStruct((size.rows, size.dim), f32),
            jax.ShapeDtypeStruct((size.heads, size.dim), f32),
        ],
        n * size.each * 4 * size.rows * size.dim * size.dim, n * wide * size.rows * 8,
        [
            pltpu.VMEM((1, size.rows), jnp.int32),
            pltpu.VMEM((1, size.heads), f32),
            pltpu.VMEM(held, bf16),
            pltpu.VMEM(held, bf16),
            pltpu.SemaphoreType.DMA((3, max(n, 2))),
        ],
        [HBM] * 4, vmem=60,
    )
    return outs[:n], outs[n], outs[n + 1]


def more_states(size, pieces, mark, rates, key_rows, value_rows):
    def body(mark_ref, rates_ref, key_ref, value_ref, *outs):
        group = partners()

        def head(ref):
            return lambda c, h, cols: ref[:, columns(size, group[pieces[c][0]], h)]

        state_payloads(
            size, pieces, mark_ref[...], rates_ref, group, outs, head(key_ref), head(value_ref)
        )

    n = len(pieces)
    return call(
        body, "states", (mark, rates, key_rows, value_rows), [size.payload] * n,
        n * size.each * 4 * size.rows * size.dim * size.dim, n * size.state * size.rows * 8,
    )


def nearby_attended(size, mark, rates, queries, key_rows, value_rows):
    def body(mark_ref, rates_ref, query_ref, key_ref, value_ref, out_ref):
        gap = pair_steps(mark_ref[...], size)
        for h in range(size.heads):
            cols = slice(h * size.dim, (h + 1) * size.dim)
            rate = square_rate(rates_ref[h : h + 1, :], size)
            weight = decay(gap, rate)
            query, key, value = query_ref[:, cols], key_ref[:, cols], value_ref[:, cols]
            high, low = halves(dot(query, key, 1, 1) * weight)
            out_ref[:, cols] = dot(
                jnp.concatenate([high, low], 1), jnp.concatenate([value, value], 0)
            )

    return call(
        body, "nearby", (mark, rates, queries, key_rows, value_rows), [size.block],
        size.heads * 6 * size.rows * size.dim * size.dim, size.features * size.rows * 10,
    )[0]


def put_rows(ref, at, rows):
    ref[at : at + rows.shape[0], :] = rows


def group_total(size, backward, wave, rates, parts, riders=(), count=False):
    mark_row = size.state + (1 if backward else 0)

    def body(rates_ref, *refs):
        ins, rides = refs[:GROUP], refs[GROUP : GROUP + len(riders)]
        outs = refs[GROUP + len(riders) :]
        place = places(backward)
        marks = [ref[mark_row : mark_row + 1, :] for ref in ins]
        end = marks[0]
        for mark in marks[1:]:
            end = jnp.minimum(end, mark) if backward else jnp.maximum(end, mark)
        steps = [
            steps_if(marks[k] == end, ((GROUP - 1 - place[k]) * size.rows).astype(f32))
            for k in range(GROUP)
        ]
        me = partners()[0]
        for h, cols in wave_heads(size, wave):
            rate = rate_of(rates_ref, size, me, h)
            total = None
            for k in range(GROUP):
                term = decay(steps[k], rate) * ins[k][cols, :]
                total = term if total is None else total + term
            outs[0][cols, :] = total
        rows = [ride[...] for ride in rides] or [ref[size.state :, :] for ref in ins]
        put_rows(outs[0], size.state, with_marks(size, end, end, sum(rows)))
        if count:
            outs[1][...] = sum(rows)

    return call(
        body, "total", (rates, *parts, *riders), [size.payload] + [size.rows_of_gain] * count,
        size.state * size.dim * 8, size.state * size.dim * 20,
    )


def group_prefixes(size, backward, wave, rates, parts, entering, riders=(), own=()):
    mark_row = size.state + (1 if backward else 0)

    def body(rates_ref, *refs):
        ins, enter, refs = refs[:GROUP], refs[GROUP], refs[GROUP + 1 :]
        rows = [ref[...] for ref in refs[: len(riders)]]
        rows += [ref[size.state :, :] for ref in refs[len(riders) : len(riders) + len(own)]]
        outs = refs[len(riders) + len(own) :]
        gains = sum(rows) + enter[size.state :, :] if own else sum(rows)
        if not rows:
            gains = jnp.zeros((size.info, size.dim), f32)
        place = places(backward)
        me = partners()[0]
        marks = [ref[mark_row : mark_row + 1, :] for ref in ins]
        block, members = lax.axis_index("seq"), lax.axis_size("seq")
        first = block >= members - GROUP if backward else block < GROUP
        outer = jnp.where(first, FAR if backward else 0.0, enter[size.state : size.state + 1, :])
        steps = []
        for to in range(GROUP):
            now = outer
            for k in range(GROUP):
                if backward:
                    now = jnp.where(place[k] < place[to], jnp.minimum(now, marks[k]), now)
                else:
                    now = jnp.where(place[k] < place[to], jnp.maximum(now, marks[k]), now)
            if to == 0 or backward:
                put_rows(outs[to], size.state, with_marks(size, now, now, gains))
            far = (place[to] * size.rows).astype(f32)
            steps.append([steps_if(jnp.logical_and(outer == now, jnp.logical_not(first)), far)])
            for k in range(GROUP):
                gap = place[to] - 1 - place[k]
                live = jnp.logical_and(marks[k] == now, gap >= 0)
                steps[to].append(steps_if(live, (gap * size.rows).astype(f32)))
        for h, cols in wave_heads(size, wave):
            rate = rate_of(rates_ref, size, me, h)
            for to in range(GROUP):
                total = decay(steps[to][0], rate) * enter[cols, :]
                for k in range(GROUP):
                    if k != to:
                        total += decay(steps[to][1 + k], rate) * ins[k][cols, :]
                outs[to][cols, :] = total

    return call(
        body, "prefixes", (rates, *parts, entering, *riders, *own), [size.payload] + [size.payload if backward else size.bare] * (GROUP - 1),
        size.state * size.dim * 40, size.state * size.dim * 36,
    )


def whole_attended(size, wave, mark, rates, queries, out_grad, gain, near, entering, before=()):
    last = wave == size.waves - 1

    def body(mark_ref, rates_ref, query_ref, grad_ref, gain_ref, near_ref, *refs):
        states, earlier, outs = refs[:GROUP], refs[GROUP : GROUP + len(before)], refs[GROUP + len(before) :]
        states = states[::-1] if last else states
        group = partners()
        mark = mark_ref[...]
        behind = steps_if(mark == states[0][size.state : size.state + 1, :], position(size) + 1.0)
        if before:
            for c in range(GROUP):
                for h in range(wave * size.each):
                    here = columns(size, group[c], h)
                    outs[0][:, here] = earlier[0][:, here]
        square = earlier[1][...] if before else jnp.zeros((size.rows, size.dim), f32)
        cross = earlier[2][...] if before else jnp.zeros((size.rows, size.dim), f32)
        for c in range(GROUP):
            for h, cols in wave_heads(size, wave):
                here = columns(size, group[c], h)
                weight = decay(behind, rate_of(rates_ref, size, group[c], h))
                query = query_ref[:, here]
                high, low = halves(states[c][cols, :])
                inter = dot(jnp.concatenate([query, query], 1), jnp.concatenate([high, low], 0))
                out = near_ref[:, here] + weight * inter
                outs[0][:, here] = out
                square += out * out
                cross += grad_ref[:, here].astype(f32) * gain_ref[:, here] * out
        if last:
            square = jnp.sum(square.T, axis=0, keepdims=True)
            cross = jnp.sum(cross.T, axis=0, keepdims=True)
            index = lax.broadcasted_iota(jnp.int32, (8, size.rows), 0)
            outs[1][...] = jnp.where(index == 0, square, jnp.where(index == 1, cross, 0.0))
        else:
            outs[1][...], outs[2][...] = square, cross

    if last:
        sums = [jax.ShapeDtypeStruct((8, size.rows), f32)]
    else:
        sums = [jax.ShapeDtypeStruct((size.rows, size.dim), f32)] * 2
    farthest_first = entering[::-1] if last else entering
    inputs = (mark, rates, queries, out_grad, gain, near, *farthest_first, *before)
    return call(
        body, "attended", inputs, [size.block] + sums,
        GROUP * size.each * 4 * size.rows * size.dim * size.dim, GROUP * size.state * size.rows * 16,
        aliases={len(inputs) - len(before): 0} if before else {},
    )


def output_grad_states(size, pieces, norm, mark, rates, queries, out_grad, gain, sums, attended):
    n = len(pieces)

    def body(mark_ref, rates_ref, query_ref, grad_ref, gain_ref, att_ref, *refs):
        sums_refs, outs = refs[: len(sums)], refs[len(sums) :]
        group = partners()
        mark = mark_ref[...]
        last, first = mark[size.rows - 1 :, :], mark[:1, :]
        wide = (size.dim, size.rows)
        square = jnp.broadcast_to(sum(ref[0:1, :] for ref in sums_refs), wide).T
        cross = jnp.broadcast_to(sum(ref[1:2, :] for ref in sums_refs), wide).T
        inv = lax.rsqrt(square / norm + 1e-06)
        pull = inv * inv * inv * cross / norm
        gone = steps_if(mark == first, position(size))
        for c, (chunk, wave) in enumerate(pieces):
            back_ref, state_ref = outs[2 * c : 2 * c + 2]
            gains = []
            for h in range(size.per):
                if wave > 0 and h // size.each != wave:
                    continue
                here, cols = columns(size, group[chunk], h), wave_columns(size, h)
                grad = grad_ref[:, here].astype(f32) * inv
                att = att_ref[:, here]
                if wave == 0:
                    gains.append(jnp.sum(grad * att, axis=0, keepdims=True))
                if h // size.each == wave:
                    weight = decay(gone, rate_of(rates_ref, size, group[chunk], h))
                    back = gain_ref[:, here] * grad - att * pull
                    back_ref[:, cols] = back
                    high, low = halves(back * weight)
                    state_ref[cols, :] = token_product(query_ref[:, here], high, low)
            put_rows(state_ref, size.state, info_rows(size, last, first, gains))

    part = jax.ShapeDtypeStruct((size.rows, size.state), f32)
    outs = call(
        body, "back", (mark, rates, queries, out_grad, gain, attended, *sums),
        [part, size.payload] * n,
        n * size.each * 4 * size.rows * size.dim * size.dim, n * size.state * size.rows * 16,
    )
    return outs[0::2], outs[1::2]


def local_gradients(size, mark, rates, queries, key_rows, value_rows, back, entering):
    pieces = all_pieces(size)
    n = len(pieces)

    def body(mark_ref, rates_ref, query_ref, key_ref, value_ref, *refs):
        backs, states = refs[:n], refs[n : 2 * n]
        out_hbm, local_key, local_value, done, sems = refs[2 * n :]
        group = partners()
        mark = mark_ref[...]
        gap, turned_gap = pair_steps(mark, size), pair_steps(mark, size, 0)
        behind = steps_if(mark == states[0][size.state : size.state + 1, :], position(size) + 1.0)
        copies = []
        for c in range(GROUP):
            for h in range(size.per):
                here = columns(size, group[c], h)
                piece = pieces.index((c, h // size.each))
                near = slice(c * size.wide + h * size.dim, c * size.wide + (h + 1) * size.dim)
                cols = slice(h % size.each * size.dim, (h % size.each + 1) * size.dim)
                rate = rate_of(rates_ref, size, group[c], h)
                rows_rate = square_rate(rate, size)
                weight, turned_weight = decay(gap, rows_rate), decay(turned_gap, rows_rate)
                query, key, value = query_ref[:, here], key_ref[:, here], value_ref[:, here]
                high, low = halves(backs[piece][:, cols])
                both, values = jnp.concatenate([high, low], 1), jnp.concatenate([value, value], 1)
                grads_high, grads_low = halves(dot(both, values, 1, 1) * weight)
                part = dot(
                    jnp.concatenate([grads_high, grads_low], 1), jnp.concatenate([key, key], 0)
                )
                state_high, state_low = halves(states[piece][cols, :])
                inter = dot(
                    jnp.concatenate([high, high, low], 1),
                    jnp.concatenate([state_high, state_low, state_high], 1),
                    1, 1,
                )
                done[c, :, h * size.dim : (h + 1) * size.dim] = (
                    part + decay(behind, rate) * inter
                ).astype(bf16)
                grads_high, grads_low = halves(dot(values, both, 1, 1) * turned_weight)
                local_key[:, near] = dot(
                    jnp.concatenate([grads_high, grads_low], 1),
                    jnp.concatenate([query, query], 0),
                )
                score_high, score_low = halves(dot(key, query, 1, 1) * turned_weight)
                local_value[:, near] = dot(
                    jnp.concatenate([score_high, score_high, score_low], 1),
                    jnp.concatenate([high, low, high], 0),
                )
            copies.append(
                pltpu.make_async_copy(
                    done.at[c], out_hbm.at[:, columns(size, group[c])], sems.at[c]
                )
            )
            copies[c].start()
        for copy in copies:
            copy.wait()

    return call(
        body, "gradients", (mark, rates, queries, key_rows, value_rows, *back, *entering),
        [jax.ShapeDtypeStruct((size.rows, size.features), bf16), size.block, size.block],
        size.heads * 26 * size.rows * size.dim * size.dim, size.features * size.rows * 24,
        [pltpu.VMEM((GROUP, size.rows, size.wide), bf16), pltpu.SemaphoreType.DMA((GROUP,))],
        None, [HBM, VMEM, VMEM],
    )


def final_gradients(size, mark, rates, key_rows, value_rows, local_key, local_value, entering):
    def body(mark_ref, rates_ref, key_ref, value_ref, local_key_ref, local_value_ref, *refs):
        n = GROUP * size.waves
        states, (keys_hbm, values_hbm, gain_hbm) = refs[:n], refs[n : n + 3]
        states = [states[last_order(size).index(i)] for i in range(n)]
        keys, values, gains, sems = refs[n + 3 :]
        group = partners()
        mark = mark_ref[...]
        left = steps_if(mark == states[0][size.state : size.state + 1, :], size.rows - position(size))
        for c in range(GROUP):
            for h in range(size.per):
                at = size.state + MARKS + h
                gains[:, columns(size, group[c], h)] = states[n - GROUP + c][at : at + 1, :]
        copies = [pltpu.make_async_copy(gains, gain_hbm, sems.at[2, 0])]
        copies[0].start()
        for c in range(GROUP):
            for h in range(size.per):
                here = columns(size, group[c], h)
                piece = c + GROUP * (h // size.each)
                at = slice(h % size.each * size.dim, (h % size.each + 1) * size.dim)
                cols = slice(h * size.dim, (h + 1) * size.dim)
                rate = rate_of(rates_ref, size, group[c], h)
                weight = decay(left, rate)
                key, value = key_ref[:, here], value_ref[:, here]
                high, low = halves(states[piece][at, :])
                from_values = dot(
                    jnp.concatenate([value, value], 1), jnp.concatenate([high, low], 1), 1, 1
                )
                from_keys = dot(jnp.concatenate([key, key], 1), jnp.concatenate([high, low], 0))
                near = slice(c * size.wide + h * size.dim, c * size.wide + (h + 1) * size.dim)
                keys[c, :, cols] = (local_key_ref[:, near] + weight * from_values).astype(bf16)
                values[c, :, cols] = (local_value_ref[:, near] + weight * from_keys).astype(bf16)
            here = columns(size, group[c])
            for copy in (
                pltpu.make_async_copy(keys.at[c], keys_hbm.at[:, here], sems.at[0, c]),
                pltpu.make_async_copy(values.at[c], values_hbm.at[:, here], sems.at[1, c]),
            ):
                copy.start()
                copies.append(copy)
        for copy in copies:
            copy.wait()

    shape = jax.ShapeDtypeStruct((size.rows, size.features), bf16)
    held = pltpu.VMEM((GROUP, size.rows, size.wide), bf16)
    return call(
        body, "final",
        (
            mark, rates, key_rows, value_rows, local_key, local_value,
            *[entering[i] for i in last_order(size)],
        ),
        [shape, shape, jax.ShapeDtypeStruct((1, size.features), f32)],
        size.heads * 8 * size.rows * size.dim * size.dim, size.features * size.rows * 24,
        [held, held, pltpu.VMEM((1, size.features), f32), pltpu.SemaphoreType.DMA((3, GROUP))],
        None, [HBM] * 3,
    )


def swap(array, distance):
    members = lax.axis_size("seq")
    return lax.ppermute(array, "seq", [(i, i ^ distance) for i in range(members)])


def exchange(payloads):
    return [payloads[0]] + [swap(payloads[k], k) for k in range(1, GROUP)]


def shifted(array, by):
    members = lax.axis_size("seq")
    pairs = [(i, i + by) for i in range(members) if 0 <= i + by < members]
    return lax.ppermute(array, "seq", pairs)


def cyclic(array, by):
    members = lax.axis_size("seq")
    return lax.ppermute(array, "seq", [(i, (i + by) % members) for i in range(members)])


def reach_of_documents(size):
    longest = lax.axis_size("seq") * size.rows // 4
    return max(longest - 2, 0) // (GROUP * size.rows) + 1


def from_other_groups(size, backward, wave, decay_span, total):
    needed = reach_of_documents(size)
    way = -GROUP if backward else GROUP
    if needed == 1:
        return cyclic(total, way)
    result = shifted(total, way)
    reach = 1
    start = partners()[0] * size.per + wave * size.each
    mine = lax.dynamic_slice(decay_span, (start,), (size.each,))
    while reach < needed:
        incoming = shifted(result, way * reach)
        passes = incoming[size.state, 0] == result[size.state, 0]
        factor = jnp.where(passes, jnp.exp(-(reach * GROUP * size.rows) / mine), 0.0)
        factor = jnp.repeat(factor, size.dim)[:, None]
        result = result.at[: size.state].add(factor * incoming[: size.state])
        reach *= 2
    return result


def local(queries, key_rows, value_rows, segment_ids, decay_span, norm_gain, out_grad):
    size = Sizes(queries, decay_span)
    norm = size.features * lax.axis_size("head")
    members = lax.axis_size("seq")
    seg = segment_ids.reshape(1, size.rows)
    gain = norm_gain.reshape(1, size.features)
    waves = range(size.waves)
    sent = [[(chunk, wave) for chunk in (3, 1, 2)] for wave in waves]
    kept = [(0, wave) for wave in waves]
    every = all_pieces(size)

    outs, mark, rates = first_states(size, sent[0], seg, decay_span, key_rows, value_rows)
    common = (mark, rates)
    states = dict(zip(sent[0], outs))
    later = sum(sent[1:], []) + kept
    states |= zip(later, more_states(size, later, *common, key_rows, value_rows))
    near = nearby_attended(size, *common, queries, key_rows, value_rows)
    parts = {w: exchange({k: states[k, w] for k in range(GROUP)}) for w in waves}
    totals = {w: group_total(size, False, w, rates, parts[w])[0] for w in waves}
    outer = {w: from_other_groups(size, False, w, decay_span, totals[w]) for w in waves}
    entering = {}
    for w in waves:
        entering[w] = exchange(group_prefixes(size, False, w, rates, parts[w], outer[w]))

    entering = sum([entering[w] for w in waves], [])
    outs = ()
    for w in waves:
        states = entering[w * GROUP : (w + 1) * GROUP]
        outs = whole_attended(size, w, *common, queries, out_grad, gain, near, states, outs)
    attended, sums = outs
    if lax.axis_size("head") == 2:
        sums = (sums, lax.ppermute(sums, "head", [(0, 1), (1, 0)]))
    else:
        sums = (lax.psum(sums, "head"),)
    back, states = {}, {}
    for pieces in [*sent, kept]:
        backs, payloads = output_grad_states(
            size, pieces, norm, *common, queries, out_grad, gain, sums, attended
        )
        back |= zip(pieces, backs)
        states |= zip(pieces, payloads)

    parts = {w: exchange({k: states[k, w] for k in range(GROUP)}) for w in waves}
    back = [back[piece] for piece in every]
    totals, leaving, last = {}, [], size.waves - 1
    rides = size.waves > 1 and reach_of_documents(size) == 1 and members > GROUP
    totals[0], *gains = group_total(size, True, 0, rates, parts[0], (), True)
    apart = 2 if rides else 1
    while apart * GROUP < members:
        gains = [sum(gains), cyclic(sum(gains), -apart * GROUP)]
        apart *= 2
    for w in waves[1:]:
        riders = gains if rides and w == last else ()
        totals[w] = group_total(size, True, w, rates, parts[w], riders)[0]
    outer = {w: from_other_groups(size, True, w, decay_span, totals[w]) for w in waves}
    for w in waves:
        riders = gains if w == last and not rides else ()
        own = (totals[w],) if w == last and rides else ()
        leaving += exchange(
            group_prefixes(size, True, w, rates, parts[w], outer[w], riders, own)
        )

    query_grad, local_key, local_value = local_gradients(
        size, *common, queries, key_rows, value_rows, back, entering
    )
    key_grad, value_grad, gain_grad = final_gradients(
        size, *common, key_rows, value_rows, local_key, local_value, leaving
    )
    return query_grad, key_grad, value_grad, gain_grad.reshape(size.features)


def solution(mesh):
    rows = P("seq", "head")
    in_specs = (rows, rows, rows, P("seq"), P("head"), P("head"), rows)
    return jax.shard_map(
        local, mesh=mesh, in_specs=in_specs, out_specs=(rows, rows, rows, P("head")), check_vma=False
    )
```
